32 devices in a mesh: dp: 8 (over z, x), tensor: 4 (over y, core).
Axes of the slice: x: 2, y: 2, z: 4, core: 2. Of those that a mesh axis runs over, the one named last changes fastest.
Arguments:
- tokens: bfloat16 [32768, 768], P(('dp', 'tensor')), may hold values from -6 to 6
- bucket: int32 [8], P('dp'), may hold values from 0 to 2, as said below
- lengths: int32 [8, 32], P('dp'), may hold values from 0 to 512, as said below
- w_query: bfloat16 [768, 768], P(None, 'tensor'), may hold values from -0.21875 to 0.21875
- b_query: bfloat16 [768], P('tensor'), may hold values from -1.75 to 1.75
- w_key: bfloat16 [768, 768], P(None, 'tensor'), may hold values from -0.21875 to 0.21875
- w_value: bfloat16 [768, 768], P(None, 'tensor'), may hold values from -0.21875 to 0.21875
- b_value: bfloat16 [768], P('tensor'), may hold values from -1.75 to 1.75
- w_out: bfloat16 [768, 768], P('tensor'), may hold values from -0.875 to 0.875
- b_out: bfloat16 [768], replicated, may hold values from -1.75 to 1.75
- norm1_gain: float32 [768], replicated, may hold values from 0.1 to 1.9
- norm1_shift: float32 [768], replicated, may hold values from -1.75 to 1.75
- w_in: bfloat16 [768, 3072], P(None, 'tensor'), may hold values from -0.21875 to 0.21875
- b_in: bfloat16 [3072], P('tensor'), may hold values from -3 to 3
- w_down: bfloat16 [3072, 768], P('tensor'), may hold values from -0.109375 to 0.109375
- b_down: bfloat16 [768], replicated, may hold values from -1.75 to 1.75
- norm2_gain: float32 [768], replicated, may hold values from 0.1 to 1.9
- norm2_shift: float32 [768], replicated, may hold values from -1.75 to 1.75
- cotangent: float32 [32768, 768], P(('dp', 'tensor')), may hold values from -6 to 6
Outputs:
- block_out: bfloat16 [32768, 768], P(('dp', 'tensor'))
- grad_tokens: float32 [32768, 768], P(('dp', 'tensor'))
- grad_w_query: float32 [768, 768], P(None, 'tensor')
- grad_b_query: float32 [768], P('tensor')
- grad_w_key: float32 [768, 768], P(None, 'tensor')
- grad_w_value: float32 [768, 768], P(None, 'tensor')
- grad_b_value: float32 [768], P('tensor')
- grad_w_out: float32 [768, 768], P('tensor')
- grad_b_out: float32 [768], replicated
- grad_norm1_gain: float32 [768], replicated
- grad_norm1_shift: float32 [768], replicated
- grad_w_in: float32 [768, 3072], P(None, 'tensor')
- grad_b_in: float32 [3072], P('tensor')
- grad_w_down: float32 [3072, 768], P('tensor')
- grad_b_down: float32 [768], replicated
- grad_norm2_gain: float32 [768], replicated
- grad_norm2_shift: float32 [768], replicated
The draws below stay inside these ranges and needn't reach their ends.
Inputs may be any that keep to these rules, and one draw needn't show every extreme that they name: bucket[g] sets the row length of group g (128, 256, 512); group 0 has bucket 2 and group 1 bucket 0. `lengths`: for group g with row length L, entries 0 to 4096/L - 1 are 1 to L, entry 0 equal to L; later entries are 0.
All inputs are finite; a program needn't handle non-finite values.
Results may differ from the reference program's by a relative error of at most 0.015.
The reference program's roundings to bfloat16 on the way count: a program that leaves them out, or rounds other values in their place, can miss the bound.
Values may be sent and summed in bfloat16 or wider, within the bound.
No kernel may reach another device: no remote copies, remote signals or barrier semaphores. Data moves between devices by JAX's collectives and lax.ppermute only.
A program may use at most 192 MiB of HBM per device.

```python
import jax
import jax.numpy as jnp
from jax import lax

D = 768
HEADS = 12
HEAD = 64
FF = 3072
BLOCK = 512
TOK_DEV = 4096
ROWS = 32
TOKENS = 32768
N_DP = 8


def shared_rows(key):
    bucket_key = jax.random.fold_in(key, 101)
    drawn = jax.random.randint(bucket_key, (N_DP,), 0, 3, dtype=jnp.int32)
    places = jnp.arange(N_DP, dtype=jnp.int32)
    kinds = jnp.where(places == 0, 2, jnp.where(places == 1, 0, drawn)).astype(jnp.int32)
    row_len = jnp.where(kinds == 0, BLOCK // 4, jnp.where(kinds == 1, BLOCK // 2, BLOCK)).astype(jnp.int32)
    length_key = jax.random.fold_in(key, 202)
    fraction = jax.random.randint(length_key, (N_DP, ROWS), 0, BLOCK, dtype=jnp.int32)
    row_lengths = 1 + fraction * row_len[:, None] // BLOCK
    row_index = jnp.arange(ROWS, dtype=jnp.int32)[None, :]
    row_lengths = jnp.where(row_index == 0, row_len[:, None], row_lengths)
    used = row_index < (TOK_DEV // row_len)[:, None]
    return (kinds, jnp.where(used, row_lengths, 0).astype(jnp.int32))


def draw_bucket(key, part):
    kinds, row_lengths = shared_rows(key)
    return kinds


def draw_lengths(key, part):
    kinds, row_lengths = shared_rows(key)
    return row_lengths


def block_levels(stream_key, extent, shards, least, high):
    loudness, own = 1.0, jax.random.fold_in(stream_key, 6)
    for axis_at, blocks in shards:
        heights = jnp.exp(jax.random.uniform(jax.random.fold_in(own, axis_at), (blocks,), jnp.float32, least / len(shards), high / len(shards)))
        loudness = loudness * jnp.repeat(heights, extent[axis_at] // blocks).reshape([-1 if axis == axis_at else 1 for axis in range(len(extent))])
    return loudness


def normal_values(own_key, extent, scale, bound, cuts=(), kind=jnp.bfloat16):
    values = jax.random.normal(own_key, extent, jnp.float32) * scale
    if len(cuts) > 0:
        values = block_levels(own_key, extent, cuts, -0.22, 0.18) * values
    return jnp.clip(values, min=-bound, max=bound).astype(kind)


def setup_inputs(seed: int = 0) -> dict:
    keys = jax.random.split(jax.random.key(seed), 20)
    return {
        "tokens": normal_values(keys[0], (TOKENS, D), 1.0, 6.0, ((0, 32),)),
        "bucket": draw_bucket(jax.random.fold_in(keys[19], 71), 0),
        "lengths": draw_lengths(jax.random.fold_in(keys[19], 71), 0),
        "w_query": normal_values(keys[3], (D, D), D ** -0.5, 0.21875, ((1, 4),)),
        "b_query": normal_values(keys[4], (D,), 0.3, 1.75, ((0, 4),)),
        "w_key": normal_values(keys[5], (D, D), D ** -0.5, 0.21875, ((1, 4),)),
        "w_value": normal_values(keys[6], (D, D), D ** -0.5, 0.21875, ((1, 4),)),
        "b_value": normal_values(keys[7], (D,), 0.3, 1.75, ((0, 4),)),
        "w_out": normal_values(keys[8], (D, D), (D // 16) ** -0.5, 0.875, ((0, 4),)),
        "b_out": normal_values(keys[9], (D,), 0.3, 1.75),
        "norm1_gain": jnp.clip(1.0 + 0.18 * jax.random.normal(keys[10], (D,), jnp.float32), 0.1, 1.9),
        "norm1_shift": normal_values(keys[11], (D,), 0.3, 1.75, (), jnp.float32),
        "w_in": normal_values(keys[12], (D, FF), D ** -0.5, 0.21875, ((1, 4),)),
        "b_in": normal_values(keys[13], (FF,), 0.5, 3.0, ((0, 4),)),
        "w_down": normal_values(keys[14], (FF, D), FF ** -0.5, 0.109375, ((0, 4),)),
        "b_down": normal_values(keys[15], (D,), 0.3, 1.75),
        "norm2_gain": jnp.clip(1.0 + 0.18 * jax.random.normal(keys[16], (D,), jnp.float32), 0.1, 1.9),
        "norm2_shift": normal_values(keys[17], (D,), 0.3, 1.75, (), jnp.float32),
        "cotangent": normal_values(keys[18], (TOKENS, D), 1.0, 6.0, ((0, 32),), jnp.float32),
    }


@jax.custom_vjp
def low(v):
    return lax.optimization_barrier(v.astype(jnp.bfloat16)).astype(jnp.float32)

@jax.custom_vjp
def low_back(v):
    return v

def low_keep(v):
    return (low(v), None)

def low_pass(kept, grad):
    return (grad,)

def back_keep(v):
    return (v, None)

def back_low(kept, grad):
    return (low(grad),)
low.defvjp(low_keep, low_pass)
low_back.defvjp(back_keep, back_low)
EPSILON = 1e-12
FULL_PRECISION = lax.Precision.HIGHEST

def product(left, right):
    return jnp.dot(left, right, precision=FULL_PRECISION)

def norm_rows(values, gain, shift):
    mean = lax.optimization_barrier(jnp.mean(values, axis=-1, keepdims=True))
    centred = values - mean
    spread = lax.optimization_barrier(jnp.mean(centred * centred, axis=-1, keepdims=True))
    return centred * lax.rsqrt(spread + EPSILON) * gain + shift

def row_layout(bucket_kind, length_table):
    row_len = jnp.where(bucket_kind == 0, BLOCK // 4, jnp.where(bucket_kind == 1, BLOCK // 2, BLOCK))
    places = jnp.arange(TOK_DEV, dtype=jnp.int32)
    row_of = places // row_len
    inside = places % row_len
    picked = row_of[:, None] == jnp.arange(ROWS, dtype=jnp.int32)[None, :]
    length_of = lax.optimization_barrier(jnp.sum(jnp.where(picked, length_table[None, :], 0), axis=1))
    return (row_of, inside < length_of)

def attention_rows(queries, key_rows, vals, row_of, valid):
    shape4 = (TOK_DEV // BLOCK, BLOCK, HEADS, HEAD)

    def one_block(block_items):
        query_blk, key_blk, value_blk, row_blk, valid_blk = block_items
        scores = jnp.einsum('qhd,khd->hqk', query_blk, key_blk, precision=FULL_PRECISION) * HEAD ** (-0.5)
        scores = low_back(scores)
        allowed = (row_blk[:, None] == row_blk[None, :]) & valid_blk[None, :]
        scores = jnp.where(allowed[None], scores, -1000000000.0)
        probs = low(jax.nn.softmax(scores, axis=-1))
        return jnp.einsum('hqk,khd->qhd', probs, value_blk, precision=FULL_PRECISION)
    context = lax.map(jax.checkpoint(one_block), (queries.reshape(shape4), key_rows.reshape(shape4), vals.reshape(shape4), row_of.reshape(-1, BLOCK), valid.reshape(-1, BLOCK)))
    return context.reshape(TOK_DEV, D)

def block_group(weights, group_tokens, bucket_kind, length_table):
    w_query, b_query, w_key, w_value, b_value, w_out, b_out, gain1, shift1, w_in, b_in, w_down, b_down, gain2, shift2 = weights
    row_of, valid = row_layout(bucket_kind, length_table)
    queries = low(low_back(product(group_tokens, w_query) + b_query))
    key_rows = low(low_back(product(group_tokens, w_key)))
    vals = low(low_back(product(group_tokens, w_value) + b_value))
    context = low(low_back(attention_rows(queries, key_rows, vals, row_of, valid)))
    attention = low_back(product(context, w_out) + b_out)
    residual = group_tokens + attention
    normed = norm_rows(residual, gain1, shift1)
    pre_act = low_back(product(low(normed), w_in) + b_in)
    activated = low(jax.nn.gelu(pre_act, approximate=False))
    ffn_out = low_back(product(activated, w_down) + b_down)
    return norm_rows(normed + ffn_out, gain2, shift2)

def reference(tokens, bucket, lengths, w_query, b_query, w_key, w_value, b_value, w_out, b_out, norm1_gain, norm1_shift, w_in, b_in, w_down, b_down, norm2_gain, norm2_shift, cotangent):
    weights = tuple((item.astype(jnp.float32) for item in (w_query, b_query, w_key, w_value, b_value, w_out, b_out, norm1_gain, norm1_shift, w_in, b_in, w_down, b_down, norm2_gain, norm2_shift)))
    token_groups = tokens.astype(jnp.float32).reshape(N_DP, TOK_DEV, D)

    def forward(params, groups):

        def one_group(group_items):
            return block_group(params, group_items[0], group_items[1], group_items[2])
        return lax.map(jax.checkpoint(one_group), (groups, bucket, lengths))
    outputs, pull = jax.vjp(forward, weights, token_groups)
    grad_params, grad_groups = pull(cotangent.astype(jnp.float32).reshape(N_DP, TOK_DEV, D))
    return (outputs.reshape(TOKENS, D).astype(jnp.bfloat16), grad_groups.reshape(TOKENS, D), grad_params[0], grad_params[1], grad_params[2], grad_params[3], grad_params[4], grad_params[5], grad_params[6], grad_params[7], grad_params[8], grad_params[9], grad_params[10], grad_params[11], grad_params[12], grad_params[13], grad_params[14])
```

```python
import jax
import jax.numpy as jnp
from jax import lax
from jax.sharding import PartitionSpec as P

HEAD = 64
BLOCK = 512
EPSILON = 1e-12
F32 = jnp.float32
BF16 = jnp.bfloat16


def norm_rows(values, gain, shift):
    mean = jnp.mean(values, axis=-1, keepdims=True)
    centred = values - mean
    spread = jnp.mean(centred * centred, axis=-1, keepdims=True)
    return centred * lax.rsqrt(spread + EPSILON) * gain + shift


def exact_gelu(values):
    return jax.nn.gelu(values, approximate=False)


def product(left, right):
    return jnp.dot(left, right, preferred_element_type=F32)


def rows_product(left, right):
    return lax.dot_general(left, right, (((0,), (0,)), ((), ())), preferred_element_type=F32)


def back_product(left, right):
    return lax.dot_general(left, right, (((1,), (1,)), ((), ())), preferred_element_type=F32)


def row_layout(bucket, lengths, first, token_count):
    bucket_kind = bucket[0]
    row_len = jnp.where(
        bucket_kind == 0, BLOCK // 4, jnp.where(bucket_kind == 1, BLOCK // 2, BLOCK)
    )
    places = first + jnp.arange(token_count, dtype=jnp.int32)
    row_of = places // row_len
    inside = places % row_len
    length_table = lengths[0]
    picked = row_of[:, None] == jnp.arange(length_table.shape[0], dtype=jnp.int32)[None, :]
    length_of = jnp.sum(jnp.where(picked, length_table[None, :], 0), axis=1)
    return (row_of, inside < length_of)


def masked_scores(query_blk, key_blk, row_blk, valid_blk):
    scores = jnp.einsum(
        "qhd,khd->hqk", query_blk, key_blk, preferred_element_type=F32
    ) * HEAD ** (-0.5)
    allowed = (row_blk[:, None] == row_blk[None, :]) & valid_blk[None, :]
    return jnp.where(allowed[None], scores, -1000000000.0)


def blocked(values):
    return values.reshape(values.shape[0] // BLOCK, BLOCK, values.shape[1] // HEAD, HEAD)


def attend_forward(queries, key_rows, vals, row_of, valid):
    def one_block(block_items):
        query_blk, key_blk, value_blk, row_blk, valid_blk = block_items
        scores = masked_scores(query_blk, key_blk, row_blk, valid_blk)
        largest = jnp.max(scores, axis=-1, keepdims=True)
        raised = jnp.exp(scores - largest)
        row_total = jnp.sum(raised, axis=-1, keepdims=True)
        probs = (raised / row_total).astype(BF16)
        context = jnp.einsum("hqk,khd->qhd", probs, value_blk, preferred_element_type=F32)
        return (context, (largest + jnp.log(row_total))[..., 0])

    context, log_total = lax.map(
        one_block,
        (
            blocked(queries),
            blocked(key_rows),
            blocked(vals),
            row_of.reshape(-1, BLOCK),
            valid.reshape(-1, BLOCK),
        ),
    )
    return (context.reshape(queries.shape).astype(BF16), log_total)


def attend_backward(queries, key_rows, vals, grad_context, log_total, row_of, valid):
    def one_block(block_items):
        query_blk, key_blk, value_blk, grad_blk, log_blk, row_blk, valid_blk = block_items
        scores = masked_scores(query_blk, key_blk, row_blk, valid_blk)
        probs = jnp.exp(scores - log_blk[..., None])
        grad_probs = jnp.einsum("qhd,khd->hqk", grad_blk, value_blk, preferred_element_type=F32)
        centre = jnp.sum(probs * grad_probs, axis=-1, keepdims=True)
        grad_scores = (probs * (grad_probs - centre)).astype(BF16)
        grad_queries = jnp.einsum(
            "hqk,khd->qhd", grad_scores, key_blk, preferred_element_type=F32
        ) * HEAD ** (-0.5)
        grad_keys = jnp.einsum(
            "hqk,qhd->khd", grad_scores, query_blk, preferred_element_type=F32
        ) * HEAD ** (-0.5)
        grad_vals = jnp.einsum(
            "hqk,qhd->khd", probs.astype(BF16), grad_blk, preferred_element_type=F32
        )
        return (grad_queries, grad_keys, grad_vals)

    grads = lax.map(
        one_block,
        (
            blocked(queries),
            blocked(key_rows),
            blocked(vals),
            blocked(grad_context),
            log_total,
            row_of.reshape(-1, BLOCK),
            valid.reshape(-1, BLOCK),
        ),
    )
    return tuple(item.reshape(queries.shape).astype(BF16) for item in grads)


def swap(values, axis, bit):
    count = lax.axis_size(axis)
    return lax.ppermute(values, axis, [(at, at ^ bit) for at in range(count)])


def pieces_of(own):
    near = swap(own, "tensor", 1)
    far = swap(own, "tensor", 2)
    return [own, near, far, swap(far, "tensor", 1)]


def dp_bits():
    bits, bit = [], 1
    while bit < lax.axis_size("dp"):
        bits.append(bit)
        bit *= 2
    return bits


def sum_over_dp(values):
    me = lax.axis_index("dp")
    for bit in dp_bits():
        half = values.shape[0] // 2
        mine = (me // bit) % 2
        kept = lax.dynamic_slice_in_dim(values, mine * half, half)
        sent = lax.dynamic_slice_in_dim(values, (1 - mine) * half, half)
        got = swap(sent, "dp", bit)
        values = (kept.astype(F32) + got.astype(F32)).astype(BF16)
    for bit in reversed(dp_bits()):
        mine = (me // bit) % 2
        got = swap(values, "dp", bit)
        values = jnp.where(
            mine == 0, jnp.concatenate((values, got)), jnp.concatenate((got, values))
        )
    return values


def to_owner(parts):
    g0, g1, g2, g3 = [part.astype(BF16) for part in parts]
    far = (g2.astype(F32) + swap(g3, "tensor", 1).astype(F32)).astype(BF16)
    mine = g0.astype(F32) + swap(g1, "tensor", 1).astype(F32)
    mine = (mine + swap(far, "tensor", 2).astype(F32)).astype(BF16)
    return sum_over_dp(mine).astype(F32)


def small_sum(values):
    for bit in (1, 2):
        values = values + swap(values, "tensor", bit)
    for bit in dp_bits():
        values = values + swap(values, "dp", bit)
    return values


def per_device(
    tokens,
    bucket,
    lengths,
    w_query,
    b_query,
    w_key,
    w_value,
    b_value,
    w_out,
    b_out,
    gain1,
    shift1,
    w_in,
    b_in,
    w_down,
    b_down,
    gain2,
    shift2,
    cotangent,
):
    rows = tokens.shape[0]
    width = w_query.shape[1]
    row_of, valid = row_layout(bucket, lengths, lax.axis_index("tensor") * rows, rows)
    biases = pieces_of(jnp.concatenate((b_query, b_value, b_in)))
    w_qkv = pieces_of(jnp.concatenate((w_query, w_key, w_value), axis=1))
    w_outs = pieces_of(w_out)
    w_ins = pieces_of(w_in)
    w_downs = pieces_of(w_down)

    q, k, v = [], [], []
    for weight, bias in zip(w_qkv, biases):
        joined = jnp.concatenate((bias[:width], jnp.zeros_like(bias[:width]), bias[width : 2 * width]))
        out = (product(tokens, weight) + joined.astype(F32)).astype(BF16)
        q.append(out[:, :width])
        k.append(out[:, width : 2 * width])
        v.append(out[:, 2 * width :])
    q, k, v = [jnp.concatenate(item, axis=1) for item in (q, k, v)]
    context, log_total = attend_forward(q, k, v, row_of, valid)
    attention = b_out.astype(F32)
    for at, weight in enumerate(w_outs):
        attention = attention + product(context[:, at * width : (at + 1) * width], weight)
    residual = tokens.astype(F32) + attention
    normed = norm_rows(residual, gain1, shift1)
    normed_low = normed.astype(BF16)
    pre, act = [], []
    ffn_out = b_down.astype(F32)
    for weight, down, bias in zip(w_ins, w_downs, biases):
        pre.append(product(normed_low, weight) + bias[2 * width :].astype(F32))
        act.append(exact_gelu(pre[-1]).astype(BF16))
        ffn_out = ffn_out + product(act[-1], down)
    summed = normed + ffn_out
    result, norm2_pull = jax.vjp(norm_rows, summed, gain2, shift2)
    grad_summed, grad_gain2, grad_shift2 = norm2_pull(cotangent)
    grad_ffn = grad_summed.astype(BF16)
    grad_bdown = jnp.sum(grad_ffn.astype(F32), axis=0)
    grad_downs = [rows_product(item, grad_ffn) for item in act]
    grad_ins, grad_bins = [], []
    grad_normed = grad_summed
    for at in range(4):
        grad_act = back_product(grad_ffn, w_downs[at])
        grad_pre = jax.vjp(exact_gelu, pre[at])[1](grad_act)[0].astype(BF16)
        grad_ins.append(rows_product(normed_low, grad_pre))
        grad_bins.append(jnp.sum(grad_pre.astype(F32), axis=0))
        grad_normed = grad_normed + back_product(grad_pre, w_ins[at])
    grad_resid, grad_gain1, grad_shift1 = jax.vjp(norm_rows, residual, gain1, shift1)[1](
        grad_normed
    )
    grad_attn = grad_resid.astype(BF16)
    grad_bout = jnp.sum(grad_attn.astype(F32), axis=0)
    grad_outs = [
        rows_product(context[:, at * width : (at + 1) * width], grad_attn) for at in range(4)
    ]
    grad_context = jnp.concatenate(
        [back_product(grad_attn, weight).astype(BF16) for weight in w_outs], axis=1
    )
    gq, gk, gv = attend_backward(q, k, v, grad_context, log_total, row_of, valid)
    grad_tokens = grad_resid
    grad_qkvs, grad_bq, grad_bv = [], [], []
    for at in range(4):
        cols = slice(at * width, (at + 1) * width)
        joined = jnp.concatenate((gq[:, cols], gk[:, cols], gv[:, cols]), axis=1)
        grad_qkvs.append(rows_product(tokens, joined))
        grad_tokens = grad_tokens + back_product(joined, w_qkv[at])
        sums = jnp.sum(joined.astype(F32), axis=0)
        grad_bq.append(sums[:width])
        grad_bv.append(sums[2 * width :])

    grad_wd = to_owner(grad_downs)
    grad_wi = to_owner(grad_ins)
    grad_wo = to_owner(grad_outs)
    grad_wqkv = to_owner(grad_qkvs)

    me = lax.axis_index("tensor")
    order = me ^ jnp.arange(4)
    split = jnp.stack(
        [jnp.concatenate((grad_bq[at], grad_bv[at], grad_bins[at])) for at in range(4)]
    )
    split = jnp.take(split, order, axis=0)
    small = jnp.stack((grad_bout, grad_gain1, grad_shift1, grad_bdown, grad_gain2, grad_shift2))
    flat = small_sum(jnp.concatenate((small.reshape(-1), split.reshape(-1))).reshape(-1, 128))
    flat = flat.reshape(-1)
    small = flat[: small.size].reshape(small.shape)
    split = lax.dynamic_index_in_dim(flat[small.size :].reshape(split.shape), me, 0, False)
    return (
        result.astype(BF16),
        grad_tokens,
        grad_wqkv[:, :width],
        split[:width],
        grad_wqkv[:, width : 2 * width],
        grad_wqkv[:, 2 * width :],
        split[width : 2 * width],
        grad_wo,
        small[0],
        small[1],
        small[2],
        grad_wi,
        split[2 * width :],
        grad_wd,
        small[3],
        small[4],
        small[5],
    )


def solution(mesh):
    group = P(("dp", "tensor"), None)
    column, row, part, whole = P(None, "tensor"), P("tensor", None), P("tensor"), P()
    in_specs = (
        group, P("dp"), P("dp", None), column, part, column, column, part, row,
        whole, whole, whole, column, part, row, whole, whole, whole, group,
    )
    out_specs = (
        group, group, column, part, column, column, part, row,
        whole, whole, whole, column, part, row, whole, whole, whole,
    )
    return jax.shard_map(
        per_device, mesh=mesh, in_specs=in_specs, out_specs=out_specs, check_vma=False
    )
```

```python
import functools

import jax
import jax.numpy as jnp
from jax import lax
from jax.experimental import pallas as pl
from jax.experimental.pallas import tpu as pltpu
from jax.sharding import PartitionSpec as P

HEAD = 64
BLOCK = 512
LANES = 128
EPSILON = 1e-12
EXTRA = 32
TAIL = 128
MASKED = -(2.0**30)
ROOT_HALF = 0.7071067811865476
PHI_SCALE = 0.3989422804014327
COSTS = {"arrange_out": 10, "attend": 10, "join": 6, "widen": 8, "narrow": 13, "down_grad": 6, "ffn_back": 0, "attend_back": 24}
COST_UNIT = 10**11
F32 = jnp.float32
BF16 = jnp.bfloat16
VMEM = 56 << 20


def dot(left, right, left_dim, right_dim):
    return lax.dot_general(
        left, right, (((left_dim,), (right_dim,)), ((), ())), preferred_element_type=F32
    )


def mean_rows(values):
    return jnp.mean(values, axis=-1, keepdims=True)


def unit_rows(values):
    centred = values - mean_rows(values)
    scale = lax.rsqrt(mean_rows(centred * centred) + EPSILON)
    return centred * scale, scale


def norm_back(grad, unit, scale, gain):
    e = grad * gain
    return scale * (e - mean_rows(e) - unit * mean_rows(e * unit))


def column_sum(values):
    return jnp.sum(values, axis=0, keepdims=True)


def call(kernel, name, steps, ins, outs, scratch=(), wait=()):
    count = len(ins)

    def body(*refs):
        kernel(*refs[:count], *refs[count + len(wait) :])

    return pl.pallas_call(
        body,
        grid=(steps,),
        in_specs=[
            pl.BlockSpec(memory_space=pltpu.SMEM) if block is None else pl.BlockSpec(block, index)
            for _, block, index in ins
        ]
        + [pl.BlockSpec(memory_space=pl.ANY)] * len(wait),
        out_specs=[pl.BlockSpec(block, index) for _, _, block, index in outs],
        out_shape=[jax.ShapeDtypeStruct(shape, dtype) for shape, dtype, _, _ in outs],
        scratch_shapes=list(scratch),
        compiler_params=pltpu.CompilerParams(
            dimension_semantics=("arbitrary",), vmem_limit_bytes=VMEM
        ),
        cost_estimate=pl.CostEstimate(flops=COSTS.get(name, 0) * COST_UNIT + 1, bytes_accessed=1, transcendentals=0),
        name=name,
    )(*[item[0] for item in ins], *wait)


def whole(array):
    rank = array.ndim
    return (array, array.shape, lambda i: (0,) * rank)


def tiled(array, rows):
    return (array, (rows, array.shape[1]), lambda i: (i, 0))


def tiled_out(shape, dtype, rows):
    return (shape, dtype, (rows, shape[1]), lambda i: (i, 0))


def whole_out(shape, dtype):
    rank = len(shape)
    return (shape, dtype, shape, lambda i: (0,) * rank)


def head_scores(q_ref, k_ref, qf, kf, pair, head):
    cols = slice(pair * LANES, (pair + 1) * LANES)
    lane = lax.broadcasted_iota(jnp.int32, (1, LANES), 1)
    queries = q_ref[:, cols]
    queries = jnp.where(lane // HEAD == head, queries, jnp.zeros_like(queries))
    keys = jnp.concatenate([k_ref[:, cols], kf], axis=1)
    return dot(keys, jnp.concatenate([queries, qf], axis=1), 1, 1)


def mask_features(first, bucket_ref, lengths_ref):
    kind = bucket_ref[0]
    row_len = jnp.where(kind == 0, BLOCK // 4, jnp.where(kind == 1, BLOCK // 2, BLOCK))
    shift = jnp.where(kind == 0, 7, jnp.where(kind == 1, 8, 9))
    slot = lax.broadcasted_iota(jnp.int32, (BLOCK, LANES), 0)
    lane = lax.broadcasted_iota(jnp.int32, (BLOCK, LANES), 1)
    same = lax.shift_right_logical(slot, shift) == lane
    base = lax.shift_right_logical(first, shift)
    length = jnp.zeros((BLOCK, LANES), jnp.int32)
    for at in range(4):
        length = jnp.where(lane == at, lengths_ref[0, base + at], length)
    seen = same & ((slot & (row_len - 1)) < length)
    queries = jnp.where(same, 1.0, 0.0).astype(BF16)
    keys = jnp.where((lane < 4) & jnp.logical_not(seen), MASKED, 0.0).astype(BF16)
    return queries, keys


def lanes_of(first, second):
    cut = 2 * HEAD
    return (first, 0, cut), (second, 0, cut), (first, cut, HEAD), (second, cut, HEAD)


def stack_rows(out, start, first, second, offset):
    for ref, at, size in lanes_of(first, second):
        out[start : start + size] = ref[offset + at : offset + at + size]
        start += size


def attend_body(tok_ref, near_ref, far_ref, qf, kf, q_ref, k_ref, v_ref, c_ref, lse_ref, wq_ref, wk_ref, wv_ref):
    span = q_ref.shape[1]
    width = span // 2

    @pl.when(pl.program_id(0) == 0)
    def _():
        for at, w_ref in enumerate((wq_ref, wk_ref, wv_ref)):
            stack_rows(w_ref, 0, near_ref, far_ref, at * width)

    tokens = tok_ref[...]
    bias_row = 4 * width
    near, far = near_ref[bias_row : bias_row + 1].astype(F32), far_ref[bias_row : bias_row + 1].astype(F32)
    bq, bv = [
        jnp.concatenate(
            [row[:, start + at : start + at + size] for row, at, size in lanes_of(near, far)], axis=1
        )
        for start in (0, width)
    ]
    q = (dot(tokens, wq_ref[...], 1, 1) + bq).astype(BF16)
    q_ref[...] = q * jnp.asarray(HEAD**-0.5, BF16)
    k_ref[...] = dot(tokens, wk_ref[...], 1, 1).astype(BF16)
    v_ref[...] = (dot(tokens, wv_ref[...], 1, 1) + bv).astype(BF16)
    items = [(pair, head) for pair in range(span // LANES) for head in range(2)]
    ahead = head_scores(q_ref, k_ref, qf, kf, *items[0])
    done = []
    for at, (pair, head) in enumerate(items):
        scores = ahead
        if at + 1 < len(items):
            ahead = head_scores(q_ref, k_ref, qf, kf, *items[at + 1])
        cols = slice(pair * LANES, (pair + 1) * LANES)
        if head == 0:
            vals = v_ref[:, cols].T
        largest = jnp.max(scores, axis=0, keepdims=True)
        raised = jnp.exp(scores - largest)
        total = jnp.sum(raised, axis=0, keepdims=True)
        lse_ref[0, at : at + 1, :] = largest + jnp.log(total)
        mixed = dot(vals[head * HEAD : (head + 1) * HEAD], raised.astype(BF16), 1, 0)
        done.append(mixed * (1.0 / total))
        if head == 1:
            c_ref[:, cols] = jnp.concatenate(done, axis=0).T.astype(BF16)
            done = []


def attend_first(bucket_ref, lengths_ref, place_ref, tok_ref, near_ref, far_ref, *outs):
    qf_ref, kf_ref = outs[8:]
    first = (place_ref[0] * pl.num_programs(0) + pl.program_id(0)) * BLOCK
    qf_ref[...], kf_ref[...] = mask_features(first, bucket_ref, lengths_ref)
    attend_body(tok_ref, near_ref, far_ref, qf_ref[...], kf_ref[...], *outs[:8])


def attend_second(qf_ref, kf_ref, tok_ref, near_ref, far_ref, *outs):
    attend_body(tok_ref, near_ref, far_ref, qf_ref[...], kf_ref[...], *outs)


def attend(lead, tokens, near, far, wait=()):
    rows, depth = tokens.shape
    span = (near.shape[0] - EXTRA) // 2
    heads = span // HEAD
    blocks = rows // BLOCK
    first = len(lead) == 3
    if first:
        ins = [(item, None, None) for item in lead]
    else:
        ins = [tiled(item, BLOCK) for item in lead]
    outs = [tiled_out((rows, span), BF16, BLOCK)] * 4
    outs += [((blocks, heads, BLOCK), F32, (1, heads, BLOCK), lambda i: (i, 0, 0))]
    outs += [whole_out((span, depth), BF16)] * 3
    if first:
        outs += [tiled_out((rows, LANES), BF16, BLOCK)] * 2
    return call(
        attend_first if first else attend_second,
        "attend",
        blocks,
        ins + [tiled(tokens, BLOCK), whole(near), whole(far)],
        outs,
        wait=wait,
    )


def out_rows(packed):
    rows, columns = packed.shape
    width = (rows - EXTRA) // 4
    return (packed, (width, columns), lambda i: (3, 0))


def join_kernel(
    tok_ref, cn_ref, cf_ref, w0_ref, w1_ref, w2_ref, w3_ref, b_ref, g_ref, s_ref, res_ref, low_ref, w_s,
):
    span = cn_ref.shape[1]

    @pl.when(pl.program_id(0) == 0)
    def _():
        stack_rows(w_s, 0, w0_ref, w1_ref, 0)
        stack_rows(w_s, span, w2_ref, w3_ref, 0)

    out = dot(cn_ref[...], w_s[:span], 1, 0) + dot(cf_ref[...], w_s[span:], 1, 0)
    residual = tok_ref[...].astype(F32) + (out + b_ref[...])
    res_ref[...] = residual
    unit, _ = unit_rows(residual)
    low_ref[...] = (unit * g_ref[...] + s_ref[...]).astype(BF16)


def join(tokens, ctx_near, ctx_far, pieces, b_out, gain, shift, wait=()):
    rows, depth = tokens.shape
    tile = 256
    return call(
        join_kernel,
        "join",
        rows // tile,
        [tiled(tokens, tile), tiled(ctx_near, tile), tiled(ctx_far, tile)]
        + [out_rows(piece) for piece in pieces]
        + [whole(b_out), whole(gain), whole(shift)],
        [tiled_out((rows, depth), F32, tile), tiled_out((rows, depth), BF16, tile)],
        [pltpu.VMEM((depth, depth), BF16)],
        wait=wait,
    )


def widen_kernel(n_ref, wa_ref, wb_ref, ba_ref, bb_ref, act_ref, fac_ref):
    normed = n_ref[...]
    wide = wa_ref.shape[1]
    for at, (ref, b_ref) in enumerate(((wa_ref, ba_ref), (wb_ref, bb_ref))):
        cols = slice(at * wide, (at + 1) * wide)
        pre = dot(normed, ref[...], 1, 0) + b_ref[1:2, :wide].astype(F32)
        below = 0.5 + 0.5 * lax.erf(pre * ROOT_HALF)
        act_ref[:, cols] = (pre * below).astype(BF16)
        density = jnp.exp(-0.5 * pre * pre) * PHI_SCALE
        fac_ref[:, cols] = (below + pre * density).astype(BF16)


def bias_rows(packed):
    rows, columns = packed.shape
    return (packed, (EXTRA, columns), lambda i: (rows // EXTRA - 1, 0))


def widen(normed, wa, wb, bias_a, bias_b, wait=()):
    rows, depth = normed.shape
    tile = 256
    units = 2 * wa.shape[1]
    return call(
        widen_kernel,
        "widen",
        rows // tile,
        [tiled(normed, tile), whole(wa), whole(wb), bias_rows(bias_a), bias_rows(bias_b)],
        [tiled_out((rows, units), BF16, tile)] * 2,
        wait=wait,
    )


def narrow_kernel(
    an_ref, af_ref, w0_ref, w1_ref, w2_ref, w3_ref, res_ref, g1_ref, s1_ref, bd_ref, g2_ref, s2_ref, cot_ref,
    out_ref, gs_ref, gf_ref, sums_ref,
):
    unit1, _ = unit_rows(res_ref[...])
    wide = w0_ref.shape[0]
    out = dot(an_ref[:, :wide], w0_ref[...], 1, 0) + dot(an_ref[:, wide:], w1_ref[...], 1, 0)
    out = out + dot(af_ref[:, :wide], w2_ref[...], 1, 0) + dot(af_ref[:, wide:], w3_ref[...], 1, 0)
    summed = (unit1 * g1_ref[...] + s1_ref[...]) + (out + bd_ref[...])
    unit, scale = unit_rows(summed)
    out_ref[...] = (unit * g2_ref[...] + s2_ref[...]).astype(BF16)
    cot = cot_ref[...]
    grad = norm_back(cot, unit, scale, g2_ref[...])
    gs_ref[...] = grad
    low = grad.astype(BF16)
    gf_ref[...] = low

    @pl.when(pl.program_id(0) == 0)
    def _():
        sums_ref[...] = jnp.zeros_like(sums_ref)

    sums_ref[0:1] += column_sum(cot * unit)
    sums_ref[1:2] += column_sum(cot)
    sums_ref[2:3] += column_sum(low.astype(F32))


def narrow(act_near, act_far, w_downs, residual, gain1, shift1, b_down, gain2, shift2, cotangent, wait=()):
    rows, depth = residual.shape
    tile = 256
    return call(
        narrow_kernel,
        "narrow",
        rows // tile,
        [tiled(act_near, tile), tiled(act_far, tile)]
        + [whole(w) for w in w_downs]
        + [tiled(residual, tile)]
        + [whole(v) for v in (gain1, shift1, b_down, gain2, shift2)]
        + [tiled(cotangent, tile)],
        [
            tiled_out((rows, depth), BF16, tile),
            tiled_out((rows, depth), F32, tile),
            tiled_out((rows, depth), BF16, tile),
            whole_out((8, depth), F32),
        ],
        wait=wait,
    )


def down_grad_kernel(gf_ref, acta_ref, actb_ref, da_ref, db_ref):
    grad = gf_ref[...]
    da_ref[...] = dot(acta_ref[...], grad, 0, 0).astype(BF16)
    db_ref[...] = dot(actb_ref[...], grad, 0, 0).astype(BF16)


def half_tile(array, which, tile):
    steps = array.shape[1] // 2 // tile
    return (array, (array.shape[0], tile), lambda i: (0, which * steps + i))


def down_grad(grad_ffn, acts, wait=()):
    rows, depth = grad_ffn.shape
    units = acts[0][0].shape[1] // 2
    tile = 256
    return call(
        down_grad_kernel,
        "down_grad",
        units // tile,
        [whole(grad_ffn)] + [half_tile(*item, tile) for item in acts],
        [tiled_out((units, depth), BF16, tile)] * 2,
        wait=wait,
    )


def ffn_back_kernel(gf_ref, n_ref, gn_in_ref, *refs):
    count = (len(refs) - 5) // 2
    piece_a, piece_b, (ga_ref, gb_ref, gba_ref, gbb_ref, gn_ref) = refs[:count], refs[count:-5], refs[-5:]

    @pl.when(pl.program_id(0) == 0)
    def _():
        gn_ref[...] = gn_in_ref[...]

    grad = gf_ref[...]
    for (fac_ref, wd_ref, wi_ref, *got), g_ref, gbias_ref in ((piece_a, ga_ref, gba_ref), (piece_b, gb_ref, gbb_ref)):
        grad_pre = (dot(grad, wd_ref[...], 1, 1) * fac_ref[...].astype(F32)).astype(BF16)
        gbias_ref[...] = column_sum(grad_pre.astype(F32))
        out = dot(n_ref[...], grad_pre, 0, 0)
        if got:
            out = out + got[0][...].astype(F32)
        g_ref[...] = out.astype(BF16)
        gn_ref[...] += dot(grad_pre, wi_ref[...], 1, 1)


def ffn_back(grad_ffn, normed, grad_normed, pieces, wait=()):
    rows, depth = grad_ffn.shape
    units = pieces[0][1].shape[0]
    tile = 256
    steps = units // tile
    column = lambda i: (0, i)
    ins = [whole(grad_ffn), whole(normed), whole(grad_normed)]
    for fac, wd, wi, *got in pieces:
        ins += [half_tile(*fac, tile), tiled(wd, tile), (wi, (depth, tile), column)]
        ins += [(item, (depth, tile), column) for item in got]
    return call(
        ffn_back_kernel,
        "ffn_back",
        steps,
        ins,
        [((depth, units), BF16, (depth, tile), column)] * 2
        + [((1, units), F32, (1, tile), column)] * 2
        + [whole_out((rows, depth), F32)],
        wait=wait,
    )


def attend_back_core(q_ref, k_ref, v_ref, lse_ref, qf, kf, dqkv_s, gctx_s):
    span = q_ref.shape[1]
    items = [(pair, head) for pair in range(span // LANES) for head in range(2)]
    lane = lax.broadcasted_iota(jnp.int32, (1, LANES), 1)

    def front(pair, head):
        cols = slice(pair * LANES, (pair + 1) * LANES)
        scores = head_scores(q_ref, k_ref, qf, kf, pair, head)
        out = gctx_s[:, cols]
        out = jnp.where(lane // HEAD == head, out, jnp.zeros_like(out))
        return scores, dot(v_ref[:, cols], out, 1, 1)

    ahead = front(*items[0])
    for at, (pair, head) in enumerate(items):
        scores, grad_probs = ahead
        if at + 1 < len(items):
            ahead = front(*items[at + 1])
        cols = slice(pair * LANES, (pair + 1) * LANES)
        mine = lane // HEAD == head
        queries, out = q_ref[:, cols], gctx_s[:, cols]
        queries = jnp.where(mine, queries, jnp.zeros_like(queries))
        out = jnp.where(mine, out, jnp.zeros_like(out))
        if head == 0:
            keys = (k_ref[:, cols] * jnp.asarray(HEAD**-0.5, BF16)).T
            dqs, dk, dv = [], 0.0, 0.0
        probs = jnp.exp(scores - lse_ref[0, at : at + 1, :])
        centre = jnp.sum(probs * grad_probs, axis=0, keepdims=True)
        grad_scores = (probs * (grad_probs - centre)).astype(BF16)
        dqs.append(dot(keys[head * HEAD : (head + 1) * HEAD], grad_scores, 1, 0))
        dk = dk + dot(grad_scores, queries, 1, 0)
        dv = dv + dot(probs.astype(BF16), out, 1, 0)
        if head == 1:
            start = pair * LANES
            dqkv_s[:, start : start + LANES] = jnp.concatenate(dqs, axis=0).T.astype(BF16)
            dqkv_s[:, span + start : span + start + LANES] = dk.astype(BF16)
            dqkv_s[:, 2 * span + start : 2 * span + start + LANES] = dv.astype(BF16)


def attend_back_body(
    gattn, tok_ref, c_ref, q_ref, k_ref, v_ref, lse_ref, qf_ref, kf_ref, wq_ref, wk_ref, wv_ref, wa_ref, wb_ref,
    fa_ref, fb_ref, sums2_ref, sums1_ref, ga_ref, gb_ref, w_s, wo_s, gctx_s, dqkv_s, gw_s, bias_s,
):
    step = pl.program_id(0)
    span = q_ref.shape[1]
    width = span // 2
    cut = 2 * HEAD

    @pl.when(step == 0)
    def _():
        for at, ref in enumerate((wq_ref, wk_ref, wv_ref)):
            w_s[at * span : (at + 1) * span] = ref[...]
        stack_rows(wo_s, 0, wa_ref, wb_ref, 0)
        gw_s[...] = jnp.zeros_like(gw_s)
        bias_s[...] = jnp.zeros_like(bias_s)

    gctx_s[...] = dot(gattn, wo_s[...], 1, 1).astype(BF16)
    gw_s[3 * span :] += dot(c_ref[...], gattn, 0, 0)
    attend_back_core(q_ref, k_ref, v_ref, lse_ref, qf_ref[...], kf_ref[...], dqkv_s, gctx_s)
    dqkv = dqkv_s[...]
    gw_s[: 3 * span] += dot(dqkv, tok_ref[...], 0, 0)
    bias_s[0:1] += column_sum(dqkv[:, :span].astype(F32))
    bias_s[1:2] += column_sum(dqkv[:, 2 * span :].astype(F32))

    @pl.when(step == pl.num_programs(0) - 1)
    def _():
        for which, (ref, f_ref) in enumerate(((ga_ref, fa_ref), (gb_ref, fb_ref))):
            two, last = which * cut, 2 * cut + which * HEAD
            for at in range(4):
                start, own = at * span, at * width
                ref[own : own + cut] = gw_s[start + two : start + two + cut].astype(BF16)
                ref[own + cut : own + width] = gw_s[start + last : start + last + HEAD].astype(BF16)
            bias = bias_s[...]
            row = [bias[at : at + 1, lo : lo + size] for at in range(2) for lo, size in ((two, cut), (last, HEAD))]
            row = jnp.concatenate(row + [jnp.zeros((1, ref.shape[1] - span), F32)], axis=1)
            extra = [row, f_ref[...], sums1_ref[0:3], sums2_ref[0:3]]
            extra.append(jnp.zeros((ref.shape[0] - 4 * width - 8, ref.shape[1]), F32))
            ref[4 * width :] = jnp.concatenate(extra, axis=0).astype(BF16)

    return dot(dqkv, w_s[...], 1, 0)


def attend_back_first(gn_ref, res_ref, g1_ref, *rest):
    ins, (ga_ref, gb_ref, gt_ref, gattn_ref, sums_ref), scratch = rest[:16], rest[16:21], rest[21:]
    unit, scale = unit_rows(res_ref[...])
    grad = gn_ref[...]
    resid = norm_back(grad, unit, scale, g1_ref[...])
    low = resid.astype(BF16)
    gattn_ref[...] = low

    @pl.when(pl.program_id(0) == 0)
    def _():
        sums_ref[...] = jnp.zeros_like(sums_ref)

    sums_ref[0:1] += column_sum(low.astype(F32))
    sums_ref[1:2] += column_sum(grad * unit)
    sums_ref[2:3] += column_sum(grad)
    gt_ref[...] = resid
    gt_ref[...] += attend_back_body(low, *ins, sums_ref, ga_ref, gb_ref, *scratch)


def attend_back_next(gattn_ref, gtin_ref, *rest):
    ins, (ga_ref, gb_ref, gt_ref), scratch = rest[:17], rest[17:20], rest[20:]
    gt_ref[...] = gtin_ref[...] + attend_back_body(gattn_ref[...], *ins, ga_ref, gb_ref, *scratch)


def attend_back(lead, tokens, saved, pieces, sums, wait=()):
    ctx, q, k, v, lse, qf, kf, wq, wk, wv = saved
    rows, depth = tokens.shape
    heads = lse.shape[1]
    blocks = rows // BLOCK
    first = len(lead) == 3
    span = q.shape[1]
    ins = [tiled(item, BLOCK) if item.shape[0] == rows else whole(item) for item in lead]
    ins += [tiled(item, BLOCK) for item in (tokens, ctx, q, k, v)]
    ins += [(lse, (1, heads, BLOCK), lambda i: (i, 0, 0)), tiled(qf, BLOCK), tiled(kf, BLOCK)]
    ins += [whole(item) for item in (wq, wk, wv)] + [out_rows(item) for item in pieces]
    ins += [whole(item) for item in sums]
    bundle = (2 * span + TAIL, depth)
    outs = [whole_out(bundle, BF16)] * 2 + [tiled_out((rows, depth), F32, BLOCK)]
    if first:
        outs += [tiled_out((rows, depth), BF16, BLOCK), whole_out((8, depth), F32)]
    return call(
        attend_back_first if first else attend_back_next,
        "attend_back",
        blocks,
        ins,
        outs,
        [
            pltpu.VMEM((3 * span, depth), BF16),
            pltpu.VMEM((span, depth), BF16),
            pltpu.VMEM((BLOCK, span), BF16),
            pltpu.VMEM((BLOCK, 3 * span), BF16),
            pltpu.VMEM((4 * span, depth), F32),
            pltpu.VMEM((8, span), F32),
        ],
        wait=wait,
    )


def picked(kernel, name, index, steps, ins, outs, wait=(), cost=10):
    count = len(ins)

    def body(_, *refs):
        kernel(*refs[:count], *refs[count + len(wait) :])

    anywhere = pl.BlockSpec(memory_space=pl.ANY)
    return pl.pallas_call(
        body,
        grid_spec=pltpu.PrefetchScalarGridSpec(
            num_scalar_prefetch=1,
            grid=(steps,),
            in_specs=[pl.BlockSpec(block, at) for _, block, at in ins] + [anywhere] * len(wait),
            out_specs=[pl.BlockSpec(block, at) for _, _, block, at in outs],
        ),
        out_shape=[jax.ShapeDtypeStruct(shape, dtype) for shape, dtype, _, _ in outs],
        compiler_params=pltpu.CompilerParams(dimension_semantics=("arbitrary",), vmem_limit_bytes=VMEM),
        cost_estimate=pl.CostEstimate(flops=cost * COST_UNIT + 1, bytes_accessed=1, transcendentals=0),
        name=name,
    )(index.astype(jnp.int32)[None], *[item[0] for item in ins], *wait)


def tiles_in(rows):
    for steps in (4, 3, 2):
        if rows % (16 * steps) == 0 and rows // steps >= 96:
            return steps
    return 1


def combine(terms, index=None, count=1, after=(), cost=10):
    if index is None:
        index = jnp.zeros((), jnp.int32)
    rows, columns = terms[0].shape
    size = rows // count
    steps = tiles_in(size)
    tile = size // steps

    def chunk(k):
        return lambda i, at: ((at[0] ^ k) * steps + i, 0)

    def kernel(*refs):
        for k in range(count):
            total = sum(ref[...].astype(F32) for ref in refs[k * len(terms) : (k + 1) * len(terms)])
            refs[count * len(terms) + k][...] = total.astype(BF16)

    return picked(
        kernel,
        "combine",
        index,
        steps,
        [(term, (tile, columns), chunk(k)) for k in range(count) for term in terms],
        [((size, columns), BF16, (tile, columns), lambda i, at: (i, 0))] * count,
        after,
        cost,
    )


def arrange(parts, index, sizes=None, split=1, after=(), cost=10):
    size, columns = parts[0].shape
    count = len(parts)
    if sizes is None:
        each = size // split

        def kernel(*refs):
            for k in range(count):

                @pl.when(pl.program_id(0) == k)
                def _(k=k):
                    for out in range(split):
                        refs[count + out][...] = refs[k][out * each : (out + 1) * each]

        return picked(
            kernel,
            "arrange",
            index,
            count,
            [(part, part.shape, lambda i, at: (0, 0)) for part in parts],
            [((count * each, columns), BF16, (each, columns), lambda i, at: (at[0] ^ i, 0))] * split,
            after,
            cost,
        )

    def kernel_out(index_ref, *refs):
        for here in range(count):

            @pl.when(index_ref[0] == here)
            def _(here=here):
                start = 0
                for out in refs[count:]:
                    end = start + out.shape[0]
                    for k in range(count):
                        low = (here ^ k) * size
                        lo, hi = max(start, low), min(end, low + size)
                        if lo < hi:
                            out[lo - start : hi - start] = refs[k][lo - low : hi - low].astype(F32)
                    start = end

    return call(
        kernel_out,
        "arrange_out",
        1,
        [(index.astype(jnp.int32)[None], None, None)] + [whole(part) for part in parts],
        [whole_out((rows, columns), F32) for rows in sizes],
    )


def swap(values, axis, bit):
    count = lax.axis_size(axis)
    return lax.ppermute(values, axis, [(at, at ^ bit) for at in range(count)])


def gate(values, *after):
    def kernel(*refs):
        pass

    anywhere = pl.BlockSpec(memory_space=pl.ANY)
    return pl.pallas_call(
        kernel,
        in_specs=[anywhere] * (1 + len(after)),
        out_specs=anywhere,
        out_shape=jax.ShapeDtypeStruct(values.shape, values.dtype),
        input_output_aliases={0: 0},
        name="gate",
    )(values, *after)


def dp_bits():
    bits, bit = [], 1
    while bit < lax.axis_size("dp"):
        bits.append(bit)
        bit *= 2
    return bits


def groups(bits):
    return [bits[:1]] + [bits[at : at + 2] for at in range(1, len(bits), 2)]


def spot(bits):
    me = lax.axis_index("dp")
    at = sum(((me // bit) % 2) << i for i, bit in enumerate(bits))
    return at, [sum(bit for i, bit in enumerate(bits) if k >> i & 1) for k in range(1 << len(bits))]


def scatter(terms, bits, after=(), cost=10):
    at, far = spot(bits)
    kept, *sent = combine(terms, at, len(far), after, cost)
    return [kept] + [swap(item, "dp", distance) for item, distance in zip(sent, far[1:])]


def sum_whole(values, steps):
    for bit in [bit for step in steps for bit in step]:
        (values,) = combine((values, swap(values, "dp", bit)))
    return values


def gather(values, bits):
    _, far = spot(bits)
    return [values] + [swap(values, "dp", distance) for distance in far[1:]]


def ordered(parts, bits, sizes=None):
    return arrange(parts, spot(bits)[0], sizes)


def parity():
    me = lax.axis_index("dp")
    return (me ^ (me >> 1)) % 2


def my_half(arrays):
    columns = arrays[0].shape[1]
    quarters = [array.shape[0] // 4 for array in arrays]

    def kernel(*refs):
        ins, outs = refs[: 2 * len(arrays)], refs[2 * len(arrays) :]
        for part in range(2):
            start = 0
            for at, rows in enumerate(quarters):
                outs[part][start : start + rows] = ins[2 * at + part][...]
                start += rows

    return picked(
        kernel,
        "my_half",
        parity(),
        1,
        [
            (array, (rows, columns), lambda i, at, part=part: (at[0] * 2 + part, 0))
            for array, rows in zip(arrays, quarters)
            for part in range(2)
        ],
        [((sum(quarters), columns), BF16, (sum(quarters), columns), lambda i, at: (0, 0))] * 2,
    )


def other_half(first, second):
    return swap(first, "dp", 1), swap(second, "dp", 2)


def per_device(
    tokens, bucket, lengths, w_query, b_query, w_key, w_value, b_value, w_out, b_out, gain1, shift1,
    w_in, b_in, w_down, b_down, gain2, shift2, cotangent,
):
    rows, depth = tokens.shape
    width = w_query.shape[1]
    me = lax.axis_index("tensor")
    line = lambda v: v.astype(F32)[None]
    b_out, gain1, shift1, b_down, gain2, shift2 = map(line, (b_out, gain1, shift1, b_down, gain2, shift2))

    row = jnp.concatenate((b_query, b_value, jnp.zeros((depth - 2 * width,), BF16)))
    biases = jnp.pad(jnp.stack((row, b_in)), ((0, EXTRA - 2), (0, 0)))
    own = jnp.concatenate((w_query.T, w_key.T, w_value.T, w_out, biases))
    p1 = swap(own, "tensor", 1)
    pa, pb = [swap(item, "tensor", 2) for item in my_half((own,))]
    wide = my_half((w_in, w_down))
    wa, wb = [swap(item, "tensor", 2) for item in wide]
    in1 = swap(w_in, "tensor", 1)
    down1 = swap(w_down, "tensor", 1)

    place_y = me.astype(jnp.int32)[None]
    qn, kn, vn, cn, lsen, *wn, qf, kf = attend((bucket, lengths, place_y), tokens, own, p1, wide)
    pa, pb = gate(pa, cn), gate(pb, cn)
    (p2,) = arrange((pa, pb, *other_half(pa, pb)), 2 * parity())
    p3 = swap(p2, "tensor", 1)
    qr, kr, vr, cr, lser, *wr = attend((qf, kf), tokens, p2, p3)
    wa, wb = gate(wa, cr), gate(wb, cr)
    others = other_half(wa, wb)
    residual, normed = join(tokens, cn, cr, (own, p1, p2, p3), b_out, gain1, shift1, (wa, wb))
    actn, facn = widen(normed, w_in, in1, own, p1)
    in2, down2 = arrange((wa, wb, *others), 2 * parity(), split=2, after=(actn,))
    in3, down3 = swap(in2, "tensor", 1), swap(down2, "tensor", 1)
    actr, facr = widen(normed, in2, in3, p2, p3)
    block_out, grad_summed, grad_ffn, sums2 = narrow(
        actn, actr, (w_down, down1, down2, down3), residual, gain1, shift1, b_down, gain2, shift2, cotangent
    )
    low, *highs = groups(dp_bits())
    d3, d2 = down_grad(grad_ffn, ((actr, 1), (actr, 0)))
    d1, d0 = down_grad(grad_ffn, ((actn, 1), (actn, 0)))
    (dfar,) = combine((d2, swap(d3, "tensor", 1)), after=(d0,), cost=10)
    i3, i2, fb3, fb2, grad_normed = ffn_back(
        grad_ffn, normed, grad_summed, (((facr, 1), down3, in3), ((facr, 0), down2, in2)), (dfar,)
    )
    i1, i0, fb1, fb0, grad_normed = ffn_back(
        grad_ffn, normed, grad_normed, (((facn, 1), down1, in1), ((facn, 0), w_down, w_in))
    )
    dfar = swap(dfar, "tensor", 2)
    i1 = swap(gate(i1, dfar), "tensor", 1)
    (ifar,) = combine((i2, swap(i3, "tensor", 1)), after=(i0,), cost=10)
    dsum = scatter((d0, swap(d1, "tensor", 1), dfar), low, (i0,), 10)
    saved_r = (cr, qr, kr, vr, lser, qf, kf, *wr)
    saved_n = (cn, qn, kn, vn, lsen, qf, kf, *wn)
    a2, a3, grad_tokens, grad_attn, sums1 = attend_back(
        (grad_normed, residual, gain1), tokens, saved_r, (p2, p3), (fb2, fb3, sums2), (dsum[0], ifar)
    )
    ifar = swap(ifar, "tensor", 2)
    a3 = swap(gate(a3, dsum[1], ifar), "tensor", 1)
    (afar,) = combine((a2, a3), cost=10)
    dsum = scatter(dsum, highs[0], (a2,), 10)
    isum = scatter((i0, i1, ifar), low, (a2,), 10)
    a0, a1, grad_tokens = attend_back(
        (grad_attn, grad_tokens), tokens, saved_n, (own, p1), (fb0, fb1, sums2, sums1), (dsum[0], isum[0], afar)
    )
    afar = swap(afar, "tensor", 2)
    a1 = swap(gate(a1, afar, *dsum[1:], *isum[1:]), "tensor", 1)
    (dsum,) = combine(dsum, after=(a0,))
    isum = scatter(isum, highs[0], (a0,))
    asum = scatter((a0, a1, afar), low)
    asum = scatter(asum, highs[0])
    (isum,) = combine(isum)
    (asum,) = combine(asum)
    dsum, isum, asum = [sum_whole(item, highs[1:]) for item in (dsum, isum, asum)]
    dsum, isum, asum = [ordered(gather(item, highs[0]), highs[0])[0] for item in (dsum, isum, asum)]
    (grad_wd,) = ordered(gather(dsum, low), low, (w_down.shape[0],))
    (grad_wi,) = ordered(gather(isum, low), low, (depth,))
    *grad_qkv, grad_wo, small = ordered(gather(asum, low), low, (width,) * 4 + (8,))
    grad_wq, grad_wk, grad_wv = [item.T for item in grad_qkv]
    return (
        block_out,
        grad_tokens,
        grad_wq,
        small[0, :width],
        grad_wk,
        grad_wv,
        small[0, width : 2 * width],
        grad_wo,
        small[2],
        small[3],
        small[4],
        grad_wi,
        small[1],
        grad_wd,
        small[7],
        small[5],
        small[6],
    )


def solution(mesh):
    group = P(("dp", "tensor"), None)
    column, row, part, full = P(None, "tensor"), P("tensor", None), P("tensor"), P()
    in_specs = (
        group, P("dp"), P("dp", None), column, part, column, column, part, row,
        full, full, full, column, part, row, full, full, full, group,
    )
    out_specs = (
        group, group, column, part, column, column, part, row,
        full, full, full, column, part, row, full, full, full,
    )
    return jax.shard_map(
        per_device, mesh=mesh, in_specs=in_specs, out_specs=out_specs, check_vma=False
    )
```

```python
import functools

import jax
import jax.numpy as jnp
from jax import lax
from jax.experimental import pallas as pl
from jax.experimental.pallas import tpu as pltpu
from jax.sharding import PartitionSpec as P

HEAD = 64
BLOCK = 512
LANES = 128
EPSILON = 1e-12
EXTRA = 64
TAIL = 128
MASKED = -(2.0**30)
ROOT_HALF = 0.7071067811865476
PHI_SCALE = 0.3989422804014327
COSTS = {"attend": 10, "join": 6, "widen": 8, "narrow": 13, "down_grad": 6, "ffn_back": 0, "attend_back": 24}
COST_UNIT = 10**11
F32 = jnp.float32
BF16 = jnp.bfloat16
VMEM = 56 << 20


def dot(left, right, left_dim, right_dim):
    return lax.dot_general(
        left, right, (((left_dim,), (right_dim,)), ((), ())), preferred_element_type=F32
    )


def mean_rows(values):
    return jnp.mean(values, axis=-1, keepdims=True)


def unit_rows(values):
    centred = values - mean_rows(values)
    scale = lax.rsqrt(mean_rows(centred * centred) + EPSILON)
    return centred * scale, scale


def norm_back(grad, unit, scale, gain):
    e = grad * gain
    return scale * (e - mean_rows(e) - unit * mean_rows(e * unit))


def column_sum(values):
    return jnp.sum(values, axis=0, keepdims=True)


def call(kernel, name, steps, ins, outs, scratch=(), wait=(), cost=10):
    count = len(ins)

    def body(*refs):
        kernel(*refs[:count], *refs[count + len(wait) :])

    return pl.pallas_call(
        body,
        grid=(steps,),
        in_specs=[
            pl.BlockSpec(memory_space=pltpu.SMEM) if block is None else pl.BlockSpec(block, index)
            for _, block, index in ins
        ]
        + [pl.BlockSpec(memory_space=pl.ANY)] * len(wait),
        out_specs=[pl.BlockSpec(block, index) for _, _, block, index in outs],
        out_shape=[jax.ShapeDtypeStruct(shape, dtype) for shape, dtype, _, _ in outs],
        scratch_shapes=list(scratch),
        compiler_params=pltpu.CompilerParams(
            dimension_semantics=("arbitrary",), vmem_limit_bytes=VMEM
        ),
        cost_estimate=pl.CostEstimate(flops=COSTS.get(name, cost) * COST_UNIT + 1, bytes_accessed=1, transcendentals=0),
        name=name,
    )(*[item[0] for item in ins], *wait)


def whole(array):
    rank = array.ndim
    return (array, array.shape, lambda i: (0,) * rank)


def tiled(array, rows):
    return (array, (rows, array.shape[1]), lambda i: (i, 0))


def tiled_out(shape, dtype, rows):
    return (shape, dtype, (rows, shape[1]), lambda i: (i, 0))


def whole_out(shape, dtype):
    rank = len(shape)
    return (shape, dtype, shape, lambda i: (0,) * rank)


def head_scores(q_ref, k_ref, qf, kf, pair, head):
    cols = slice(pair * LANES, (pair + 1) * LANES)
    lane = lax.broadcasted_iota(jnp.int32, (1, LANES), 1)
    queries = q_ref[:, cols]
    queries = jnp.where(lane // HEAD == head, queries, jnp.zeros_like(queries))
    keys = jnp.concatenate([k_ref[:, cols], kf], axis=1)
    return dot(keys, jnp.concatenate([queries, qf], axis=1), 1, 1)


def mask_features(first, bucket_ref, lengths_ref):
    kind = bucket_ref[0]
    row_len = jnp.where(kind == 0, BLOCK // 4, jnp.where(kind == 1, BLOCK // 2, BLOCK))
    shift = jnp.where(kind == 0, 7, jnp.where(kind == 1, 8, 9))
    slot = lax.broadcasted_iota(jnp.int32, (BLOCK, LANES), 0)
    lane = lax.broadcasted_iota(jnp.int32, (BLOCK, LANES), 1)
    same = lax.shift_right_logical(slot, shift) == lane
    base = lax.shift_right_logical(first, shift)
    length = jnp.zeros((BLOCK, LANES), jnp.int32)
    for at in range(4):
        length = jnp.where(lane == at, lengths_ref[0, base + at], length)
    seen = same & ((slot & (row_len - 1)) < length)
    queries = jnp.where(same, 1.0, 0.0).astype(BF16)
    keys = jnp.where((lane < 4) & jnp.logical_not(seen), MASKED, 0.0).astype(BF16)
    return queries, keys


def lanes_of(first, second):
    cut = 2 * HEAD
    return (first, 0, cut), (second, 0, cut), (first, cut, HEAD), (second, cut, HEAD)


def stack_rows(out, start, first, second, offset):
    for ref, at, size in lanes_of(first, second):
        out[start : start + size] = ref[offset + at : offset + at + size]
        start += size


def attend_body(tok_ref, near_ref, far_ref, qf, kf, q_ref, k_ref, v_ref, c_ref, lse_ref, wq_ref, wk_ref, wv_ref):
    span = q_ref.shape[1]
    width = span // 2

    @pl.when(pl.program_id(0) == 0)
    def _():
        for at, w_ref in enumerate((wq_ref, wk_ref, wv_ref)):
            stack_rows(w_ref, 0, near_ref, far_ref, at * width)

    tokens = tok_ref[...]
    bias_row = 4 * width
    near, far = near_ref[bias_row : bias_row + 1].astype(F32), far_ref[bias_row : bias_row + 1].astype(F32)
    bq, bv = [
        jnp.concatenate(
            [row[:, start + at : start + at + size] for row, at, size in lanes_of(near, far)], axis=1
        )
        for start in (0, width)
    ]
    q = (dot(tokens, wq_ref[...], 1, 1) + bq).astype(BF16)
    q_ref[...] = q * jnp.asarray(HEAD**-0.5, BF16)
    k_ref[...] = dot(tokens, wk_ref[...], 1, 1).astype(BF16)
    v_ref[...] = (dot(tokens, wv_ref[...], 1, 1) + bv).astype(BF16)
    items = [(pair, head) for pair in range(span // LANES) for head in range(2)]
    ahead = head_scores(q_ref, k_ref, qf, kf, *items[0])
    done = []
    for at, (pair, head) in enumerate(items):
        scores = ahead
        if at + 1 < len(items):
            ahead = head_scores(q_ref, k_ref, qf, kf, *items[at + 1])
        cols = slice(pair * LANES, (pair + 1) * LANES)
        if head == 0:
            vals = v_ref[:, cols].T
        largest = jnp.max(scores, axis=0, keepdims=True)
        raised = jnp.exp(scores - largest)
        total = jnp.sum(raised, axis=0, keepdims=True)
        lse_ref[0, at : at + 1, :] = largest + jnp.log(total)
        mixed = dot(vals[head * HEAD : (head + 1) * HEAD], raised.astype(BF16), 1, 0)
        done.append(mixed * (1.0 / total))
        if head == 1:
            c_ref[:, cols] = jnp.concatenate(done, axis=0).T.astype(BF16)
            done = []


def attend_first(bucket_ref, lengths_ref, place_ref, tok_ref, near_ref, far_ref, *outs):
    qf_ref, kf_ref = outs[8:]
    first = (place_ref[0] * pl.num_programs(0) + pl.program_id(0)) * BLOCK
    qf_ref[...], kf_ref[...] = mask_features(first, bucket_ref, lengths_ref)
    attend_body(tok_ref, near_ref, far_ref, qf_ref[...], kf_ref[...], *outs[:8])


def attend_second(qf_ref, kf_ref, tok_ref, near_ref, far_ref, *outs):
    attend_body(tok_ref, near_ref, far_ref, qf_ref[...], kf_ref[...], *outs)


def attend(lead, tokens, near, far, wait=()):
    rows, depth = tokens.shape
    span = (near.shape[0] - EXTRA) // 2
    heads = span // HEAD
    blocks = rows // BLOCK
    first = len(lead) == 3
    if first:
        ins = [(item, None, None) for item in lead]
    else:
        ins = [tiled(item, BLOCK) for item in lead]
    outs = [tiled_out((rows, span), BF16, BLOCK)] * 4
    outs += [((blocks, heads, BLOCK), F32, (1, heads, BLOCK), lambda i: (i, 0, 0))]
    outs += [whole_out((span, depth), BF16)] * 3
    if first:
        outs += [tiled_out((rows, LANES), BF16, BLOCK)] * 2
    return call(
        attend_first if first else attend_second,
        "attend",
        blocks,
        ins + [tiled(tokens, BLOCK), whole(near), whole(far)],
        outs,
        wait=wait,
    )


def out_rows(packed):
    rows, columns = packed.shape
    width = (rows - EXTRA) // 4
    return (packed, (width, columns), lambda i: (3, 0))


def join_kernel(
    tok_ref, cn_ref, cf_ref, w0_ref, w1_ref, w2_ref, w3_ref, b_ref, g_ref, s_ref, res_ref, low_ref, w_s,
):
    span = cn_ref.shape[1]

    @pl.when(pl.program_id(0) == 0)
    def _():
        stack_rows(w_s, 0, w0_ref, w1_ref, 0)
        stack_rows(w_s, span, w2_ref, w3_ref, 0)

    out = dot(cn_ref[...], w_s[:span], 1, 0) + dot(cf_ref[...], w_s[span:], 1, 0)
    residual = tok_ref[...].astype(F32) + (out + b_ref[...])
    res_ref[...] = residual
    unit, _ = unit_rows(residual)
    low_ref[...] = (unit * g_ref[...] + s_ref[...]).astype(BF16)


def join(tokens, ctx_near, ctx_far, pieces, b_out, gain, shift, wait=()):
    rows, depth = tokens.shape
    tile = 256
    return call(
        join_kernel,
        "join",
        rows // tile,
        [tiled(tokens, tile), tiled(ctx_near, tile), tiled(ctx_far, tile)]
        + [out_rows(piece) for piece in pieces]
        + [whole(b_out), whole(gain), whole(shift)],
        [tiled_out((rows, depth), F32, tile), tiled_out((rows, depth), BF16, tile)],
        [pltpu.VMEM((depth, depth), BF16)],
        wait=wait,
    )


def widen_kernel(n_ref, wa_ref, wb_ref, ba_ref, bb_ref, act_ref, fac_ref):
    normed = n_ref[...]
    wide = wa_ref.shape[1]
    for at, (ref, b_ref) in enumerate(((wa_ref, ba_ref), (wb_ref, bb_ref))):
        cols = slice(at * wide, (at + 1) * wide)
        pre = dot(normed, ref[...], 1, 0) + b_ref[1:2, :wide].astype(F32)
        below = 0.5 + 0.5 * lax.erf(pre * ROOT_HALF)
        act_ref[:, cols] = (pre * below).astype(BF16)
        density = jnp.exp(-0.5 * pre * pre) * PHI_SCALE
        fac_ref[:, cols] = (below + pre * density).astype(BF16)


def bias_rows(packed):
    rows, columns = packed.shape
    return (packed, (EXTRA, columns), lambda i: (rows // EXTRA - 1, 0))


def widen(normed, wa, wb, bias_a, bias_b, wait=()):
    rows, depth = normed.shape
    tile = 256
    units = 2 * wa.shape[1]
    return call(
        widen_kernel,
        "widen",
        rows // tile,
        [tiled(normed, tile), whole(wa), whole(wb), bias_rows(bias_a), bias_rows(bias_b)],
        [tiled_out((rows, units), BF16, tile)] * 2,
        wait=wait,
    )


def narrow_kernel(
    an_ref, af_ref, w0_ref, w1_ref, w2_ref, w3_ref, res_ref, g1_ref, s1_ref, bd_ref, g2_ref, s2_ref, cot_ref,
    out_ref, gs_ref, gf_ref, sums_ref,
):
    unit1, _ = unit_rows(res_ref[...])
    wide = w0_ref.shape[0]
    out = dot(an_ref[:, :wide], w0_ref[...], 1, 0) + dot(an_ref[:, wide:], w1_ref[...], 1, 0)
    out = out + dot(af_ref[:, :wide], w2_ref[...], 1, 0) + dot(af_ref[:, wide:], w3_ref[...], 1, 0)
    summed = (unit1 * g1_ref[...] + s1_ref[...]) + (out + bd_ref[...])
    unit, scale = unit_rows(summed)
    out_ref[...] = (unit * g2_ref[...] + s2_ref[...]).astype(BF16)
    cot = cot_ref[...]
    grad = norm_back(cot, unit, scale, g2_ref[...])
    gs_ref[...] = grad
    low = grad.astype(BF16)
    gf_ref[...] = low

    @pl.when(pl.program_id(0) == 0)
    def _():
        sums_ref[...] = jnp.zeros_like(sums_ref)

    sums_ref[0:1] += column_sum(cot * unit)
    sums_ref[1:2] += column_sum(cot)
    sums_ref[2:3] += column_sum(low.astype(F32))


def narrow(act_near, act_far, w_downs, residual, gain1, shift1, b_down, gain2, shift2, cotangent, wait=()):
    rows, depth = residual.shape
    tile = 256
    return call(
        narrow_kernel,
        "narrow",
        rows // tile,
        [tiled(act_near, tile), tiled(act_far, tile)]
        + [whole(w) for w in w_downs]
        + [tiled(residual, tile)]
        + [whole(v) for v in (gain1, shift1, b_down, gain2, shift2)]
        + [tiled(cotangent, tile)],
        [
            tiled_out((rows, depth), BF16, tile),
            tiled_out((rows, depth), F32, tile),
            tiled_out((rows, depth), BF16, tile),
            whole_out((8, depth), F32),
        ],
        wait=wait,
    )


def down_grad_kernel(gf_ref, acta_ref, actb_ref, da_ref, db_ref):
    grad = gf_ref[...]
    da_ref[...] = dot(acta_ref[...], grad, 0, 0).astype(BF16)
    db_ref[...] = dot(actb_ref[...], grad, 0, 0).astype(BF16)


def half_tile(array, which, tile):
    steps = array.shape[1] // 2 // tile
    return (array, (array.shape[0], tile), lambda i: (0, which * steps + i))


def down_grad(grad_ffn, acts, wait=()):
    rows, depth = grad_ffn.shape
    units = acts[0][0].shape[1] // 2
    tile = 256
    return call(
        down_grad_kernel,
        "down_grad",
        units // tile,
        [whole(grad_ffn)] + [half_tile(*item, tile) for item in acts],
        [tiled_out((units, depth), BF16, tile)] * 2,
        wait=wait,
    )


def ffn_back_kernel(gf_ref, n_ref, gn_in_ref, *refs):
    count = (len(refs) - 5) // 2
    piece_a, piece_b, (ga_ref, gb_ref, gba_ref, gbb_ref, gn_ref) = refs[:count], refs[count:-5], refs[-5:]

    @pl.when(pl.program_id(0) == 0)
    def _():
        gn_ref[...] = gn_in_ref[...]

    grad = gf_ref[...]
    for (fac_ref, wd_ref, wi_ref, *got), g_ref, gbias_ref in ((piece_a, ga_ref, gba_ref), (piece_b, gb_ref, gbb_ref)):
        grad_pre = (dot(grad, wd_ref[...], 1, 1) * fac_ref[...].astype(F32)).astype(BF16)
        gbias_ref[...] = column_sum(grad_pre.astype(F32))
        out = dot(n_ref[...], grad_pre, 0, 0)
        if got:
            out = out + got[0][...].astype(F32)
        g_ref[...] = out.astype(BF16)
        gn_ref[...] += dot(grad_pre, wi_ref[...], 1, 1)


def ffn_back(grad_ffn, normed, grad_normed, pieces, wait=()):
    rows, depth = grad_ffn.shape
    units = pieces[0][1].shape[0]
    tile = units
    steps = units // tile
    column = lambda i: (0, i)
    ins = [whole(grad_ffn), whole(normed), whole(grad_normed)]
    for fac, wd, wi, *got in pieces:
        ins += [half_tile(*fac, tile), tiled(wd, tile), (wi, (depth, tile), column)]
        ins += [(item, (depth, tile), column) for item in got]
    return call(
        ffn_back_kernel,
        "ffn_back",
        steps,
        ins,
        [((depth, units), BF16, (depth, tile), column)] * 2
        + [((1, units), F32, (1, tile), column)] * 2
        + [whole_out((rows, depth), F32)],
        wait=wait,
    )


def attend_back_core(q_ref, k_ref, v_ref, lse_ref, qf, kf, dqkv_s, gctx_s):
    span = q_ref.shape[1]
    items = [(pair, head) for pair in range(span // LANES) for head in range(2)]
    lane = lax.broadcasted_iota(jnp.int32, (1, LANES), 1)

    def front(pair, head):
        cols = slice(pair * LANES, (pair + 1) * LANES)
        scores = head_scores(q_ref, k_ref, qf, kf, pair, head)
        out = gctx_s[:, cols]
        out = jnp.where(lane // HEAD == head, out, jnp.zeros_like(out))
        return scores, dot(v_ref[:, cols], out, 1, 1)

    ahead = front(*items[0])
    for at, (pair, head) in enumerate(items):
        scores, grad_probs = ahead
        if at + 1 < len(items):
            ahead = front(*items[at + 1])
        cols = slice(pair * LANES, (pair + 1) * LANES)
        mine = lane // HEAD == head
        queries, out = q_ref[:, cols], gctx_s[:, cols]
        queries = jnp.where(mine, queries, jnp.zeros_like(queries))
        out = jnp.where(mine, out, jnp.zeros_like(out))
        if head == 0:
            keys = (k_ref[:, cols] * jnp.asarray(HEAD**-0.5, BF16)).T
            dqs, dk, dv = [], 0.0, 0.0
        probs = jnp.exp(scores - lse_ref[0, at : at + 1, :])
        centre = jnp.sum(probs * grad_probs, axis=0, keepdims=True)
        grad_scores = (probs * (grad_probs - centre)).astype(BF16)
        dqs.append(dot(keys[head * HEAD : (head + 1) * HEAD], grad_scores, 1, 0))
        dk = dk + dot(grad_scores, queries, 1, 0)
        dv = dv + dot(probs.astype(BF16), out, 1, 0)
        if head == 1:
            start = pair * LANES
            dqkv_s[:, start : start + LANES] = jnp.concatenate(dqs, axis=0).T.astype(BF16)
            dqkv_s[:, span + start : span + start + LANES] = dk.astype(BF16)
            dqkv_s[:, 2 * span + start : 2 * span + start + LANES] = dv.astype(BF16)


def attend_back_body(
    gattn, tok_ref, c_ref, q_ref, k_ref, v_ref, lse_ref, qf_ref, kf_ref, wq_ref, wk_ref, wv_ref, wa_ref, wb_ref,
    fa_ref, fb_ref, sums2_ref, sums1_ref, ga_ref, gb_ref, w_s, wo_s, gctx_s, dqkv_s, gw_s, bias_s,
):
    step = pl.program_id(0)
    span = q_ref.shape[1]
    width = span // 2
    cut = 2 * HEAD

    @pl.when(step == 0)
    def _():
        for at, ref in enumerate((wq_ref, wk_ref, wv_ref)):
            w_s[at * span : (at + 1) * span] = ref[...]
        stack_rows(wo_s, 0, wa_ref, wb_ref, 0)
        gw_s[...] = jnp.zeros_like(gw_s)
        bias_s[...] = jnp.zeros_like(bias_s)

    gctx_s[...] = dot(gattn, wo_s[...], 1, 1).astype(BF16)
    gw_s[3 * span :] += dot(c_ref[...], gattn, 0, 0)
    attend_back_core(q_ref, k_ref, v_ref, lse_ref, qf_ref[...], kf_ref[...], dqkv_s, gctx_s)
    dqkv = dqkv_s[...]
    gw_s[: 3 * span] += dot(dqkv, tok_ref[...], 0, 0)
    bias_s[0:1] += column_sum(dqkv[:, :span].astype(F32))
    bias_s[1:2] += column_sum(dqkv[:, 2 * span :].astype(F32))

    @pl.when(step == pl.num_programs(0) - 1)
    def _():
        for which, (ref, f_ref) in enumerate(((ga_ref, fa_ref), (gb_ref, fb_ref))):
            two, last = which * cut, 2 * cut + which * HEAD
            for at in range(4):
                start, own = at * span, at * width
                ref[own : own + cut] = gw_s[start + two : start + two + cut].astype(BF16)
                ref[own + cut : own + width] = gw_s[start + last : start + last + HEAD].astype(BF16)
            bias = bias_s[...]
            row = [bias[at : at + 1, lo : lo + size] for at in range(2) for lo, size in ((two, cut), (last, HEAD))]
            row = jnp.concatenate(row + [jnp.zeros((1, ref.shape[1] - span), F32)], axis=1)
            extra = [row, f_ref[...], sums1_ref[0:3], sums2_ref[0:3]]
            extra.append(jnp.zeros((ref.shape[0] - 4 * width - 8, ref.shape[1]), F32))
            ref[4 * width :] = jnp.concatenate(extra, axis=0).astype(BF16)

    return dot(dqkv, w_s[...], 1, 0)


def attend_back_first(gn_ref, res_ref, g1_ref, *rest):
    ins, (ga_ref, gb_ref, gt_ref, gattn_ref, sums_ref), scratch = rest[:16], rest[16:21], rest[21:]
    unit, scale = unit_rows(res_ref[...])
    grad = gn_ref[...]
    resid = norm_back(grad, unit, scale, g1_ref[...])
    low = resid.astype(BF16)
    gattn_ref[...] = low

    @pl.when(pl.program_id(0) == 0)
    def _():
        sums_ref[...] = jnp.zeros_like(sums_ref)

    sums_ref[0:1] += column_sum(low.astype(F32))
    sums_ref[1:2] += column_sum(grad * unit)
    sums_ref[2:3] += column_sum(grad)
    gt_ref[...] = resid
    gt_ref[...] += attend_back_body(low, *ins, sums_ref, ga_ref, gb_ref, *scratch)


def attend_back_next(gattn_ref, gtin_ref, *rest):
    ins, (ga_ref, gb_ref, gt_ref), scratch = rest[:17], rest[17:20], rest[20:]
    gt_ref[...] = gtin_ref[...] + attend_back_body(gattn_ref[...], *ins, ga_ref, gb_ref, *scratch)


def attend_back(lead, tokens, saved, pieces, sums, wait=()):
    ctx, q, k, v, lse, qf, kf, wq, wk, wv = saved
    rows, depth = tokens.shape
    heads = lse.shape[1]
    blocks = rows // BLOCK
    first = len(lead) == 3
    span = q.shape[1]
    ins = [tiled(item, BLOCK) if item.shape[0] == rows else whole(item) for item in lead]
    ins += [tiled(item, BLOCK) for item in (tokens, ctx, q, k, v)]
    ins += [(lse, (1, heads, BLOCK), lambda i: (i, 0, 0)), tiled(qf, BLOCK), tiled(kf, BLOCK)]
    ins += [whole(item) for item in (wq, wk, wv)] + [out_rows(item) for item in pieces]
    ins += [whole(item) for item in sums]
    bundle = (2 * span + TAIL, depth)
    outs = [whole_out(bundle, BF16)] * 2 + [tiled_out((rows, depth), F32, BLOCK)]
    if first:
        outs += [tiled_out((rows, depth), BF16, BLOCK), whole_out((8, depth), F32)]
    return call(
        attend_back_first if first else attend_back_next,
        "attend_back",
        blocks,
        ins,
        outs,
        [
            pltpu.VMEM((3 * span, depth), BF16),
            pltpu.VMEM((span, depth), BF16),
            pltpu.VMEM((BLOCK, span), BF16),
            pltpu.VMEM((BLOCK, 3 * span), BF16),
            pltpu.VMEM((4 * span, depth), F32),
            pltpu.VMEM((8, span), F32),
        ],
        wait=wait,
    )


def picked(kernel, name, index, steps, ins, outs, wait=(), cost=10):
    count = len(ins)

    def body(_, *refs):
        kernel(*refs[:count], *refs[count + len(wait) :])

    anywhere = pl.BlockSpec(memory_space=pl.ANY)
    return pl.pallas_call(
        body,
        grid_spec=pltpu.PrefetchScalarGridSpec(
            num_scalar_prefetch=1,
            grid=(steps,),
            in_specs=[pl.BlockSpec(block, at) for _, block, at in ins] + [anywhere] * len(wait),
            out_specs=[pl.BlockSpec(block, at) for _, _, block, at in outs],
        ),
        out_shape=[jax.ShapeDtypeStruct(shape, dtype) for shape, dtype, _, _ in outs],
        compiler_params=pltpu.CompilerParams(dimension_semantics=("arbitrary",), vmem_limit_bytes=VMEM),
        cost_estimate=pl.CostEstimate(flops=cost * COST_UNIT + 1, bytes_accessed=1, transcendentals=0),
        name=name,
    )(index.astype(jnp.int32)[None], *[item[0] for item in ins], *wait)


def tiles_in(rows):
    return 2 if rows % 32 == 0 else 1


def combine(terms, index=None, count=1, after=(), cost=10):
    if index is None:
        index = jnp.zeros((), jnp.int32)
    rows, columns = terms[0].shape
    size = rows // count
    steps = tiles_in(size)
    tile = size // steps

    def chunk(k):
        return lambda i, at: ((at[0] ^ k) * steps + i, 0)

    def kernel(*refs):
        for k in range(count):
            total = sum(ref[...].astype(F32) for ref in refs[k * len(terms) : (k + 1) * len(terms)])
            refs[count * len(terms) + k][...] = total.astype(BF16)

    return picked(
        kernel,
        "combine",
        index,
        steps,
        [(term, (tile, columns), chunk(k)) for k in range(count) for term in terms],
        [((size, columns), BF16, (tile, columns), lambda i, at: (i, 0))] * count,
        after,
        cost,
    )


def arrange(parts, index, sizes=None, split=1, after=(), cost=10):
    size, columns = parts[0].shape
    count = len(parts)
    if sizes is None:
        each = size // split

        def kernel(index_ref, *refs):
            for here in range(count):

                @pl.when(index_ref[0] == here)
                def _(here=here):
                    for k in range(count):
                        start = (here ^ k) * each
                        for out in range(split):
                            refs[count + out][start : start + each] = refs[k][out * each : (out + 1) * each]

        return call(
            kernel,
            "arrange",
            1,
            [(index.astype(jnp.int32)[None], None, None)] + [whole(part) for part in parts],
            [whole_out((count * each, columns), BF16)] * split,
            wait=after,
            cost=cost,
        )

    def kernel_out(index_ref, *refs):
        for here in range(count):

            @pl.when(index_ref[0] == here)
            def _(here=here):
                start = 0
                for out in refs[count:]:
                    end = start + out.shape[0]
                    for k in range(count):
                        low = (here ^ k) * size
                        lo, hi = max(start, low), min(end, low + size)
                        if lo < hi:
                            out[lo - start : hi - start] = refs[k][lo - low : hi - low].astype(F32)
                    start = end

    return call(
        kernel_out,
        "arrange_out",
        1,
        [(index.astype(jnp.int32)[None], None, None)] + [whole(part) for part in parts],
        [whole_out((rows, columns), F32) for rows in sizes],
    )


def swap(values, axis, bit):
    count = lax.axis_size(axis)
    return lax.ppermute(values, axis, [(at, at ^ bit) for at in range(count)])


def gate(values, *after):
    def kernel(*refs):
        pass

    anywhere = pl.BlockSpec(memory_space=pl.ANY)
    return pl.pallas_call(
        kernel,
        in_specs=[anywhere] * (1 + len(after)),
        out_specs=anywhere,
        out_shape=jax.ShapeDtypeStruct(values.shape, values.dtype),
        input_output_aliases={0: 0},
        name="gate",
    )(values, *after)


def dp_bits():
    bits, bit = [], 1
    while bit < lax.axis_size("dp"):
        bits.append(bit)
        bit *= 2
    return bits


def groups(bits):
    return [bits[:1]] + [bits[at : at + 2] for at in range(1, len(bits), 2)]


def spot(bits):
    me = lax.axis_index("dp")
    at = sum(((me // bit) % 2) << i for i, bit in enumerate(bits))
    return at, [sum(bit for i, bit in enumerate(bits) if k >> i & 1) for k in range(1 << len(bits))]


def scatter(terms, bits, after=(), cost=10):
    at, far = spot(bits)
    kept, *sent = combine(terms, at, len(far), after, cost)
    return [kept] + [swap(item, "dp", distance) for item, distance in zip(sent, far[1:])]


def sum_whole(values, steps):
    for bit in [bit for step in steps for bit in step]:
        (values,) = combine((values, swap(values, "dp", bit)))
    return values


def gather(values, bits):
    _, far = spot(bits)
    return [values] + [swap(values, "dp", distance) for distance in far[1:]]


def ordered(parts, bits, sizes=None):
    return arrange(parts, spot(bits)[0], sizes)


def parity():
    me = lax.axis_index("dp")
    return (me ^ (me >> 1)) % 2


def my_half(arrays):
    columns = arrays[0].shape[1]
    quarters = [array.shape[0] // 4 for array in arrays]

    def kernel(*refs):
        ins, outs = refs[: 2 * len(arrays)], refs[2 * len(arrays) :]
        for part in range(2):
            start = 0
            for at, rows in enumerate(quarters):
                outs[part][start : start + rows] = ins[2 * at + part][...]
                start += rows

    return picked(
        kernel,
        "my_half",
        parity(),
        1,
        [
            (array, (rows, columns), lambda i, at, part=part: (at[0] * 2 + part, 0))
            for array, rows in zip(arrays, quarters)
            for part in range(2)
        ],
        [((sum(quarters), columns), BF16, (sum(quarters), columns), lambda i, at: (0, 0))] * 2,
    )


def pack(arrays):
    rows = sum(array.shape[0] for array in arrays)
    columns = arrays[0].shape[1]
    quarter = rows // 4

    def kernel(index_ref, *refs):
        ins, (out, *parts) = refs[: len(arrays)], refs[len(arrays) :]
        start = 0
        for ref in ins:
            out[start : start + ref.shape[0]] = ref[...]
            start += ref.shape[0]
        for side in range(2):

            @pl.when(index_ref[0] == side)
            def _(side=side):
                for at, part in enumerate(parts):
                    low = (2 * side + at) * quarter
                    part[...] = out[low : low + quarter]

    return call(
        kernel,
        "pack",
        1,
        [(parity().astype(jnp.int32)[None], None, None)] + [whole(array) for array in arrays],
        [whole_out((rows, columns), BF16)] + [whole_out((quarter, columns), BF16)] * 2,
    )


def other_half(first, second):
    return swap(first, "dp", 1), swap(second, "dp", 2)


def per_device(
    tokens, bucket, lengths, w_query, b_query, w_key, w_value, b_value, w_out, b_out, gain1, shift1,
    w_in, b_in, w_down, b_down, gain2, shift2, cotangent,
):
    rows, depth = tokens.shape
    width = w_query.shape[1]
    me = lax.axis_index("tensor")
    line = lambda v: v.astype(F32)[None]
    b_out, gain1, shift1, b_down, gain2, shift2 = map(line, (b_out, gain1, shift1, b_down, gain2, shift2))

    row = jnp.concatenate((b_query, b_value, jnp.zeros((depth - 2 * width,), BF16)))
    biases = jnp.pad(jnp.stack((row, b_in)), ((0, EXTRA - 2), (0, 0)))
    own, *parts = pack((w_query.T, w_key.T, w_value.T, w_out, biases))
    p1 = swap(own, "tensor", 1)
    pa, pb = [swap(item, "tensor", 2) for item in parts]
    wide = my_half((w_in, w_down))
    wa, wb = [swap(item, "tensor", 2) for item in wide]
    in1 = swap(w_in, "tensor", 1)
    down1 = swap(w_down, "tensor", 1)

    place_y = me.astype(jnp.int32)[None]
    (p2,) = arrange((pa, pb, *other_half(pa, pb)), 2 * parity(), cost=0)
    p3 = swap(p2, "tensor", 1)
    qn, kn, vn, cn, lsen, *wn, qf, kf = attend((bucket, lengths, place_y), tokens, own, p1, (*wide, p2, wa))
    qr, kr, vr, cr, lser, *wr = attend((qf, kf), tokens, p2, p3)
    wa, wb = gate(wa, cn), gate(wb, cn)
    others = other_half(wa, wb)
    in2, down2 = arrange((wa, wb, *others), 2 * parity(), split=2, after=(cr,))
    in3, down3 = swap(in2, "tensor", 1), swap(down2, "tensor", 1)
    residual, normed = join(tokens, cn, cr, (own, p1, p2, p3), b_out, gain1, shift1, (in2,))
    actn, facn = widen(normed, w_in, in1, own, p1)
    actr, facr = widen(normed, in2, in3, p2, p3)
    block_out, grad_summed, grad_ffn, sums2 = narrow(
        actn, actr, (w_down, down1, down2, down3), residual, gain1, shift1, b_down, gain2, shift2, cotangent
    )
    low, *highs = groups(dp_bits())
    d3, d2 = down_grad(grad_ffn, ((actr, 1), (actr, 0)))
    d1, d0 = down_grad(grad_ffn, ((actn, 1), (actn, 0)))
    (dfar,) = combine((d2, swap(d3, "tensor", 1)), after=(d0,), cost=10)
    i3, i2, fb3, fb2, grad_normed = ffn_back(
        grad_ffn, normed, grad_summed, (((facr, 1), down3, in3), ((facr, 0), down2, in2)), (dfar,)
    )
    i1, i0, fb1, fb0, grad_normed = ffn_back(
        grad_ffn, normed, grad_normed, (((facn, 1), down1, in1), ((facn, 0), w_down, w_in))
    )
    dfar = swap(dfar, "tensor", 2)
    i1 = swap(gate(i1, dfar), "tensor", 1)
    (ifar,) = combine((i2, swap(gate(i3, i0, dfar), "tensor", 1)), cost=10)
    dsum = scatter((d0, swap(d1, "tensor", 1), dfar), low, (i0,), 10)
    saved_r = (cr, qr, kr, vr, lser, qf, kf, *wr)
    saved_n = (cn, qn, kn, vn, lsen, qf, kf, *wn)
    a2, a3, grad_tokens, grad_attn, sums1 = attend_back(
        (grad_normed, residual, gain1), tokens, saved_r, (p2, p3), (fb2, fb3, sums2), (dsum[0], ifar)
    )
    ifar = swap(ifar, "tensor", 2)
    a3 = swap(gate(a3, dsum[1], ifar), "tensor", 1)
    (afar,) = combine((a2, a3), cost=10)
    dsum = scatter(dsum, highs[0], (a3,), 10)
    isum = scatter((i0, i1, ifar), low, (a3,), 10)
    a0, a1, grad_tokens = attend_back(
        (grad_attn, grad_tokens), tokens, saved_n, (own, p1), (fb0, fb1, sums2, sums1), (dsum[0], isum[0], afar)
    )
    afar = swap(afar, "tensor", 2)
    a1 = swap(gate(a1, afar, *dsum[1:], *isum[1:]), "tensor", 1)
    high, more = highs[0], highs[1:]
    asum = scatter((a0, a1, afar), low, cost=0)
    (dsum,) = combine(dsum, after=(asum[0],), cost=0)
    dparts = gather(sum_whole(dsum, more), high)
    isum = scatter(isum, high, (asum[0],), 0)
    asum = scatter(asum, high, (*dparts[1:], *isum[1:]), 0)
    dparts = gather(ordered(dparts, high)[0], low)
    (isum,) = combine(isum, cost=0)
    iparts = gather(sum_whole(isum, more), high)
    (asum,) = combine(asum, after=(dparts[1],), cost=0)
    aparts = gather(sum_whole(asum, more), high)
    iparts = gather(ordered(iparts, high)[0], low)
    (asum,) = ordered(aparts, high)
    (grad_wd,) = ordered(dparts, low, (w_down.shape[0],))
    (grad_wi,) = ordered(iparts, low, (depth,))
    *grad_qkv, grad_wo, small = ordered(gather(asum, low), low, (width,) * 4 + (8,))
    grad_wq, grad_wk, grad_wv = [item.T for item in grad_qkv]
    return (
        block_out,
        grad_tokens,
        grad_wq,
        small[0, :width],
        grad_wk,
        grad_wv,
        small[0, width : 2 * width],
        grad_wo,
        small[2],
        small[3],
        small[4],
        grad_wi,
        small[1],
        grad_wd,
        small[7],
        small[5],
        small[6],
    )


def solution(mesh):
    group = P(("dp", "tensor"), None)
    column, row, part, full = P(None, "tensor"), P("tensor", None), P("tensor"), P()
    in_specs = (
        group, P("dp"), P("dp", None), column, part, column, column, part, row,
        full, full, full, column, part, row, full, full, full, group,
    )
    out_specs = (
        group, group, column, part, column, column, part, row,
        full, full, full, column, part, row, full, full, full,
    )
    return jax.shard_map(
        per_device, mesh=mesh, in_specs=in_specs, out_specs=out_specs, check_vma=False
    )
```

```python
import functools

import jax
import jax.numpy as jnp
from jax import lax
from jax.experimental import pallas as pl
from jax.experimental.pallas import tpu as pltpu
from jax.sharding import PartitionSpec as P

HEAD = 64
BLOCK = 512
LANES = 128
EPSILON = 1e-12
EXTRA = 64
TAIL = 128
MASKED = -(2.0**30)
ROOT_HALF = 0.7071067811865476
PHI_SCALE = 0.3989422804014327
COSTS = {"attend": 10, "join": 6, "widen": 8, "narrow": 13, "down_grad": 6, "ffn_back": 0, "attend_back": 24}
COST_UNIT = 10**11
F32 = jnp.float32
BF16 = jnp.bfloat16
VMEM = 63 << 20


def dot(left, right, left_dim, right_dim):
    return lax.dot_general(
        left, right, (((left_dim,), (right_dim,)), ((), ())), preferred_element_type=F32
    )


def mean_rows(values):
    return jnp.mean(values, axis=-1, keepdims=True)


def unit_rows(values):
    centred = values - mean_rows(values)
    scale = lax.rsqrt(mean_rows(centred * centred) + EPSILON)
    return centred * scale, scale


def norm_back(grad, unit, scale, gain):
    e = grad * gain
    return scale * (e - mean_rows(e) - unit * mean_rows(e * unit))


def column_sum(values):
    return jnp.sum(values, axis=0, keepdims=True)


def call(kernel, name, steps, ins, outs, scratch=(), wait=(), cost=10):
    count = len(ins)

    def body(*refs):
        kernel(*refs[:count], *refs[count + len(wait) :])

    return pl.pallas_call(
        body,
        grid=(steps,),
        in_specs=[
            pl.BlockSpec(memory_space=pltpu.SMEM) if block is None else pl.BlockSpec(block, index)
            for _, block, index in ins
        ]
        + [pl.BlockSpec(memory_space=pl.ANY)] * len(wait),
        out_specs=[pl.BlockSpec(block, index) for _, _, block, index in outs],
        out_shape=[jax.ShapeDtypeStruct(shape, dtype) for shape, dtype, _, _ in outs],
        scratch_shapes=list(scratch),
        compiler_params=pltpu.CompilerParams(
            dimension_semantics=("arbitrary",), vmem_limit_bytes=VMEM
        ),
        cost_estimate=pl.CostEstimate(flops=COSTS.get(name, cost) * COST_UNIT + 1, bytes_accessed=1, transcendentals=0),
        name=name,
    )(*[item[0] for item in ins], *wait)


def whole(array):
    rank = array.ndim
    return (array, array.shape, lambda i: (0,) * rank)


def tiled(array, rows):
    return (array, (rows, array.shape[1]), lambda i: (i, 0))


def tiled_out(shape, dtype, rows):
    return (shape, dtype, (rows, shape[1]), lambda i: (i, 0))


def whole_out(shape, dtype):
    rank = len(shape)
    return (shape, dtype, shape, lambda i: (0,) * rank)


def head_scores(q_ref, k_ref, qf, kf, pair, head):
    cols = slice(pair * LANES, (pair + 1) * LANES)
    lane = lax.broadcasted_iota(jnp.int32, (1, LANES), 1)
    queries = q_ref[:, cols]
    queries = jnp.where(lane // HEAD == head, queries, jnp.zeros_like(queries))
    keys = jnp.concatenate([k_ref[:, cols], kf], axis=1)
    return dot(keys, jnp.concatenate([queries, qf], axis=1), 1, 1)


def mask_features(first, bucket_ref, lengths_ref):
    kind = bucket_ref[0]
    row_len = jnp.where(kind == 0, BLOCK // 4, jnp.where(kind == 1, BLOCK // 2, BLOCK))
    shift = jnp.where(kind == 0, 7, jnp.where(kind == 1, 8, 9))
    slot = lax.broadcasted_iota(jnp.int32, (BLOCK, LANES), 0)
    lane = lax.broadcasted_iota(jnp.int32, (BLOCK, LANES), 1)
    same = lax.shift_right_logical(slot, shift) == lane
    base = lax.shift_right_logical(first, shift)
    length = jnp.zeros((BLOCK, LANES), jnp.int32)
    for at in range(4):
        length = jnp.where(lane == at, lengths_ref[0, base + at], length)
    seen = same & ((slot & (row_len - 1)) < length)
    queries = jnp.where(same, 1.0, 0.0).astype(BF16)
    keys = jnp.where((lane < 4) & jnp.logical_not(seen), MASKED, 0.0).astype(BF16)
    return queries, keys


def lanes_of(first, second):
    cut = 2 * HEAD
    return (first, 0, cut), (second, 0, cut), (first, cut, HEAD), (second, cut, HEAD)


def stack_rows(out, start, first, second, offset):
    for ref, at, size in lanes_of(first, second):
        out[start : start + size] = ref[offset + at : offset + at + size]
        start += size


def attend_body(tok_ref, near_ref, far_ref, qf, kf, q_ref, k_ref, v_ref, c_ref, lse_ref, wq_ref, wk_ref, wv_ref):
    span = q_ref.shape[1]
    width = span // 2

    @pl.when(pl.program_id(0) == 0)
    def _():
        for at, w_ref in enumerate((wq_ref, wk_ref, wv_ref)):
            stack_rows(w_ref, 0, near_ref, far_ref, at * width)

    tokens = tok_ref[...]
    bias_row = 4 * width
    near, far = near_ref[bias_row : bias_row + 1].astype(F32), far_ref[bias_row : bias_row + 1].astype(F32)
    bq, bv = [
        jnp.concatenate(
            [row[:, start + at : start + at + size] for row, at, size in lanes_of(near, far)], axis=1
        )
        for start in (0, width)
    ]
    q = (dot(tokens, wq_ref[...], 1, 1) + bq).astype(BF16)
    q_ref[...] = q * jnp.asarray(HEAD**-0.5, BF16)
    k_ref[...] = dot(tokens, wk_ref[...], 1, 1).astype(BF16)
    v_ref[...] = (dot(tokens, wv_ref[...], 1, 1) + bv).astype(BF16)
    items = [(pair, head) for pair in range(span // LANES) for head in range(2)]
    ahead = head_scores(q_ref, k_ref, qf, kf, *items[0])
    done = []
    for at, (pair, head) in enumerate(items):
        scores = ahead
        if at + 1 < len(items):
            ahead = head_scores(q_ref, k_ref, qf, kf, *items[at + 1])
        cols = slice(pair * LANES, (pair + 1) * LANES)
        if head == 0:
            vals = v_ref[:, cols].T
        largest = jnp.max(scores, axis=0, keepdims=True)
        raised = jnp.exp(scores - largest)
        total = jnp.sum(raised, axis=0, keepdims=True)
        lse_ref[0, at : at + 1, :] = largest + jnp.log(total)
        mixed = dot(vals[head * HEAD : (head + 1) * HEAD], raised.astype(BF16), 1, 0)
        done.append(mixed * (1.0 / total))
        if head == 1:
            c_ref[:, cols] = jnp.concatenate(done, axis=0).T.astype(BF16)
            done = []


def attend_first(bucket_ref, lengths_ref, place_ref, tok_ref, near_ref, far_ref, *outs):
    qf_ref, kf_ref = outs[8:]
    first = (place_ref[0] * pl.num_programs(0) + pl.program_id(0)) * BLOCK
    qf_ref[...], kf_ref[...] = mask_features(first, bucket_ref, lengths_ref)
    attend_body(tok_ref, near_ref, far_ref, qf_ref[...], kf_ref[...], *outs[:8])


def attend_second(qf_ref, kf_ref, tok_ref, near_ref, far_ref, *outs):
    attend_body(tok_ref, near_ref, far_ref, qf_ref[...], kf_ref[...], *outs)


def attend(lead, tokens, near, far, wait=()):
    rows, depth = tokens.shape
    span = (near.shape[0] - EXTRA) // 2
    heads = span // HEAD
    blocks = rows // BLOCK
    first = len(lead) == 3
    if first:
        ins = [(item, None, None) for item in lead]
    else:
        ins = [tiled(item, BLOCK) for item in lead]
    outs = [tiled_out((rows, span), BF16, BLOCK)] * 4
    outs += [((blocks, heads, BLOCK), F32, (1, heads, BLOCK), lambda i: (i, 0, 0))]
    outs += [whole_out((span, depth), BF16)] * 3
    if first:
        outs += [tiled_out((rows, LANES), BF16, BLOCK)] * 2
    return call(
        attend_first if first else attend_second,
        "attend",
        blocks,
        ins + [tiled(tokens, BLOCK), whole(near), whole(far)],
        outs,
        wait=wait,
    )


def out_rows(packed):
    rows, columns = packed.shape
    width = (rows - EXTRA) // 4
    return (packed, (width, columns), lambda i: (3, 0))


def join_kernel(
    tok_ref, cn_ref, cf_ref, w0_ref, w1_ref, w2_ref, w3_ref, b_ref, g_ref, s_ref, res_ref, low_ref, w_s,
):
    span = cn_ref.shape[1]

    @pl.when(pl.program_id(0) == 0)
    def _():
        stack_rows(w_s, 0, w0_ref, w1_ref, 0)
        stack_rows(w_s, span, w2_ref, w3_ref, 0)

    out = dot(cn_ref[...], w_s[:span], 1, 0) + dot(cf_ref[...], w_s[span:], 1, 0)
    residual = tok_ref[...].astype(F32) + (out + b_ref[...])
    res_ref[...] = residual
    unit, _ = unit_rows(residual)
    low_ref[...] = (unit * g_ref[...] + s_ref[...]).astype(BF16)


def join(tokens, ctx_near, ctx_far, pieces, b_out, gain, shift, wait=()):
    rows, depth = tokens.shape
    tile = 256
    return call(
        join_kernel,
        "join",
        rows // tile,
        [tiled(tokens, tile), tiled(ctx_near, tile), tiled(ctx_far, tile)]
        + [out_rows(piece) for piece in pieces]
        + [whole(b_out), whole(gain), whole(shift)],
        [tiled_out((rows, depth), F32, tile), tiled_out((rows, depth), BF16, tile)],
        [pltpu.VMEM((depth, depth), BF16)],
        wait=wait,
    )


def widen_kernel(n_ref, wa_ref, wb_ref, ba_ref, bb_ref, act_ref, fac_ref):
    normed = n_ref[...]
    wide = wa_ref.shape[1]
    for at, (ref, b_ref) in enumerate(((wa_ref, ba_ref), (wb_ref, bb_ref))):
        cols = slice(at * wide, (at + 1) * wide)
        pre = dot(normed, ref[...], 1, 0) + b_ref[1:2, :wide].astype(F32)
        below = 0.5 + 0.5 * lax.erf(pre * ROOT_HALF)
        act_ref[:, cols] = (pre * below).astype(BF16)
        density = jnp.exp(-0.5 * pre * pre) * PHI_SCALE
        fac_ref[:, cols] = (below + pre * density).astype(BF16)


def bias_rows(packed):
    rows, columns = packed.shape
    return (packed, (EXTRA, columns), lambda i: (rows // EXTRA - 1, 0))


def widen(normed, wa, wb, bias_a, bias_b, wait=()):
    rows, depth = normed.shape
    tile = 256
    units = 2 * wa.shape[1]
    return call(
        widen_kernel,
        "widen",
        rows // tile,
        [tiled(normed, tile), whole(wa), whole(wb), bias_rows(bias_a), bias_rows(bias_b)],
        [tiled_out((rows, units), BF16, tile)] * 2,
        wait=wait,
    )


def narrow_kernel(
    an_ref, af_ref, w0_ref, w1_ref, w2_ref, w3_ref, res_ref, g1_ref, s1_ref, bd_ref, g2_ref, s2_ref, cot_ref,
    out_ref, gs_ref, gf_ref, sums_ref,
):
    unit1, _ = unit_rows(res_ref[...])
    wide = w0_ref.shape[0]
    out = dot(an_ref[:, :wide], w0_ref[...], 1, 0) + dot(an_ref[:, wide:], w1_ref[...], 1, 0)
    out = out + dot(af_ref[:, :wide], w2_ref[...], 1, 0) + dot(af_ref[:, wide:], w3_ref[...], 1, 0)
    summed = (unit1 * g1_ref[...] + s1_ref[...]) + (out + bd_ref[...])
    unit, scale = unit_rows(summed)
    out_ref[...] = (unit * g2_ref[...] + s2_ref[...]).astype(BF16)
    cot = cot_ref[...]
    grad = norm_back(cot, unit, scale, g2_ref[...])
    gs_ref[...] = grad
    low = grad.astype(BF16)
    gf_ref[...] = low

    @pl.when(pl.program_id(0) == 0)
    def _():
        sums_ref[...] = jnp.zeros_like(sums_ref)

    sums_ref[0:1] += column_sum(cot * unit)
    sums_ref[1:2] += column_sum(cot)
    sums_ref[2:3] += column_sum(low.astype(F32))


def narrow(act_near, act_far, w_downs, residual, gain1, shift1, b_down, gain2, shift2, cotangent, wait=()):
    rows, depth = residual.shape
    tile = 256
    return call(
        narrow_kernel,
        "narrow",
        rows // tile,
        [tiled(act_near, tile), tiled(act_far, tile)]
        + [whole(w) for w in w_downs]
        + [tiled(residual, tile)]
        + [whole(v) for v in (gain1, shift1, b_down, gain2, shift2)]
        + [tiled(cotangent, tile)],
        [
            tiled_out((rows, depth), BF16, tile),
            tiled_out((rows, depth), F32, tile),
            tiled_out((rows, depth), BF16, tile),
            whole_out((8, depth), F32),
        ],
        wait=wait,
    )


def down_grad_kernel(gf_ref, acta_ref, actb_ref, da_ref, db_ref):
    grad = gf_ref[...]
    da_ref[...] = dot(acta_ref[...], grad, 0, 0).astype(BF16)
    db_ref[...] = dot(actb_ref[...], grad, 0, 0).astype(BF16)


def half_tile(array, which, tile):
    steps = array.shape[1] // 2 // tile
    return (array, (array.shape[0], tile), lambda i: (0, which * steps + i))


def down_grad(grad_ffn, acts, wait=()):
    rows, depth = grad_ffn.shape
    units = acts[0][0].shape[1] // 2
    tile = 256
    return call(
        down_grad_kernel,
        "down_grad",
        units // tile,
        [whole(grad_ffn)] + [half_tile(*item, tile) for item in acts],
        [tiled_out((units, depth), BF16, tile)] * 2,
        wait=wait,
    )


def ffn_back_kernel(gf_ref, n_ref, gn_in_ref, *refs):
    count = (len(refs) - 5) // 2
    piece_a, piece_b, (ga_ref, gb_ref, gba_ref, gbb_ref, gn_ref) = refs[:count], refs[count:-5], refs[-5:]

    @pl.when(pl.program_id(0) == 0)
    def _():
        gn_ref[...] = gn_in_ref[...]

    grad = gf_ref[...]
    for (fac_ref, wd_ref, wi_ref, *got), g_ref, gbias_ref in ((piece_a, ga_ref, gba_ref), (piece_b, gb_ref, gbb_ref)):
        grad_pre = (dot(grad, wd_ref[...], 1, 1) * fac_ref[...].astype(F32)).astype(BF16)
        gbias_ref[...] = column_sum(grad_pre.astype(F32))
        out = dot(n_ref[...], grad_pre, 0, 0)
        if got:
            out = out + got[0][...].astype(F32)
        g_ref[...] = out.astype(BF16)
        gn_ref[...] += dot(grad_pre, wi_ref[...], 1, 1)


def ffn_back(grad_ffn, normed, grad_normed, pieces, wait=()):
    rows, depth = grad_ffn.shape
    units = pieces[0][1].shape[0]
    tile = units
    steps = units // tile
    column = lambda i: (0, i)
    ins = [whole(grad_ffn), whole(normed), whole(grad_normed)]
    for fac, wd, wi, *got in pieces:
        ins += [half_tile(*fac, tile), tiled(wd, tile), (wi, (depth, tile), column)]
        ins += [(item, (depth, tile), column) for item in got]
    return call(
        ffn_back_kernel,
        "ffn_back",
        steps,
        ins,
        [((depth, units), BF16, (depth, tile), column)] * 2
        + [((1, units), F32, (1, tile), column)] * 2
        + [whole_out((rows, depth), F32)],
        wait=wait,
    )


def attend_back_core(q_ref, k_ref, v_ref, lse_ref, qf, kf, dqkv_s, gctx_s):
    span = q_ref.shape[1]
    items = [(pair, head) for pair in range(span // LANES) for head in range(2)]
    lane = lax.broadcasted_iota(jnp.int32, (1, LANES), 1)

    def front(pair, head):
        cols = slice(pair * LANES, (pair + 1) * LANES)
        scores = head_scores(q_ref, k_ref, qf, kf, pair, head)
        out = gctx_s[:, cols]
        out = jnp.where(lane // HEAD == head, out, jnp.zeros_like(out))
        return scores, dot(v_ref[:, cols], out, 1, 1)

    ahead = front(*items[0])
    for at, (pair, head) in enumerate(items):
        scores, grad_probs = ahead
        if at + 1 < len(items):
            ahead = front(*items[at + 1])
        cols = slice(pair * LANES, (pair + 1) * LANES)
        mine = lane // HEAD == head
        queries, out = q_ref[:, cols], gctx_s[:, cols]
        queries = jnp.where(mine, queries, jnp.zeros_like(queries))
        out = jnp.where(mine, out, jnp.zeros_like(out))
        if head == 0:
            keys = (k_ref[:, cols] * jnp.asarray(HEAD**-0.5, BF16)).T
            dqs, dk, dv = [], 0.0, 0.0
        probs = jnp.exp(scores - lse_ref[0, at : at + 1, :])
        centre = jnp.sum(probs * grad_probs, axis=0, keepdims=True)
        grad_scores = (probs * (grad_probs - centre)).astype(BF16)
        dqs.append(dot(keys[head * HEAD : (head + 1) * HEAD], grad_scores, 1, 0))
        dk = dk + dot(grad_scores, queries, 1, 0)
        dv = dv + dot(probs.astype(BF16), out, 1, 0)
        if head == 1:
            start = pair * LANES
            dqkv_s[:, start : start + LANES] = jnp.concatenate(dqs, axis=0).T.astype(BF16)
            dqkv_s[:, span + start : span + start + LANES] = dk.astype(BF16)
            dqkv_s[:, 2 * span + start : 2 * span + start + LANES] = dv.astype(BF16)


def attend_back_body(
    gattn, tok_ref, c_ref, q_ref, k_ref, v_ref, lse_ref, qf_ref, kf_ref, wq_ref, wk_ref, wv_ref, wa_ref, wb_ref,
    fa_ref, fb_ref, sums2_ref, sums1_ref, ga_ref, gb_ref, w_s, wo_s, gctx_s, dqkv_s, gw_s, bias_s,
):
    step = pl.program_id(0)
    span = q_ref.shape[1]
    width = span // 2
    cut = 2 * HEAD

    @pl.when(step == 0)
    def _():
        for at, ref in enumerate((wq_ref, wk_ref, wv_ref)):
            w_s[at * span : (at + 1) * span] = ref[...]
        stack_rows(wo_s, 0, wa_ref, wb_ref, 0)
        gw_s[...] = jnp.zeros_like(gw_s)
        bias_s[...] = jnp.zeros_like(bias_s)

    gctx_s[...] = dot(gattn, wo_s[...], 1, 1).astype(BF16)
    gw_s[3 * span :] += dot(c_ref[...], gattn, 0, 0)
    attend_back_core(q_ref, k_ref, v_ref, lse_ref, qf_ref[...], kf_ref[...], dqkv_s, gctx_s)
    dqkv = dqkv_s[...]
    gw_s[: 3 * span] += dot(dqkv, tok_ref[...], 0, 0)
    bias_s[0:1] += column_sum(dqkv[:, :span].astype(F32))
    bias_s[1:2] += column_sum(dqkv[:, 2 * span :].astype(F32))

    @pl.when(step == pl.num_programs(0) - 1)
    def _():
        for which, (ref, f_ref) in enumerate(((ga_ref, fa_ref), (gb_ref, fb_ref))):
            two, last = which * cut, 2 * cut + which * HEAD
            for at in range(4):
                start, own = at * span, at * width
                ref[own : own + cut] = gw_s[start + two : start + two + cut].astype(BF16)
                ref[own + cut : own + width] = gw_s[start + last : start + last + HEAD].astype(BF16)
            bias = bias_s[...]
            row = [bias[at : at + 1, lo : lo + size] for at in range(2) for lo, size in ((two, cut), (last, HEAD))]
            row = jnp.concatenate(row + [jnp.zeros((1, ref.shape[1] - span), F32)], axis=1)
            extra = [row, f_ref[...], sums1_ref[0:3], sums2_ref[0:3]]
            extra.append(jnp.zeros((ref.shape[0] - 4 * width - 8, ref.shape[1]), F32))
            ref[4 * width :] = jnp.concatenate(extra, axis=0).astype(BF16)

    return dot(dqkv, w_s[...], 1, 0)


def attend_back_first(gn_ref, res_ref, g1_ref, *rest):
    ins, (ga_ref, gb_ref, gt_ref, gattn_ref, sums_ref), scratch = rest[:16], rest[16:21], rest[21:]
    unit, scale = unit_rows(res_ref[...])
    grad = gn_ref[...]
    resid = norm_back(grad, unit, scale, g1_ref[...])
    low = resid.astype(BF16)
    gattn_ref[...] = low

    @pl.when(pl.program_id(0) == 0)
    def _():
        sums_ref[...] = jnp.zeros_like(sums_ref)

    sums_ref[0:1] += column_sum(low.astype(F32))
    sums_ref[1:2] += column_sum(grad * unit)
    sums_ref[2:3] += column_sum(grad)
    gt_ref[...] = resid
    gt_ref[...] += attend_back_body(low, *ins, sums_ref, ga_ref, gb_ref, *scratch)


def attend_back_next(gattn_ref, gtin_ref, *rest):
    ins, (ga_ref, gb_ref, gt_ref), scratch = rest[:17], rest[17:20], rest[20:]
    gt_ref[...] = gtin_ref[...] + attend_back_body(gattn_ref[...], *ins, ga_ref, gb_ref, *scratch)


def attend_back(lead, tokens, saved, pieces, sums, wait=()):
    ctx, q, k, v, lse, qf, kf, wq, wk, wv = saved
    rows, depth = tokens.shape
    heads = lse.shape[1]
    blocks = rows // BLOCK
    first = len(lead) == 3
    span = q.shape[1]
    ins = [tiled(item, BLOCK) if item.shape[0] == rows else whole(item) for item in lead]
    ins += [tiled(item, BLOCK) for item in (tokens, ctx, q, k, v)]
    ins += [(lse, (1, heads, BLOCK), lambda i: (i, 0, 0)), tiled(qf, BLOCK), tiled(kf, BLOCK)]
    ins += [whole(item) for item in (wq, wk, wv)] + [out_rows(item) for item in pieces]
    ins += [whole(item) for item in sums]
    bundle = (2 * span + TAIL, depth)
    outs = [whole_out(bundle, BF16)] * 2 + [tiled_out((rows, depth), F32, BLOCK)]
    if first:
        outs += [tiled_out((rows, depth), BF16, BLOCK), whole_out((8, depth), F32)]
    return call(
        attend_back_first if first else attend_back_next,
        "attend_back",
        blocks,
        ins,
        outs,
        [
            pltpu.VMEM((3 * span, depth), BF16),
            pltpu.VMEM((span, depth), BF16),
            pltpu.VMEM((BLOCK, span), BF16),
            pltpu.VMEM((BLOCK, 3 * span), BF16),
            pltpu.VMEM((4 * span, depth), F32),
            pltpu.VMEM((8, span), F32),
        ],
        wait=wait,
    )


def picked(kernel, name, index, steps, ins, outs, wait=(), cost=10):
    count = len(ins)

    def body(_, *refs):
        kernel(*refs[:count], *refs[count + len(wait) :])

    anywhere = pl.BlockSpec(memory_space=pl.ANY)
    return pl.pallas_call(
        body,
        grid_spec=pltpu.PrefetchScalarGridSpec(
            num_scalar_prefetch=1,
            grid=(steps,),
            in_specs=[pl.BlockSpec(block, at) for _, block, at in ins] + [anywhere] * len(wait),
            out_specs=[pl.BlockSpec(block, at) for _, _, block, at in outs],
        ),
        out_shape=[jax.ShapeDtypeStruct(shape, dtype) for shape, dtype, _, _ in outs],
        compiler_params=pltpu.CompilerParams(dimension_semantics=("arbitrary",), vmem_limit_bytes=VMEM),
        cost_estimate=pl.CostEstimate(flops=cost * COST_UNIT + 1, bytes_accessed=1, transcendentals=0),
        name=name,
    )(index.astype(jnp.int32)[None], *[item[0] for item in ins], *wait)


def tiles_in(rows):
    return 2 if rows % 32 == 0 else 1


def combine(terms, index=None, count=1, after=(), cost=10):
    if index is None:
        index = jnp.zeros((), jnp.int32)
    rows, columns = terms[0].shape
    size = rows // count
    steps = tiles_in(size)
    tile = size // steps

    def chunk(k):
        return lambda i, at: ((at[0] ^ k) * steps + i, 0)

    def kernel(*refs):
        for k in range(count):
            total = sum(ref[...].astype(F32) for ref in refs[k * len(terms) : (k + 1) * len(terms)])
            refs[count * len(terms) + k][...] = total.astype(BF16)

    return picked(
        kernel,
        "combine",
        index,
        steps,
        [(term, (tile, columns), chunk(k)) for k in range(count) for term in terms],
        [((size, columns), BF16, (tile, columns), lambda i, at: (i, 0))] * count,
        after,
        cost,
    )


def arrange(parts, index, sizes=None, split=1, after=(), cost=10):
    size, columns = parts[0].shape
    count = len(parts)
    if sizes is None:
        each = size // split

        def kernel(index_ref, *refs):
            for here in range(count):

                @pl.when(index_ref[0] == here)
                def _(here=here):
                    for k in range(count):
                        start = (here ^ k) * each
                        for out in range(split):
                            refs[count + out][start : start + each] = refs[k][out * each : (out + 1) * each]

        return call(
            kernel,
            "arrange",
            1,
            [(index.astype(jnp.int32)[None], None, None)] + [whole(part) for part in parts],
            [whole_out((count * each, columns), BF16)] * split,
            wait=after,
            cost=cost,
        )

    def kernel_out(index_ref, *refs):
        for here in range(count):

            @pl.when(index_ref[0] == here)
            def _(here=here):
                start = 0
                for out in refs[count:]:
                    end = start + out.shape[0]
                    for k in range(count):
                        low = (here ^ k) * size
                        lo, hi = max(start, low), min(end, low + size)
                        if lo < hi:
                            out[lo - start : hi - start] = refs[k][lo - low : hi - low].astype(F32)
                    start = end

    return call(
        kernel_out,
        "arrange_out",
        1,
        [(index.astype(jnp.int32)[None], None, None)] + [whole(part) for part in parts],
        [whole_out((rows, columns), F32) for rows in sizes],
    )


def swap(values, axis, bit):
    count = lax.axis_size(axis)
    return lax.ppermute(values, axis, [(at, at ^ bit) for at in range(count)])


def gate(values, *after):
    def kernel(*refs):
        pass

    anywhere = pl.BlockSpec(memory_space=pl.ANY)
    return pl.pallas_call(
        kernel,
        in_specs=[anywhere] * (1 + len(after)),
        out_specs=anywhere,
        out_shape=jax.ShapeDtypeStruct(values.shape, values.dtype),
        input_output_aliases={0: 0},
        name="gate",
    )(values, *after)


def dp_bits():
    bits, bit = [], 1
    while bit < lax.axis_size("dp"):
        bits.append(bit)
        bit *= 2
    return bits


def groups(bits):
    return [bits[:1]] + [bits[at : at + 2] for at in range(1, len(bits), 2)]


def spot(bits):
    me = lax.axis_index("dp")
    at = sum(((me // bit) % 2) << i for i, bit in enumerate(bits))
    return at, [sum(bit for i, bit in enumerate(bits) if k >> i & 1) for k in range(1 << len(bits))]


def scatter(terms, bits, after=(), cost=10):
    at, far = spot(bits)
    kept, *sent = combine(terms, at, len(far), after, cost)
    return [kept] + [swap(item, "dp", distance) for item, distance in zip(sent, far[1:])]


def sum_whole(values, steps):
    for bit in [bit for step in steps for bit in step]:
        (values,) = combine((values, swap(values, "dp", bit)))
    return values


def gather(values, bits):
    _, far = spot(bits)
    return [values] + [swap(values, "dp", distance) for distance in far[1:]]


def ordered(parts, bits, sizes=None):
    return arrange(parts, spot(bits)[0], sizes)


def parity():
    me = lax.axis_index("dp")
    return (me ^ (me >> 1)) % 2


def my_half(arrays):
    columns = arrays[0].shape[1]
    quarters = [array.shape[0] // 4 for array in arrays]

    def kernel(*refs):
        ins, outs = refs[: 2 * len(arrays)], refs[2 * len(arrays) :]
        for part in range(2):
            start = 0
            for at, rows in enumerate(quarters):
                outs[part][start : start + rows] = ins[2 * at + part][...]
                start += rows

    return picked(
        kernel,
        "my_half",
        parity(),
        1,
        [
            (array, (rows, columns), lambda i, at, part=part: (at[0] * 2 + part, 0))
            for array, rows in zip(arrays, quarters)
            for part in range(2)
        ],
        [((sum(quarters), columns), BF16, (sum(quarters), columns), lambda i, at: (0, 0))] * 2,
    )


def pack(arrays):
    rows = sum(array.shape[0] for array in arrays)
    columns = arrays[0].shape[1]
    quarter = rows // 4

    def kernel(index_ref, *refs):
        ins, (out, *parts) = refs[: len(arrays)], refs[len(arrays) :]
        start = 0
        for ref in ins:
            out[start : start + ref.shape[0]] = ref[...]
            start += ref.shape[0]
        for side in range(2):

            @pl.when(index_ref[0] == side)
            def _(side=side):
                for at, part in enumerate(parts):
                    low = (2 * side + at) * quarter
                    part[...] = out[low : low + quarter]

    return call(
        kernel,
        "pack",
        1,
        [(parity().astype(jnp.int32)[None], None, None)] + [whole(array) for array in arrays],
        [whole_out((rows, columns), BF16)] + [whole_out((quarter, columns), BF16)] * 2,
    )


def other_half(first, second):
    return swap(first, "dp", 1), swap(second, "dp", 2)


def per_device(
    tokens, bucket, lengths, w_query, b_query, w_key, w_value, b_value, w_out, b_out, gain1, shift1,
    w_in, b_in, w_down, b_down, gain2, shift2, cotangent,
):
    rows, depth = tokens.shape
    width = w_query.shape[1]
    me = lax.axis_index("tensor")
    line = lambda v: v.astype(F32)[None]
    b_out, gain1, shift1, b_down, gain2, shift2 = map(line, (b_out, gain1, shift1, b_down, gain2, shift2))

    row = jnp.concatenate((b_query, b_value, jnp.zeros((depth - 2 * width,), BF16)))
    biases = jnp.pad(jnp.stack((row, b_in)), ((0, EXTRA - 2), (0, 0)))
    own, *parts = pack((w_query.T, w_key.T, w_value.T, w_out, biases))
    p1 = swap(own, "tensor", 1)
    pa, pb = [swap(item, "tensor", 2) for item in parts]
    wide = my_half((w_in, w_down))
    wa, wb = [swap(item, "tensor", 2) for item in wide]
    in1 = swap(w_in, "tensor", 1)
    down1 = swap(w_down, "tensor", 1)

    place_y = me.astype(jnp.int32)[None]
    (p2,) = arrange((pa, pb, *other_half(pa, pb)), 2 * parity(), cost=0)
    p3 = swap(p2, "tensor", 1)
    qn, kn, vn, cn, lsen, *wn, qf, kf = attend((bucket, lengths, place_y), tokens, own, p1, (*wide, p2, wa))
    qr, kr, vr, cr, lser, *wr = attend((qf, kf), tokens, p2, p3)
    wa, wb = gate(wa, cn), gate(wb, cn)
    others = other_half(wa, wb)
    in2, down2 = arrange((wa, wb, *others), 2 * parity(), split=2, after=(cr,))
    in3, down3 = swap(in2, "tensor", 1), swap(down2, "tensor", 1)
    residual, normed = join(tokens, cn, cr, (own, p1, p2, p3), b_out, gain1, shift1, (in2,))
    actn, facn = widen(normed, w_in, in1, own, p1)
    actr, facr = widen(normed, in2, in3, p2, p3)
    block_out, grad_summed, grad_ffn, sums2 = narrow(
        actn, actr, (w_down, down1, down2, down3), residual, gain1, shift1, b_down, gain2, shift2, cotangent
    )
    low, *highs = groups(dp_bits())
    d3, d2 = down_grad(grad_ffn, ((actr, 1), (actr, 0)))
    d1, d0 = down_grad(grad_ffn, ((actn, 1), (actn, 0)))
    (dfar,) = combine((d2, swap(d3, "tensor", 1)), after=(d0,), cost=10)
    i3, i2, fb3, fb2, grad_normed = ffn_back(
        grad_ffn, normed, grad_summed, (((facr, 1), down3, in3), ((facr, 0), down2, in2)), (dfar,)
    )
    i1, i0, fb1, fb0, grad_normed = ffn_back(
        grad_ffn, normed, grad_normed, (((facn, 1), down1, in1), ((facn, 0), w_down, w_in))
    )
    dfar = swap(dfar, "tensor", 2)
    i1 = swap(gate(i1, dfar), "tensor", 1)
    (ifar,) = combine((i2, swap(gate(i3, i0, dfar), "tensor", 1)), cost=10)
    dsum = scatter((d0, swap(d1, "tensor", 1), dfar), low, (i0,), 10)
    saved_r = (cr, qr, kr, vr, lser, qf, kf, *wr)
    saved_n = (cn, qn, kn, vn, lsen, qf, kf, *wn)
    a2, a3, grad_tokens, grad_attn, sums1 = attend_back(
        (grad_normed, residual, gain1), tokens, saved_r, (p2, p3), (fb2, fb3, sums2), (dsum[0], ifar)
    )
    ifar = swap(ifar, "tensor", 2)
    a3 = swap(gate(a3, dsum[1], ifar), "tensor", 1)
    (afar,) = combine((a2, a3), cost=10)
    dsum = scatter(dsum, highs[0], (a3,), 10)
    isum = scatter((i0, i1, ifar), low, (a3,), 10)
    a0, a1, grad_tokens = attend_back(
        (grad_attn, grad_tokens), tokens, saved_n, (own, p1), (fb0, fb1, sums2, sums1), (dsum[0], isum[0], afar)
    )
    afar = swap(afar, "tensor", 2)
    a1 = swap(gate(a1, afar, *dsum[1:], *isum[1:]), "tensor", 1)
    high, more = highs[0], highs[1:]
    asum = scatter((a0, a1, afar), low, cost=0)
    (dsum,) = combine(dsum, after=(asum[0],), cost=0)
    dparts = gather(sum_whole(dsum, more), high)
    isum = scatter(isum, high, (asum[0],), 0)
    asum = scatter(asum, high, (*dparts[1:], *isum[1:]), 0)
    dparts = gather(ordered(dparts, high)[0], low)
    (isum,) = combine(isum, cost=0)
    iparts = gather(sum_whole(isum, more), high)
    (asum,) = combine(asum, after=(dparts[1],), cost=0)
    aparts = gather(sum_whole(asum, more), high)
    iparts = gather(ordered(iparts, high)[0], low)
    (asum,) = ordered(aparts, high)
    (grad_wd,) = ordered(dparts, low, (w_down.shape[0],))
    (grad_wi,) = ordered(iparts, low, (depth,))
    *grad_qkv, grad_wo, small = ordered(gather(asum, low), low, (width,) * 4 + (8,))
    grad_wq, grad_wk, grad_wv = [item.T for item in grad_qkv]
    return (
        block_out,
        grad_tokens,
        grad_wq,
        small[0, :width],
        grad_wk,
        grad_wv,
        small[0, width : 2 * width],
        grad_wo,
        small[2],
        small[3],
        small[4],
        grad_wi,
        small[1],
        grad_wd,
        small[7],
        small[5],
        small[6],
    )


def solution(mesh):
    group = P(("dp", "tensor"), None)
    column, row, part, full = P(None, "tensor"), P("tensor", None), P("tensor"), P()
    in_specs = (
        group, P("dp"), P("dp", None), column, part, column, column, part, row,
        full, full, full, column, part, row, full, full, full, group,
    )
    out_specs = (
        group, group, column, part, column, column, part, row,
        full, full, full, column, part, row, full, full, full,
    )
    return jax.shard_map(
        per_device, mesh=mesh, in_specs=in_specs, out_specs=out_specs, check_vma=False
    )
```

```python
import functools

import jax
import jax.numpy as jnp
from jax import lax
from jax.experimental import pallas as pl
from jax.experimental.pallas import tpu as pltpu
from jax.sharding import PartitionSpec as P

HEAD = 64
BLOCK = 512
LANES = 128
EPSILON = 1e-12
EXTRA = 64
TAIL = 128
MASKED = -(2.0**30)
ROOT_HALF = 0.7071067811865476
PHI_SCALE = 0.3989422804014327
COSTS = {"attend": 10, "join": 6, "widen": 8, "narrow": 13, "down_grad": 6, "ffn_back": 0, "attend_back": 24}
COST_UNIT = 10**11
F32 = jnp.float32
BF16 = jnp.bfloat16
VMEM = 63 << 20


def dot(left, right, left_dim, right_dim):
    return lax.dot_general(
        left, right, (((left_dim,), (right_dim,)), ((), ())), preferred_element_type=F32
    )


def mean_rows(values):
    return jnp.mean(values, axis=-1, keepdims=True)


def unit_rows(values):
    centred = values - mean_rows(values)
    scale = lax.rsqrt(mean_rows(centred * centred) + EPSILON)
    return centred * scale, scale


def norm_back(grad, unit, scale, gain):
    e = grad * gain
    return scale * (e - mean_rows(e) - unit * mean_rows(e * unit))


def column_sum(values):
    return jnp.sum(values, axis=0, keepdims=True)


def call(kernel, name, steps, ins, outs, scratch=(), wait=(), cost=10):
    count = len(ins)

    def body(*refs):
        kernel(*refs[:count], *refs[count + len(wait) :])

    return pl.pallas_call(
        body,
        grid=(steps,),
        in_specs=[
            pl.BlockSpec(memory_space=pltpu.SMEM) if block is None else pl.BlockSpec(block, index)
            for _, block, index in ins
        ]
        + [pl.BlockSpec(memory_space=pl.ANY)] * len(wait),
        out_specs=[pl.BlockSpec(block, index) for _, _, block, index in outs],
        out_shape=[jax.ShapeDtypeStruct(shape, dtype) for shape, dtype, _, _ in outs],
        scratch_shapes=list(scratch),
        compiler_params=pltpu.CompilerParams(
            dimension_semantics=("arbitrary",), vmem_limit_bytes=VMEM
        ),
        cost_estimate=pl.CostEstimate(flops=COSTS.get(name, cost) * COST_UNIT + 1, bytes_accessed=1, transcendentals=0),
        name=name,
    )(*[item[0] for item in ins], *wait)


def whole(array):
    rank = array.ndim
    return (array, array.shape, lambda i: (0,) * rank)


def tiled(array, rows):
    return (array, (rows, array.shape[1]), lambda i: (i, 0))


def tiled_out(shape, dtype, rows):
    return (shape, dtype, (rows, shape[1]), lambda i: (i, 0))


def whole_out(shape, dtype):
    rank = len(shape)
    return (shape, dtype, shape, lambda i: (0,) * rank)


def head_scores(q_ref, k_ref, qf, kf, pair, head):
    cols = slice(pair * LANES, (pair + 1) * LANES)
    lane = lax.broadcasted_iota(jnp.int32, (1, LANES), 1)
    queries = q_ref[:, cols]
    queries = jnp.where(lane // HEAD == head, queries, jnp.zeros_like(queries))
    keys = jnp.concatenate([k_ref[:, cols], kf], axis=1)
    return dot(keys, jnp.concatenate([queries, qf], axis=1), 1, 1)


def mask_features(first, bucket_ref, lengths_ref):
    kind = bucket_ref[0]
    row_len = jnp.where(kind == 0, BLOCK // 4, jnp.where(kind == 1, BLOCK // 2, BLOCK))
    shift = jnp.where(kind == 0, 7, jnp.where(kind == 1, 8, 9))
    slot = lax.broadcasted_iota(jnp.int32, (BLOCK, LANES), 0)
    lane = lax.broadcasted_iota(jnp.int32, (BLOCK, LANES), 1)
    same = lax.shift_right_logical(slot, shift) == lane
    base = lax.shift_right_logical(first, shift)
    length = jnp.zeros((BLOCK, LANES), jnp.int32)
    for at in range(4):
        length = jnp.where(lane == at, lengths_ref[0, base + at], length)
    seen = same & ((slot & (row_len - 1)) < length)
    queries = jnp.where(same, 1.0, 0.0).astype(BF16)
    keys = jnp.where((lane < 4) & jnp.logical_not(seen), MASKED, 0.0).astype(BF16)
    return queries, keys


def lanes_of(first, second):
    cut = 2 * HEAD
    return (first, 0, cut), (second, 0, cut), (first, cut, HEAD), (second, cut, HEAD)


def stack_rows(out, start, first, second, offset):
    for ref, at, size in lanes_of(first, second):
        out[start : start + size] = ref[offset + at : offset + at + size]
        start += size


def attend_body(tok_ref, near_ref, far_ref, qf, kf, q_ref, k_ref, v_ref, c_ref, lse_ref, wq_ref, wk_ref, wv_ref):
    span = q_ref.shape[1]
    width = span // 2

    @pl.when(pl.program_id(0) == 0)
    def _():
        for at, w_ref in enumerate((wq_ref, wk_ref, wv_ref)):
            stack_rows(w_ref, 0, near_ref, far_ref, at * width)

    tokens = tok_ref[...]
    bias_row = 4 * width
    near, far = near_ref[bias_row : bias_row + 1].astype(F32), far_ref[bias_row : bias_row + 1].astype(F32)
    bq, bv = [
        jnp.concatenate(
            [row[:, start + at : start + at + size] for row, at, size in lanes_of(near, far)], axis=1
        )
        for start in (0, width)
    ]
    q = (dot(tokens, wq_ref[...], 1, 1) + bq).astype(BF16)
    q_ref[...] = q * jnp.asarray(HEAD**-0.5, BF16)
    k_ref[...] = dot(tokens, wk_ref[...], 1, 1).astype(BF16)
    v_ref[...] = (dot(tokens, wv_ref[...], 1, 1) + bv).astype(BF16)
    items = [(pair, head) for pair in range(span // LANES) for head in range(2)]
    ahead = head_scores(q_ref, k_ref, qf, kf, *items[0])
    done = []
    for at, (pair, head) in enumerate(items):
        scores = ahead
        if at + 1 < len(items):
            ahead = head_scores(q_ref, k_ref, qf, kf, *items[at + 1])
        cols = slice(pair * LANES, (pair + 1) * LANES)
        if head == 0:
            vals = v_ref[:, cols].T
        largest = jnp.max(scores, axis=0, keepdims=True)
        raised = jnp.exp(scores - largest)
        total = jnp.sum(raised, axis=0, keepdims=True)
        lse_ref[0, at : at + 1, :] = largest + jnp.log(total)
        mixed = dot(vals[head * HEAD : (head + 1) * HEAD], raised.astype(BF16), 1, 0)
        done.append(mixed * (1.0 / total))
        if head == 1:
            c_ref[:, cols] = jnp.concatenate(done, axis=0).T.astype(BF16)
            done = []


def attend_first(bucket_ref, lengths_ref, place_ref, tok_ref, near_ref, far_ref, *outs):
    qf_ref, kf_ref = outs[8:]
    first = (place_ref[0] * pl.num_programs(0) + pl.program_id(0)) * BLOCK
    qf_ref[...], kf_ref[...] = mask_features(first, bucket_ref, lengths_ref)
    attend_body(tok_ref, near_ref, far_ref, qf_ref[...], kf_ref[...], *outs[:8])


def attend_second(qf_ref, kf_ref, tok_ref, near_ref, far_ref, *outs):
    attend_body(tok_ref, near_ref, far_ref, qf_ref[...], kf_ref[...], *outs)


def attend(lead, tokens, near, far, wait=()):
    rows, depth = tokens.shape
    span = (near.shape[0] - EXTRA) // 2
    heads = span // HEAD
    blocks = rows // BLOCK
    first = len(lead) == 3
    if first:
        ins = [(item, None, None) for item in lead]
    else:
        ins = [tiled(item, BLOCK) for item in lead]
    outs = [tiled_out((rows, span), BF16, BLOCK)] * 4
    outs += [((blocks, heads, BLOCK), F32, (1, heads, BLOCK), lambda i: (i, 0, 0))]
    outs += [whole_out((span, depth), BF16)] * 3
    if first:
        outs += [tiled_out((rows, LANES), BF16, BLOCK)] * 2
    return call(
        attend_first if first else attend_second,
        "attend",
        blocks,
        ins + [tiled(tokens, BLOCK), whole(near), whole(far)],
        outs,
        wait=wait,
    )


def out_rows(packed):
    rows, columns = packed.shape
    width = (rows - EXTRA) // 4
    return (packed, (width, columns), lambda i: (3, 0))


def join_kernel(
    tok_ref, cn_ref, cf_ref, w0_ref, w1_ref, w2_ref, w3_ref, b_ref, g_ref, s_ref, res_ref, low_ref, w_s,
):
    span = cn_ref.shape[1]

    @pl.when(pl.program_id(0) == 0)
    def _():
        stack_rows(w_s, 0, w0_ref, w1_ref, 0)
        stack_rows(w_s, span, w2_ref, w3_ref, 0)

    out = dot(cn_ref[...], w_s[:span], 1, 0) + dot(cf_ref[...], w_s[span:], 1, 0)
    residual = tok_ref[...].astype(F32) + (out + b_ref[...])
    res_ref[...] = residual
    unit, _ = unit_rows(residual)
    low_ref[...] = (unit * g_ref[...] + s_ref[...]).astype(BF16)


def join(tokens, ctx_near, ctx_far, pieces, b_out, gain, shift, wait=()):
    rows, depth = tokens.shape
    tile = 256
    return call(
        join_kernel,
        "join",
        rows // tile,
        [tiled(tokens, tile), tiled(ctx_near, tile), tiled(ctx_far, tile)]
        + [out_rows(piece) for piece in pieces]
        + [whole(b_out), whole(gain), whole(shift)],
        [tiled_out((rows, depth), F32, tile), tiled_out((rows, depth), BF16, tile)],
        [pltpu.VMEM((depth, depth), BF16)],
        wait=wait,
    )


def widen_kernel(n_ref, wa_ref, wb_ref, ba_ref, bb_ref, act_ref, fac_ref):
    normed = n_ref[...]
    wide = wa_ref.shape[1]
    for at, (ref, b_ref) in enumerate(((wa_ref, ba_ref), (wb_ref, bb_ref))):
        cols = slice(at * wide, (at + 1) * wide)
        pre = dot(normed, ref[...], 1, 0) + b_ref[1:2, :wide].astype(F32)
        below = 0.5 + 0.5 * lax.erf(pre * ROOT_HALF)
        act_ref[:, cols] = (pre * below).astype(BF16)
        density = jnp.exp(-0.5 * pre * pre) * PHI_SCALE
        fac_ref[:, cols] = (below + pre * density).astype(BF16)


def bias_rows(packed):
    rows, columns = packed.shape
    return (packed, (EXTRA, columns), lambda i: (rows // EXTRA - 1, 0))


def widen(normed, wa, wb, bias_a, bias_b, wait=()):
    rows, depth = normed.shape
    tile = 256
    units = 2 * wa.shape[1]
    return call(
        widen_kernel,
        "widen",
        rows // tile,
        [tiled(normed, tile), whole(wa), whole(wb), bias_rows(bias_a), bias_rows(bias_b)],
        [tiled_out((rows, units), BF16, tile)] * 2,
        wait=wait,
    )


def narrow_kernel(
    an_ref, af_ref, w0_ref, w1_ref, w2_ref, w3_ref, res_ref, g1_ref, s1_ref, bd_ref, g2_ref, s2_ref, cot_ref,
    out_ref, gs_ref, gf_ref, sums_ref,
):
    unit1, _ = unit_rows(res_ref[...])
    wide = w0_ref.shape[0]
    out = dot(an_ref[:, :wide], w0_ref[...], 1, 0) + dot(an_ref[:, wide:], w1_ref[...], 1, 0)
    out = out + dot(af_ref[:, :wide], w2_ref[...], 1, 0) + dot(af_ref[:, wide:], w3_ref[...], 1, 0)
    summed = (unit1 * g1_ref[...] + s1_ref[...]) + (out + bd_ref[...])
    unit, scale = unit_rows(summed)
    out_ref[...] = (unit * g2_ref[...] + s2_ref[...]).astype(BF16)
    cot = cot_ref[...]
    grad = norm_back(cot, unit, scale, g2_ref[...])
    gs_ref[...] = grad
    low = grad.astype(BF16)
    gf_ref[...] = low

    @pl.when(pl.program_id(0) == 0)
    def _():
        sums_ref[...] = jnp.zeros_like(sums_ref)

    sums_ref[0:1] += column_sum(cot * unit)
    sums_ref[1:2] += column_sum(cot)
    sums_ref[2:3] += column_sum(low.astype(F32))


def narrow(act_near, act_far, w_downs, residual, gain1, shift1, b_down, gain2, shift2, cotangent, wait=()):
    rows, depth = residual.shape
    tile = 256
    return call(
        narrow_kernel,
        "narrow",
        rows // tile,
        [tiled(act_near, tile), tiled(act_far, tile)]
        + [whole(w) for w in w_downs]
        + [tiled(residual, tile)]
        + [whole(v) for v in (gain1, shift1, b_down, gain2, shift2)]
        + [tiled(cotangent, tile)],
        [
            tiled_out((rows, depth), BF16, tile),
            tiled_out((rows, depth), F32, tile),
            tiled_out((rows, depth), BF16, tile),
            whole_out((8, depth), F32),
        ],
        wait=wait,
    )


def down_grad_kernel(gf_ref, acta_ref, actb_ref, da_ref, db_ref):
    grad = gf_ref[...]
    da_ref[...] = dot(acta_ref[...], grad, 0, 0).astype(BF16)
    db_ref[...] = dot(actb_ref[...], grad, 0, 0).astype(BF16)


def half_tile(array, which, tile):
    steps = array.shape[1] // 2 // tile
    return (array, (array.shape[0], tile), lambda i: (0, which * steps + i))


def down_grad(grad_ffn, acts, wait=()):
    rows, depth = grad_ffn.shape
    units = acts[0][0].shape[1] // 2
    tile = units // 2
    return call(
        down_grad_kernel,
        "down_grad",
        units // tile,
        [whole(grad_ffn)] + [half_tile(*item, tile) for item in acts],
        [tiled_out((units, depth), BF16, tile)] * 2,
        wait=wait,
    )


def ffn_back_kernel(gf_ref, n_ref, gn_in_ref, *refs):
    count = (len(refs) - 5) // 2
    piece_a, piece_b, (ga_ref, gb_ref, gba_ref, gbb_ref, gn_ref) = refs[:count], refs[count:-5], refs[-5:]

    @pl.when(pl.program_id(0) == 0)
    def _():
        gn_ref[...] = gn_in_ref[...]

    grad = gf_ref[...]
    for (fac_ref, wd_ref, wi_ref, *got), g_ref, gbias_ref in ((piece_a, ga_ref, gba_ref), (piece_b, gb_ref, gbb_ref)):
        grad_pre = (dot(grad, wd_ref[...], 1, 1) * fac_ref[...].astype(F32)).astype(BF16)
        gbias_ref[...] = column_sum(grad_pre.astype(F32))
        out = dot(n_ref[...], grad_pre, 0, 0)
        if got:
            out = out + got[0][...].astype(F32)
        g_ref[...] = out.astype(BF16)
        gn_ref[...] += dot(grad_pre, wi_ref[...], 1, 1)


def ffn_back(grad_ffn, normed, grad_normed, pieces, wait=()):
    rows, depth = grad_ffn.shape
    units = pieces[0][1].shape[0]
    tile = units
    steps = units // tile
    column = lambda i: (0, i)
    ins = [whole(grad_ffn), whole(normed), whole(grad_normed)]
    for fac, wd, wi, *got in pieces:
        ins += [half_tile(*fac, tile), tiled(wd, tile), (wi, (depth, tile), column)]
        ins += [(item, (depth, tile), column) for item in got]
    return call(
        ffn_back_kernel,
        "ffn_back",
        steps,
        ins,
        [((depth, units), BF16, (depth, tile), column)] * 2
        + [((1, units), F32, (1, tile), column)] * 2
        + [whole_out((rows, depth), F32)],
        wait=wait,
    )


def attend_back_core(q_ref, k_ref, v_ref, lse_ref, qf, kf, dqkv_s, gctx_s):
    span = q_ref.shape[1]
    items = [(pair, head) for pair in range(span // LANES) for head in range(2)]
    lane = lax.broadcasted_iota(jnp.int32, (1, LANES), 1)

    def front(pair, head):
        cols = slice(pair * LANES, (pair + 1) * LANES)
        scores = head_scores(q_ref, k_ref, qf, kf, pair, head)
        out = gctx_s[:, cols]
        out = jnp.where(lane // HEAD == head, out, jnp.zeros_like(out))
        return scores, dot(v_ref[:, cols], out, 1, 1)

    ahead = front(*items[0])
    for at, (pair, head) in enumerate(items):
        scores, grad_probs = ahead
        if at + 1 < len(items):
            ahead = front(*items[at + 1])
        cols = slice(pair * LANES, (pair + 1) * LANES)
        mine = lane // HEAD == head
        queries, out = q_ref[:, cols], gctx_s[:, cols]
        queries = jnp.where(mine, queries, jnp.zeros_like(queries))
        out = jnp.where(mine, out, jnp.zeros_like(out))
        if head == 0:
            keys = (k_ref[:, cols] * jnp.asarray(HEAD**-0.5, BF16)).T
            dqs, dk, dv = [], 0.0, 0.0
        probs = jnp.exp(scores - lse_ref[0, at : at + 1, :])
        centre = jnp.sum(probs * grad_probs, axis=0, keepdims=True)
        grad_scores = (probs * (grad_probs - centre)).astype(BF16)
        dqs.append(dot(keys[head * HEAD : (head + 1) * HEAD], grad_scores, 1, 0))
        dk = dk + dot(grad_scores, queries, 1, 0)
        dv = dv + dot(probs.astype(BF16), out, 1, 0)
        if head == 1:
            start = pair * LANES
            dqkv_s[:, start : start + LANES] = jnp.concatenate(dqs, axis=0).T.astype(BF16)
            dqkv_s[:, span + start : span + start + LANES] = dk.astype(BF16)
            dqkv_s[:, 2 * span + start : 2 * span + start + LANES] = dv.astype(BF16)


def attend_back_body(
    gattn, tok_ref, c_ref, q_ref, k_ref, v_ref, lse_ref, qf_ref, kf_ref, wq_ref, wk_ref, wv_ref, wa_ref, wb_ref,
    fa_ref, fb_ref, sums2_ref, sums1_ref, ga_ref, gb_ref, w_s, wo_s, gctx_s, dqkv_s, gw_s, bias_s,
):
    step = pl.program_id(0)
    span = q_ref.shape[1]
    width = span // 2
    cut = 2 * HEAD

    @pl.when(step == 0)
    def _():
        for at, ref in enumerate((wq_ref, wk_ref, wv_ref)):
            w_s[at * span : (at + 1) * span] = ref[...]
        stack_rows(wo_s, 0, wa_ref, wb_ref, 0)
        gw_s[...] = jnp.zeros_like(gw_s)
        bias_s[...] = jnp.zeros_like(bias_s)

    gctx_s[...] = dot(gattn, wo_s[...], 1, 1).astype(BF16)
    gw_s[3 * span :] += dot(c_ref[...], gattn, 0, 0)
    attend_back_core(q_ref, k_ref, v_ref, lse_ref, qf_ref[...], kf_ref[...], dqkv_s, gctx_s)
    dqkv = dqkv_s[...]
    gw_s[: 3 * span] += dot(dqkv, tok_ref[...], 0, 0)
    bias_s[0:1] += column_sum(dqkv[:, :span].astype(F32))
    bias_s[1:2] += column_sum(dqkv[:, 2 * span :].astype(F32))

    @pl.when(step == pl.num_programs(0) - 1)
    def _():
        for which, (ref, f_ref) in enumerate(((ga_ref, fa_ref), (gb_ref, fb_ref))):
            two, last = which * cut, 2 * cut + which * HEAD
            for at in range(4):
                start, own = at * span, at * width
                ref[own : own + cut] = gw_s[start + two : start + two + cut].astype(BF16)
                ref[own + cut : own + width] = gw_s[start + last : start + last + HEAD].astype(BF16)
            bias = bias_s[...]
            row = [bias[at : at + 1, lo : lo + size] for at in range(2) for lo, size in ((two, cut), (last, HEAD))]
            row = jnp.concatenate(row + [jnp.zeros((1, ref.shape[1] - span), F32)], axis=1)
            extra = [row, f_ref[...], sums1_ref[0:3], sums2_ref[0:3]]
            extra.append(jnp.zeros((ref.shape[0] - 4 * width - 8, ref.shape[1]), F32))
            ref[4 * width :] = jnp.concatenate(extra, axis=0).astype(BF16)

    return dot(dqkv, w_s[...], 1, 0)


def attend_back_first(gn_ref, res_ref, g1_ref, *rest):
    ins, (ga_ref, gb_ref, gt_ref, gattn_ref, sums_ref), scratch = rest[:16], rest[16:21], rest[21:]
    unit, scale = unit_rows(res_ref[...])
    grad = gn_ref[...]
    resid = norm_back(grad, unit, scale, g1_ref[...])
    low = resid.astype(BF16)
    gattn_ref[...] = low

    @pl.when(pl.program_id(0) == 0)
    def _():
        sums_ref[...] = jnp.zeros_like(sums_ref)

    sums_ref[0:1] += column_sum(low.astype(F32))
    sums_ref[1:2] += column_sum(grad * unit)
    sums_ref[2:3] += column_sum(grad)
    gt_ref[...] = resid
    gt_ref[...] += attend_back_body(low, *ins, sums_ref, ga_ref, gb_ref, *scratch)


def attend_back_next(gattn_ref, gtin_ref, *rest):
    ins, (ga_ref, gb_ref, gt_ref), scratch = rest[:17], rest[17:20], rest[20:]
    gt_ref[...] = gtin_ref[...] + attend_back_body(gattn_ref[...], *ins, ga_ref, gb_ref, *scratch)


def attend_back(lead, tokens, saved, pieces, sums, wait=()):
    ctx, q, k, v, lse, qf, kf, wq, wk, wv = saved
    rows, depth = tokens.shape
    heads = lse.shape[1]
    blocks = rows // BLOCK
    first = len(lead) == 3
    span = q.shape[1]
    ins = [tiled(item, BLOCK) if item.shape[0] == rows else whole(item) for item in lead]
    ins += [tiled(item, BLOCK) for item in (tokens, ctx, q, k, v)]
    ins += [(lse, (1, heads, BLOCK), lambda i: (i, 0, 0)), tiled(qf, BLOCK), tiled(kf, BLOCK)]
    ins += [whole(item) for item in (wq, wk, wv)] + [out_rows(item) for item in pieces]
    ins += [whole(item) for item in sums]
    bundle = (2 * span + TAIL, depth)
    outs = [whole_out(bundle, BF16)] * 2 + [tiled_out((rows, depth), F32, BLOCK)]
    if first:
        outs += [tiled_out((rows, depth), BF16, BLOCK), whole_out((8, depth), F32)]
    return call(
        attend_back_first if first else attend_back_next,
        "attend_back",
        blocks,
        ins,
        outs,
        [
            pltpu.VMEM((3 * span, depth), BF16),
            pltpu.VMEM((span, depth), BF16),
            pltpu.VMEM((BLOCK, span), BF16),
            pltpu.VMEM((BLOCK, 3 * span), BF16),
            pltpu.VMEM((4 * span, depth), F32),
            pltpu.VMEM((8, span), F32),
        ],
        wait=wait,
    )


def picked(kernel, name, index, steps, ins, outs, wait=(), cost=10):
    count = len(ins)

    def body(_, *refs):
        kernel(*refs[:count], *refs[count + len(wait) :])

    anywhere = pl.BlockSpec(memory_space=pl.ANY)
    return pl.pallas_call(
        body,
        grid_spec=pltpu.PrefetchScalarGridSpec(
            num_scalar_prefetch=1,
            grid=(steps,),
            in_specs=[pl.BlockSpec(block, at) for _, block, at in ins] + [anywhere] * len(wait),
            out_specs=[pl.BlockSpec(block, at) for _, _, block, at in outs],
        ),
        out_shape=[jax.ShapeDtypeStruct(shape, dtype) for shape, dtype, _, _ in outs],
        compiler_params=pltpu.CompilerParams(dimension_semantics=("arbitrary",), vmem_limit_bytes=VMEM),
        cost_estimate=pl.CostEstimate(flops=cost * COST_UNIT + 1, bytes_accessed=1, transcendentals=0),
        name=name,
    )(index.astype(jnp.int32)[None], *[item[0] for item in ins], *wait)


def tiles_in(rows):
    return 2 if rows % 32 == 0 else 1


def combine(terms, index=None, count=1, after=(), cost=10):
    if index is None:
        index = jnp.zeros((), jnp.int32)
    rows, columns = terms[0].shape
    size = rows // count
    steps = tiles_in(size)
    tile = size // steps

    def chunk(k):
        return lambda i, at: ((at[0] ^ k) * steps + i, 0)

    def kernel(*refs):
        for k in range(count):
            total = sum(ref[...].astype(F32) for ref in refs[k * len(terms) : (k + 1) * len(terms)])
            refs[count * len(terms) + k][...] = total.astype(BF16)

    return picked(
        kernel,
        "combine",
        index,
        steps,
        [(term, (tile, columns), chunk(k)) for k in range(count) for term in terms],
        [((size, columns), BF16, (tile, columns), lambda i, at: (i, 0))] * count,
        after,
        cost,
    )


def arrange(parts, index, sizes=None, split=1, after=(), cost=10):
    size, columns = parts[0].shape
    count = len(parts)
    if sizes is None:
        each = size // split

        def kernel(index_ref, *refs):
            for here in range(count):

                @pl.when(index_ref[0] == here)
                def _(here=here):
                    for k in range(count):
                        start = (here ^ k) * each
                        for out in range(split):
                            refs[count + out][start : start + each] = refs[k][out * each : (out + 1) * each]

        return call(
            kernel,
            "arrange",
            1,
            [(index.astype(jnp.int32)[None], None, None)] + [whole(part) for part in parts],
            [whole_out((count * each, columns), BF16)] * split,
            wait=after,
            cost=cost,
        )

    def kernel_out(index_ref, *refs):
        for here in range(count):

            @pl.when(index_ref[0] == here)
            def _(here=here):
                start = 0
                for out in refs[count:]:
                    end = start + out.shape[0]
                    for k in range(count):
                        low = (here ^ k) * size
                        lo, hi = max(start, low), min(end, low + size)
                        if lo < hi:
                            out[lo - start : hi - start] = refs[k][lo - low : hi - low].astype(F32)
                    start = end

    return call(
        kernel_out,
        "arrange_out",
        1,
        [(index.astype(jnp.int32)[None], None, None)] + [whole(part) for part in parts],
        [whole_out((rows, columns), F32) for rows in sizes],
    )


def swap(values, axis, bit):
    count = lax.axis_size(axis)
    return lax.ppermute(values, axis, [(at, at ^ bit) for at in range(count)])


def gate(values, *after):
    def kernel(*refs):
        pass

    anywhere = pl.BlockSpec(memory_space=pl.ANY)
    return pl.pallas_call(
        kernel,
        in_specs=[anywhere] * (1 + len(after)),
        out_specs=anywhere,
        out_shape=jax.ShapeDtypeStruct(values.shape, values.dtype),
        input_output_aliases={0: 0},
        name="gate",
    )(values, *after)


def dp_bits():
    bits, bit = [], 1
    while bit < lax.axis_size("dp"):
        bits.append(bit)
        bit *= 2
    return bits


def groups(bits):
    return [bits[:1]] + [bits[at : at + 2] for at in range(1, len(bits), 2)]


def spot(bits):
    me = lax.axis_index("dp")
    at = sum(((me // bit) % 2) << i for i, bit in enumerate(bits))
    return at, [sum(bit for i, bit in enumerate(bits) if k >> i & 1) for k in range(1 << len(bits))]


def scatter(terms, bits, after=(), cost=10):
    at, far = spot(bits)
    kept, *sent = combine(terms, at, len(far), after, cost)
    return [kept] + [swap(item, "dp", distance) for item, distance in zip(sent, far[1:])]


def sum_whole(values, steps):
    for bit in [bit for step in steps for bit in step]:
        (values,) = combine((values, swap(values, "dp", bit)))
    return values


def gather(values, bits):
    _, far = spot(bits)
    return [values] + [swap(values, "dp", distance) for distance in far[1:]]


def ordered(parts, bits, sizes=None):
    return arrange(parts, spot(bits)[0], sizes)


def parity():
    me = lax.axis_index("dp")
    return (me ^ (me >> 1)) % 2


def my_half(arrays):
    columns = arrays[0].shape[1]
    quarters = [array.shape[0] // 4 for array in arrays]

    def kernel(*refs):
        ins, outs = refs[: 2 * len(arrays)], refs[2 * len(arrays) :]
        for part in range(2):
            start = 0
            for at, rows in enumerate(quarters):
                outs[part][start : start + rows] = ins[2 * at + part][...]
                start += rows

    return picked(
        kernel,
        "my_half",
        parity(),
        1,
        [
            (array, (rows, columns), lambda i, at, part=part: (at[0] * 2 + part, 0))
            for array, rows in zip(arrays, quarters)
            for part in range(2)
        ],
        [((sum(quarters), columns), BF16, (sum(quarters), columns), lambda i, at: (0, 0))] * 2,
    )


def pack(arrays):
    rows = sum(array.shape[0] for array in arrays)
    columns = arrays[0].shape[1]
    quarter = rows // 4

    def kernel(index_ref, *refs):
        ins, (out, *parts) = refs[: len(arrays)], refs[len(arrays) :]
        start = 0
        for ref in ins:
            out[start : start + ref.shape[0]] = ref[...]
            start += ref.shape[0]
        for side in range(2):

            @pl.when(index_ref[0] == side)
            def _(side=side):
                for at, part in enumerate(parts):
                    low = (2 * side + at) * quarter
                    part[...] = out[low : low + quarter]

    return call(
        kernel,
        "pack",
        1,
        [(parity().astype(jnp.int32)[None], None, None)] + [whole(array) for array in arrays],
        [whole_out((rows, columns), BF16)] + [whole_out((quarter, columns), BF16)] * 2,
    )


def other_half(first, second):
    return swap(first, "dp", 1), swap(second, "dp", 2)


def per_device(
    tokens, bucket, lengths, w_query, b_query, w_key, w_value, b_value, w_out, b_out, gain1, shift1,
    w_in, b_in, w_down, b_down, gain2, shift2, cotangent,
):
    rows, depth = tokens.shape
    width = w_query.shape[1]
    me = lax.axis_index("tensor")
    line = lambda v: v.astype(F32)[None]
    b_out, gain1, shift1, b_down, gain2, shift2 = map(line, (b_out, gain1, shift1, b_down, gain2, shift2))

    row = jnp.concatenate((b_query, b_value, jnp.zeros((depth - 2 * width,), BF16)))
    biases = jnp.pad(jnp.stack((row, b_in)), ((0, EXTRA - 2), (0, 0)))
    own, *parts = pack((w_query.T, w_key.T, w_value.T, w_out, biases))
    p1 = swap(own, "tensor", 1)
    pa, pb = [swap(item, "tensor", 2) for item in parts]
    wide = my_half((w_in, w_down))
    wa, wb = [swap(item, "tensor", 2) for item in wide]
    in1 = swap(w_in, "tensor", 1)
    down1 = swap(w_down, "tensor", 1)

    place_y = me.astype(jnp.int32)[None]
    (p2,) = arrange((pa, pb, *other_half(pa, pb)), 2 * parity(), cost=0)
    p3 = swap(p2, "tensor", 1)
    qn, kn, vn, cn, lsen, *wn, qf, kf = attend((bucket, lengths, place_y), tokens, own, p1, (*wide, p2, wa))
    qr, kr, vr, cr, lser, *wr = attend((qf, kf), tokens, p2, p3)
    wa, wb = gate(wa, cn), gate(wb, cn)
    others = other_half(wa, wb)
    residual, normed = join(tokens, cn, cr, (own, p1, p2, p3), b_out, gain1, shift1)
    in2, down2 = arrange((wa, wb, *others), 2 * parity(), split=2, after=(normed,))
    in3, down3 = swap(in2, "tensor", 1), swap(down2, "tensor", 1)
    actn, facn = widen(normed, w_in, in1, own, p1, (in2,))
    actr, facr = widen(normed, in2, in3, p2, p3)
    block_out, grad_summed, grad_ffn, sums2 = narrow(
        actn, actr, (w_down, down1, down2, down3), residual, gain1, shift1, b_down, gain2, shift2, cotangent
    )
    low, *highs = groups(dp_bits())
    d3, d2 = down_grad(grad_ffn, ((actr, 1), (actr, 0)))
    d1, d0 = down_grad(grad_ffn, ((actn, 1), (actn, 0)))
    (dfar,) = combine((d2, swap(d3, "tensor", 1)), after=(d0,), cost=10)
    i3, i2, fb3, fb2, grad_normed = ffn_back(
        grad_ffn, normed, grad_summed, (((facr, 1), down3, in3), ((facr, 0), down2, in2)), (dfar,)
    )
    i1, i0, fb1, fb0, grad_normed = ffn_back(
        grad_ffn, normed, grad_normed, (((facn, 1), down1, in1), ((facn, 0), w_down, w_in))
    )
    dfar = swap(dfar, "tensor", 2)
    i1 = swap(gate(i1, dfar), "tensor", 1)
    (ifar,) = combine((i2, swap(gate(i3, i0, dfar), "tensor", 1)), cost=10)
    dsum = scatter((d0, swap(d1, "tensor", 1), dfar), low, (i0,), 10)
    saved_r = (cr, qr, kr, vr, lser, qf, kf, *wr)
    saved_n = (cn, qn, kn, vn, lsen, qf, kf, *wn)
    a2, a3, grad_tokens, grad_attn, sums1 = attend_back(
        (grad_normed, residual, gain1), tokens, saved_r, (p2, p3), (fb2, fb3, sums2), (dsum[0], ifar)
    )
    ifar = swap(ifar, "tensor", 2)
    a3 = swap(gate(a3, dsum[1], ifar), "tensor", 1)
    (afar,) = combine((a2, a3), cost=10)
    dsum = scatter(dsum, highs[0], (a3,), 10)
    isum = scatter((i0, i1, ifar), low, (a3,), 10)
    a0, a1, grad_tokens = attend_back(
        (grad_attn, grad_tokens), tokens, saved_n, (own, p1), (fb0, fb1, sums2, sums1), (dsum[0], isum[0], afar)
    )
    afar = swap(afar, "tensor", 2)
    a1 = swap(gate(a1, afar, *dsum[1:], *isum[1:]), "tensor", 1)
    high, more = highs[0], highs[1:]
    asum = scatter((a0, a1, afar), low, cost=0)
    (dsum,) = combine(dsum, after=(asum[0],), cost=0)
    dparts = gather(sum_whole(dsum, more), high)
    isum = scatter(isum, high, (asum[0],), 0)
    asum = scatter(asum, high, (*dparts[1:], *isum[1:]), 0)
    dparts = gather(ordered(dparts, high)[0], low)
    (isum,) = combine(isum, cost=0)
    iparts = gather(sum_whole(isum, more), high)
    (asum,) = combine(asum, after=(dparts[1],), cost=0)
    aparts = gather(sum_whole(asum, more), high)
    iparts = gather(ordered(iparts, high)[0], low)
    (asum,) = ordered(aparts, high)
    (grad_wd,) = ordered(dparts, low, (w_down.shape[0],))
    (grad_wi,) = ordered(iparts, low, (depth,))
    *grad_qkv, grad_wo, small = ordered(gather(asum, low), low, (width,) * 4 + (8,))
    grad_wq, grad_wk, grad_wv = [item.T for item in grad_qkv]
    return (
        block_out,
        grad_tokens,
        grad_wq,
        small[0, :width],
        grad_wk,
        grad_wv,
        small[0, width : 2 * width],
        grad_wo,
        small[2],
        small[3],
        small[4],
        grad_wi,
        small[1],
        grad_wd,
        small[7],
        small[5],
        small[6],
    )


def solution(mesh):
    group = P(("dp", "tensor"), None)
    column, row, part, full = P(None, "tensor"), P("tensor", None), P("tensor"), P()
    in_specs = (
        group, P("dp"), P("dp", None), column, part, column, column, part, row,
        full, full, full, column, part, row, full, full, full, group,
    )
    out_specs = (
        group, group, column, part, column, column, part, row,
        full, full, full, column, part, row, full, full, full,
    )
    return jax.shard_map(
        per_device, mesh=mesh, in_specs=in_specs, out_specs=out_specs, check_vma=False
    )
```

```python
import functools

import jax
import jax.numpy as jnp
from jax import lax
from jax.experimental import pallas as pl
from jax.experimental.pallas import tpu as pltpu
from jax.sharding import PartitionSpec as P

HEAD = 64
BLOCK = 512
LANES = 128
EPSILON = 1e-12
EXTRA = 64
TAIL = 128
MASKED = -(2.0**30)
ROOT_HALF = 0.7071067811865476
PHI_SCALE = 0.3989422804014327
COSTS = {"attend": 10, "join": 6, "widen": 8, "narrow": 13, "down_grad": 6, "ffn_back": 0, "attend_back": 24}
COST_UNIT = 10**11
F32 = jnp.float32
BF16 = jnp.bfloat16
VMEM = 63 << 20


def dot(left, right, left_dim, right_dim):
    return lax.dot_general(
        left, right, (((left_dim,), (right_dim,)), ((), ())), preferred_element_type=F32
    )


def mean_rows(values):
    return jnp.mean(values, axis=-1, keepdims=True)


def unit_rows(values):
    centred = values - mean_rows(values)
    scale = lax.rsqrt(mean_rows(centred * centred) + EPSILON)
    return centred * scale, scale


def norm_back(grad, unit, scale, gain):
    e = grad * gain
    return scale * (e - mean_rows(e) - unit * mean_rows(e * unit))


def column_sum(values):
    return jnp.sum(values, axis=0, keepdims=True)


def call(kernel, name, steps, ins, outs, scratch=(), wait=(), cost=10):
    count = len(ins)

    def body(*refs):
        kernel(*refs[:count], *refs[count + len(wait) :])

    return pl.pallas_call(
        body,
        grid=(steps,),
        in_specs=[
            pl.BlockSpec(memory_space=pltpu.SMEM) if block is None else pl.BlockSpec(block, index)
            for _, block, index in ins
        ]
        + [pl.BlockSpec(memory_space=pl.ANY)] * len(wait),
        out_specs=[pl.BlockSpec(block, index) for _, _, block, index in outs],
        out_shape=[jax.ShapeDtypeStruct(shape, dtype) for shape, dtype, _, _ in outs],
        scratch_shapes=list(scratch),
        compiler_params=pltpu.CompilerParams(
            dimension_semantics=("arbitrary",), vmem_limit_bytes=VMEM
        ),
        cost_estimate=pl.CostEstimate(flops=COSTS.get(name, cost) * COST_UNIT + 1, bytes_accessed=1, transcendentals=0),
        name=name,
    )(*[item[0] for item in ins], *wait)


def whole(array):
    rank = array.ndim
    return (array, array.shape, lambda i: (0,) * rank)


def tiled(array, rows):
    return (array, (rows, array.shape[1]), lambda i: (i, 0))


def tiled_out(shape, dtype, rows):
    return (shape, dtype, (rows, shape[1]), lambda i: (i, 0))


def whole_out(shape, dtype):
    rank = len(shape)
    return (shape, dtype, shape, lambda i: (0,) * rank)


def head_scores(q_ref, k_ref, qf, kf, pair, head):
    cols = slice(pair * LANES, (pair + 1) * LANES)
    lane = lax.broadcasted_iota(jnp.int32, (1, LANES), 1)
    queries = q_ref[:, cols]
    queries = jnp.where(lane // HEAD == head, queries, jnp.zeros_like(queries))
    keys = jnp.concatenate([k_ref[:, cols], kf], axis=1)
    return dot(keys, jnp.concatenate([queries, qf], axis=1), 1, 1)


def mask_features(first, bucket_ref, lengths_ref):
    kind = bucket_ref[0]
    row_len = jnp.where(kind == 0, BLOCK // 4, jnp.where(kind == 1, BLOCK // 2, BLOCK))
    shift = jnp.where(kind == 0, 7, jnp.where(kind == 1, 8, 9))
    slot = lax.broadcasted_iota(jnp.int32, (BLOCK, LANES), 0)
    lane = lax.broadcasted_iota(jnp.int32, (BLOCK, LANES), 1)
    same = lax.shift_right_logical(slot, shift) == lane
    base = lax.shift_right_logical(first, shift)
    length = jnp.zeros((BLOCK, LANES), jnp.int32)
    for at in range(4):
        length = jnp.where(lane == at, lengths_ref[0, base + at], length)
    seen = same & ((slot & (row_len - 1)) < length)
    queries = jnp.where(same, 1.0, 0.0).astype(BF16)
    keys = jnp.where((lane < 4) & jnp.logical_not(seen), MASKED, 0.0).astype(BF16)
    return queries, keys


def lanes_of(first, second):
    cut = 2 * HEAD
    return (first, 0, cut), (second, 0, cut), (first, cut, HEAD), (second, cut, HEAD)


def stack_rows(out, start, first, second, offset):
    for ref, at, size in lanes_of(first, second):
        out[start : start + size] = ref[offset + at : offset + at + size]
        start += size


def attend_body(tok_ref, near_ref, far_ref, qf, kf, q_ref, k_ref, v_ref, c_ref, lse_ref, wq_ref, wk_ref, wv_ref):
    span = q_ref.shape[1]
    width = span // 2

    @pl.when(pl.program_id(0) == 0)
    def _():
        for at, w_ref in enumerate((wq_ref, wk_ref, wv_ref)):
            stack_rows(w_ref, 0, near_ref, far_ref, at * width)

    tokens = tok_ref[...]
    bias_row = 4 * width
    near, far = near_ref[bias_row : bias_row + 1].astype(F32), far_ref[bias_row : bias_row + 1].astype(F32)
    bq, bv = [
        jnp.concatenate(
            [row[:, start + at : start + at + size] for row, at, size in lanes_of(near, far)], axis=1
        )
        for start in (0, width)
    ]
    q = (dot(tokens, wq_ref[...], 1, 1) + bq).astype(BF16)
    q_ref[...] = q * jnp.asarray(HEAD**-0.5, BF16)
    k_ref[...] = dot(tokens, wk_ref[...], 1, 1).astype(BF16)
    v_ref[...] = (dot(tokens, wv_ref[...], 1, 1) + bv).astype(BF16)
    items = [(pair, head) for pair in range(span // LANES) for head in range(2)]
    ahead = head_scores(q_ref, k_ref, qf, kf, *items[0])
    done = []
    for at, (pair, head) in enumerate(items):
        scores = ahead
        if at + 1 < len(items):
            ahead = head_scores(q_ref, k_ref, qf, kf, *items[at + 1])
        cols = slice(pair * LANES, (pair + 1) * LANES)
        if head == 0:
            vals = v_ref[:, cols].T
        largest = jnp.max(scores, axis=0, keepdims=True)
        raised = jnp.exp(scores - largest)
        total = jnp.sum(raised, axis=0, keepdims=True)
        lse_ref[0, at : at + 1, :] = largest + jnp.log(total)
        mixed = dot(vals[head * HEAD : (head + 1) * HEAD], raised.astype(BF16), 1, 0)
        done.append(mixed * (1.0 / total))
        if head == 1:
            c_ref[:, cols] = jnp.concatenate(done, axis=0).T.astype(BF16)
            done = []


def attend_first(bucket_ref, lengths_ref, place_ref, tok_ref, near_ref, far_ref, *outs):
    qf_ref, kf_ref = outs[8:]
    first = (place_ref[0] * pl.num_programs(0) + pl.program_id(0)) * BLOCK
    qf_ref[...], kf_ref[...] = mask_features(first, bucket_ref, lengths_ref)
    attend_body(tok_ref, near_ref, far_ref, qf_ref[...], kf_ref[...], *outs[:8])


def attend_second(qf_ref, kf_ref, tok_ref, near_ref, far_ref, *outs):
    attend_body(tok_ref, near_ref, far_ref, qf_ref[...], kf_ref[...], *outs)


def attend(lead, tokens, near, far, wait=()):
    rows, depth = tokens.shape
    span = (near.shape[0] - EXTRA) // 2
    heads = span // HEAD
    blocks = rows // BLOCK
    first = len(lead) == 3
    if first:
        ins = [(item, None, None) for item in lead]
    else:
        ins = [tiled(item, BLOCK) for item in lead]
    outs = [tiled_out((rows, span), BF16, BLOCK)] * 4
    outs += [((blocks, heads, BLOCK), F32, (1, heads, BLOCK), lambda i: (i, 0, 0))]
    outs += [whole_out((span, depth), BF16)] * 3
    if first:
        outs += [tiled_out((rows, LANES), BF16, BLOCK)] * 2
    return call(
        attend_first if first else attend_second,
        "attend",
        blocks,
        ins + [tiled(tokens, BLOCK), whole(near), whole(far)],
        outs,
        wait=wait,
    )


def out_rows(packed):
    rows, columns = packed.shape
    width = (rows - EXTRA) // 4
    return (packed, (width, columns), lambda i: (3, 0))


def join_kernel(
    tok_ref, cn_ref, cf_ref, w0_ref, w1_ref, w2_ref, w3_ref, b_ref, g_ref, s_ref, res_ref, low_ref, w_s,
):
    span = cn_ref.shape[1]

    @pl.when(pl.program_id(0) == 0)
    def _():
        stack_rows(w_s, 0, w0_ref, w1_ref, 0)
        stack_rows(w_s, span, w2_ref, w3_ref, 0)

    out = dot(cn_ref[...], w_s[:span], 1, 0) + dot(cf_ref[...], w_s[span:], 1, 0)
    residual = tok_ref[...].astype(F32) + (out + b_ref[...])
    res_ref[...] = residual
    unit, _ = unit_rows(residual)
    low_ref[...] = (unit * g_ref[...] + s_ref[...]).astype(BF16)


def join(tokens, ctx_near, ctx_far, pieces, b_out, gain, shift, wait=()):
    rows, depth = tokens.shape
    tile = 256
    return call(
        join_kernel,
        "join",
        rows // tile,
        [tiled(tokens, tile), tiled(ctx_near, tile), tiled(ctx_far, tile)]
        + [out_rows(piece) for piece in pieces]
        + [whole(b_out), whole(gain), whole(shift)],
        [tiled_out((rows, depth), F32, tile), tiled_out((rows, depth), BF16, tile)],
        [pltpu.VMEM((depth, depth), BF16)],
        wait=wait,
    )


def widen_kernel(n_ref, wa_ref, wb_ref, ba_ref, bb_ref, act_ref, fac_ref):
    normed = n_ref[...]
    wide = wa_ref.shape[1]
    for at, (ref, b_ref) in enumerate(((wa_ref, ba_ref), (wb_ref, bb_ref))):
        cols = slice(at * wide, (at + 1) * wide)
        pre = dot(normed, ref[...], 1, 0) + b_ref[1:2, :wide].astype(F32)
        below = 0.5 + 0.5 * lax.erf(pre * ROOT_HALF)
        act_ref[:, cols] = (pre * below).astype(BF16)
        density = jnp.exp(-0.5 * pre * pre) * PHI_SCALE
        fac_ref[:, cols] = (below + pre * density).astype(BF16)


def bias_rows(packed):
    rows, columns = packed.shape
    return (packed, (EXTRA, columns), lambda i: (rows // EXTRA - 1, 0))


def widen(normed, wa, wb, bias_a, bias_b, wait=()):
    rows, depth = normed.shape
    tile = 256
    units = 2 * wa.shape[1]
    return call(
        widen_kernel,
        "widen",
        rows // tile,
        [tiled(normed, tile), whole(wa), whole(wb), bias_rows(bias_a), bias_rows(bias_b)],
        [tiled_out((rows, units), BF16, tile)] * 2,
        wait=wait,
    )


def narrow_kernel(
    an_ref, af_ref, w0_ref, w1_ref, w2_ref, w3_ref, res_ref, g1_ref, s1_ref, bd_ref, g2_ref, s2_ref, cot_ref,
    out_ref, gs_ref, gf_ref, sums_ref,
):
    unit1, _ = unit_rows(res_ref[...])
    wide = w0_ref.shape[0]
    out = dot(an_ref[:, :wide], w0_ref[...], 1, 0) + dot(an_ref[:, wide:], w1_ref[...], 1, 0)
    out = out + dot(af_ref[:, :wide], w2_ref[...], 1, 0) + dot(af_ref[:, wide:], w3_ref[...], 1, 0)
    summed = (unit1 * g1_ref[...] + s1_ref[...]) + (out + bd_ref[...])
    unit, scale = unit_rows(summed)
    out_ref[...] = (unit * g2_ref[...] + s2_ref[...]).astype(BF16)
    cot = cot_ref[...]
    grad = norm_back(cot, unit, scale, g2_ref[...])
    gs_ref[...] = grad
    low = grad.astype(BF16)
    gf_ref[...] = low

    @pl.when(pl.program_id(0) == 0)
    def _():
        sums_ref[...] = jnp.zeros_like(sums_ref)

    sums_ref[0:1] += column_sum(cot * unit)
    sums_ref[1:2] += column_sum(cot)
    sums_ref[2:3] += column_sum(low.astype(F32))


def narrow(act_near, act_far, w_downs, residual, gain1, shift1, b_down, gain2, shift2, cotangent, wait=()):
    rows, depth = residual.shape
    tile = 256
    return call(
        narrow_kernel,
        "narrow",
        rows // tile,
        [tiled(act_near, tile), tiled(act_far, tile)]
        + [whole(w) for w in w_downs]
        + [tiled(residual, tile)]
        + [whole(v) for v in (gain1, shift1, b_down, gain2, shift2)]
        + [tiled(cotangent, tile)],
        [
            tiled_out((rows, depth), BF16, tile),
            tiled_out((rows, depth), F32, tile),
            tiled_out((rows, depth), BF16, tile),
            whole_out((8, depth), F32),
        ],
        wait=wait,
    )


def down_grad_kernel(gf_ref, acta_ref, actb_ref, da_ref, db_ref):
    grad = gf_ref[...]
    da_ref[...] = dot(acta_ref[...], grad, 0, 0).astype(BF16)
    db_ref[...] = dot(actb_ref[...], grad, 0, 0).astype(BF16)


def half_tile(array, which, tile):
    steps = array.shape[1] // 2 // tile
    return (array, (array.shape[0], tile), lambda i: (0, which * steps + i))


def down_grad(grad_ffn, acts, wait=()):
    rows, depth = grad_ffn.shape
    units = acts[0][0].shape[1] // 2
    tile = units // 2
    return call(
        down_grad_kernel,
        "down_grad",
        units // tile,
        [whole(grad_ffn)] + [half_tile(*item, tile) for item in acts],
        [tiled_out((units, depth), BF16, tile)] * 2,
        wait=wait,
    )


def ffn_back_kernel(gf_ref, n_ref, gn_in_ref, *refs):
    count = (len(refs) - 5) // 2
    piece_a, piece_b, (ga_ref, gb_ref, gba_ref, gbb_ref, gn_ref) = refs[:count], refs[count:-5], refs[-5:]

    @pl.when(pl.program_id(0) == 0)
    def _():
        gn_ref[...] = gn_in_ref[...]

    grad = gf_ref[...]
    for (fac_ref, wd_ref, wi_ref, *got), g_ref, gbias_ref in ((piece_a, ga_ref, gba_ref), (piece_b, gb_ref, gbb_ref)):
        grad_pre = (dot(grad, wd_ref[...], 1, 1) * fac_ref[...].astype(F32)).astype(BF16)
        gbias_ref[...] = column_sum(grad_pre.astype(F32))
        out = dot(n_ref[...], grad_pre, 0, 0)
        if got:
            out = out + got[0][...].astype(F32)
        g_ref[...] = out.astype(BF16)
        gn_ref[...] += dot(grad_pre, wi_ref[...], 1, 1)


def ffn_back(grad_ffn, normed, grad_normed, pieces, wait=()):
    rows, depth = grad_ffn.shape
    units = pieces[0][1].shape[0]
    tile = units
    steps = units // tile
    column = lambda i: (0, i)
    ins = [whole(grad_ffn), whole(normed), whole(grad_normed)]
    for fac, wd, wi, *got in pieces:
        ins += [half_tile(*fac, tile), tiled(wd, tile), (wi, (depth, tile), column)]
        ins += [(item, (depth, tile), column) for item in got]
    return call(
        ffn_back_kernel,
        "ffn_back",
        steps,
        ins,
        [((depth, units), BF16, (depth, tile), column)] * 2
        + [((1, units), F32, (1, tile), column)] * 2
        + [whole_out((rows, depth), F32)],
        wait=wait,
    )


def attend_back_core(q_ref, k_ref, v_ref, lse_ref, qf, kf, dqkv_s, gctx_s):
    span = q_ref.shape[1]
    items = [(pair, head) for pair in range(span // LANES) for head in range(2)]
    lane = lax.broadcasted_iota(jnp.int32, (1, LANES), 1)

    def front(pair, head):
        cols = slice(pair * LANES, (pair + 1) * LANES)
        scores = head_scores(q_ref, k_ref, qf, kf, pair, head)
        out = gctx_s[:, cols]
        out = jnp.where(lane // HEAD == head, out, jnp.zeros_like(out))
        return scores, dot(v_ref[:, cols], out, 1, 1)

    ahead = front(*items[0])
    for at, (pair, head) in enumerate(items):
        scores, grad_probs = ahead
        if at + 1 < len(items):
            ahead = front(*items[at + 1])
        cols = slice(pair * LANES, (pair + 1) * LANES)
        mine = lane // HEAD == head
        queries, out = q_ref[:, cols], gctx_s[:, cols]
        queries = jnp.where(mine, queries, jnp.zeros_like(queries))
        out = jnp.where(mine, out, jnp.zeros_like(out))
        if head == 0:
            keys = (k_ref[:, cols] * jnp.asarray(HEAD**-0.5, BF16)).T
            dqs, dk, dv = [], 0.0, 0.0
        probs = jnp.exp(scores - lse_ref[0, at : at + 1, :])
        centre = jnp.sum(probs * grad_probs, axis=0, keepdims=True)
        grad_scores = (probs * (grad_probs - centre)).astype(BF16)
        dqs.append(dot(keys[head * HEAD : (head + 1) * HEAD], grad_scores, 1, 0))
        dk = dk + dot(grad_scores, queries, 1, 0)
        dv = dv + dot(probs.astype(BF16), out, 1, 0)
        if head == 1:
            start = pair * LANES
            dqkv_s[:, start : start + LANES] = jnp.concatenate(dqs, axis=0).T.astype(BF16)
            dqkv_s[:, span + start : span + start + LANES] = dk.astype(BF16)
            dqkv_s[:, 2 * span + start : 2 * span + start + LANES] = dv.astype(BF16)


def attend_back_body(
    gattn, tok_ref, c_ref, q_ref, k_ref, v_ref, lse_ref, qf_ref, kf_ref, wq_ref, wk_ref, wv_ref, wa_ref, wb_ref,
    fa_ref, fb_ref, sums2_ref, sums1_ref, ga_ref, gb_ref, w_s, wo_s, gctx_s, dqkv_s, gw_s, bias_s,
):
    step = pl.program_id(0)
    span = q_ref.shape[1]
    width = span // 2
    cut = 2 * HEAD

    @pl.when(step == 0)
    def _():
        for at, ref in enumerate((wq_ref, wk_ref, wv_ref)):
            w_s[at * span : (at + 1) * span] = ref[...]
        stack_rows(wo_s, 0, wa_ref, wb_ref, 0)
        gw_s[...] = jnp.zeros_like(gw_s)
        bias_s[...] = jnp.zeros_like(bias_s)

    gctx_s[...] = dot(gattn, wo_s[...], 1, 1).astype(BF16)
    gw_s[3 * span :] += dot(c_ref[...], gattn, 0, 0)
    attend_back_core(q_ref, k_ref, v_ref, lse_ref, qf_ref[...], kf_ref[...], dqkv_s, gctx_s)
    dqkv = dqkv_s[...]
    gw_s[: 3 * span] += dot(dqkv, tok_ref[...], 0, 0)
    bias_s[0:1] += column_sum(dqkv[:, :span].astype(F32))
    bias_s[1:2] += column_sum(dqkv[:, 2 * span :].astype(F32))

    @pl.when(step == pl.num_programs(0) - 1)
    def _():
        for which, (ref, f_ref) in enumerate(((ga_ref, fa_ref), (gb_ref, fb_ref))):
            two, last = which * cut, 2 * cut + which * HEAD
            for at in range(4):
                start, own = at * span, at * width
                ref[own : own + cut] = gw_s[start + two : start + two + cut].astype(BF16)
                ref[own + cut : own + width] = gw_s[start + last : start + last + HEAD].astype(BF16)
            bias = bias_s[...]
            row = [bias[at : at + 1, lo : lo + size] for at in range(2) for lo, size in ((two, cut), (last, HEAD))]
            row = jnp.concatenate(row + [jnp.zeros((1, ref.shape[1] - span), F32)], axis=1)
            extra = [row, f_ref[...], sums1_ref[0:3], sums2_ref[0:3]]
            extra.append(jnp.zeros((ref.shape[0] - 4 * width - 8, ref.shape[1]), F32))
            ref[4 * width :] = jnp.concatenate(extra, axis=0).astype(BF16)

    return dot(dqkv, w_s[...], 1, 0)


def attend_back_first(gn_ref, res_ref, g1_ref, *rest):
    ins, (ga_ref, gb_ref, gt_ref, gattn_ref, sums_ref), scratch = rest[:16], rest[16:21], rest[21:]
    unit, scale = unit_rows(res_ref[...])
    grad = gn_ref[...]
    resid = norm_back(grad, unit, scale, g1_ref[...])
    low = resid.astype(BF16)
    gattn_ref[...] = low

    @pl.when(pl.program_id(0) == 0)
    def _():
        sums_ref[...] = jnp.zeros_like(sums_ref)

    sums_ref[0:1] += column_sum(low.astype(F32))
    sums_ref[1:2] += column_sum(grad * unit)
    sums_ref[2:3] += column_sum(grad)
    gt_ref[...] = resid
    gt_ref[...] += attend_back_body(low, *ins, sums_ref, ga_ref, gb_ref, *scratch)


def attend_back_next(gattn_ref, gtin_ref, *rest):
    ins, (ga_ref, gb_ref, gt_ref), scratch = rest[:17], rest[17:20], rest[20:]
    gt_ref[...] = gtin_ref[...] + attend_back_body(gattn_ref[...], *ins, ga_ref, gb_ref, *scratch)


def attend_back(lead, tokens, saved, pieces, sums, wait=()):
    ctx, q, k, v, lse, qf, kf, wq, wk, wv = saved
    rows, depth = tokens.shape
    heads = lse.shape[1]
    blocks = rows // BLOCK
    first = len(lead) == 3
    span = q.shape[1]
    ins = [tiled(item, BLOCK) if item.shape[0] == rows else whole(item) for item in lead]
    ins += [tiled(item, BLOCK) for item in (tokens, ctx, q, k, v)]
    ins += [(lse, (1, heads, BLOCK), lambda i: (i, 0, 0)), tiled(qf, BLOCK), tiled(kf, BLOCK)]
    ins += [whole(item) for item in (wq, wk, wv)] + [out_rows(item) for item in pieces]
    ins += [whole(item) for item in sums]
    bundle = (2 * span + TAIL, depth)
    outs = [whole_out(bundle, BF16)] * 2 + [tiled_out((rows, depth), F32, BLOCK)]
    if first:
        outs += [tiled_out((rows, depth), BF16, BLOCK), whole_out((8, depth), F32)]
    return call(
        attend_back_first if first else attend_back_next,
        "attend_back",
        blocks,
        ins,
        outs,
        [
            pltpu.VMEM((3 * span, depth), BF16),
            pltpu.VMEM((span, depth), BF16),
            pltpu.VMEM((BLOCK, span), BF16),
            pltpu.VMEM((BLOCK, 3 * span), BF16),
            pltpu.VMEM((4 * span, depth), F32),
            pltpu.VMEM((8, span), F32),
        ],
        wait=wait,
    )


def picked(kernel, name, index, steps, ins, outs, wait=(), cost=10):
    count = len(ins)

    def body(_, *refs):
        kernel(*refs[:count], *refs[count + len(wait) :])

    anywhere = pl.BlockSpec(memory_space=pl.ANY)
    return pl.pallas_call(
        body,
        grid_spec=pltpu.PrefetchScalarGridSpec(
            num_scalar_prefetch=1,
            grid=(steps,),
            in_specs=[pl.BlockSpec(block, at) for _, block, at in ins] + [anywhere] * len(wait),
            out_specs=[pl.BlockSpec(block, at) for _, _, block, at in outs],
        ),
        out_shape=[jax.ShapeDtypeStruct(shape, dtype) for shape, dtype, _, _ in outs],
        compiler_params=pltpu.CompilerParams(dimension_semantics=("arbitrary",), vmem_limit_bytes=VMEM),
        cost_estimate=pl.CostEstimate(flops=cost * COST_UNIT + 1, bytes_accessed=1, transcendentals=0),
        name=name,
    )(index.astype(jnp.int32)[None], *[item[0] for item in ins], *wait)


def tiles_in(rows):
    return 2 if rows % 32 == 0 else 1


def combine(terms, index=None, count=1, after=(), cost=10):
    if index is None:
        index = jnp.zeros((), jnp.int32)
    rows, columns = terms[0].shape
    size = rows // count
    steps = tiles_in(size)
    tile = size // steps

    def chunk(k):
        return lambda i, at: ((at[0] ^ k) * steps + i, 0)

    def kernel(*refs):
        for k in range(count):
            total = sum(ref[...].astype(F32) for ref in refs[k * len(terms) : (k + 1) * len(terms)])
            refs[count * len(terms) + k][...] = total.astype(BF16)

    return picked(
        kernel,
        "combine",
        index,
        steps,
        [(term, (tile, columns), chunk(k)) for k in range(count) for term in terms],
        [((size, columns), BF16, (tile, columns), lambda i, at: (i, 0))] * count,
        after,
        cost,
    )


def arrange(parts, index, sizes=None, split=1, after=(), cost=10):
    size, columns = parts[0].shape
    count = len(parts)
    if sizes is None:
        each = size // split

        def kernel(index_ref, *refs):
            for here in range(count):

                @pl.when(index_ref[0] == here)
                def _(here=here):
                    for k in range(count):
                        start = (here ^ k) * each
                        for out in range(split):
                            refs[count + out][start : start + each] = refs[k][out * each : (out + 1) * each]

        return call(
            kernel,
            "arrange",
            1,
            [(index.astype(jnp.int32)[None], None, None)] + [whole(part) for part in parts],
            [whole_out((count * each, columns), BF16)] * split,
            wait=after,
            cost=cost,
        )

    def kernel_out(index_ref, *refs):
        for here in range(count):

            @pl.when(index_ref[0] == here)
            def _(here=here):
                start = 0
                for out in refs[count:]:
                    end = start + out.shape[0]
                    for k in range(count):
                        low = (here ^ k) * size
                        lo, hi = max(start, low), min(end, low + size)
                        if lo < hi:
                            out[lo - start : hi - start] = refs[k][lo - low : hi - low].astype(F32)
                    start = end

    return call(
        kernel_out,
        "arrange_out",
        1,
        [(index.astype(jnp.int32)[None], None, None)] + [whole(part) for part in parts],
        [whole_out((rows, columns), F32) for rows in sizes],
    )


def swap(values, axis, bit):
    count = lax.axis_size(axis)
    return lax.ppermute(values, axis, [(at, at ^ bit) for at in range(count)])


def gate(values, *after):
    def kernel(*refs):
        pass

    anywhere = pl.BlockSpec(memory_space=pl.ANY)
    return pl.pallas_call(
        kernel,
        in_specs=[anywhere] * (1 + len(after)),
        out_specs=anywhere,
        out_shape=jax.ShapeDtypeStruct(values.shape, values.dtype),
        input_output_aliases={0: 0},
        name="gate",
    )(values, *after)


def dp_bits():
    bits, bit = [], 1
    while bit < lax.axis_size("dp"):
        bits.append(bit)
        bit *= 2
    return bits


def groups(bits):
    return [bits[:1]] + [bits[at : at + 2] for at in range(1, len(bits), 2)]


def spot(bits):
    me = lax.axis_index("dp")
    at = sum(((me // bit) % 2) << i for i, bit in enumerate(bits))
    return at, [sum(bit for i, bit in enumerate(bits) if k >> i & 1) for k in range(1 << len(bits))]


def scatter(terms, bits, after=(), cost=10):
    at, far = spot(bits)
    kept, *sent = combine(terms, at, len(far), after, cost)
    return [kept] + [swap(item, "dp", distance) for item, distance in zip(sent, far[1:])]


def sum_whole(values, steps):
    for bit in [bit for step in steps for bit in step]:
        (values,) = combine((values, swap(values, "dp", bit)))
    return values


def gather(values, bits):
    _, far = spot(bits)
    return [values] + [swap(values, "dp", distance) for distance in far[1:]]


def ordered(parts, bits, sizes=None):
    return arrange(parts, spot(bits)[0], sizes)


def parity():
    me = lax.axis_index("dp")
    return (me ^ (me >> 1)) % 2


def my_half(arrays):
    columns = arrays[0].shape[1]
    quarters = [array.shape[0] // 4 for array in arrays]

    def kernel(*refs):
        ins, outs = refs[: 2 * len(arrays)], refs[2 * len(arrays) :]
        for part in range(2):
            start = 0
            for at, rows in enumerate(quarters):
                outs[part][start : start + rows] = ins[2 * at + part][...]
                start += rows

    return picked(
        kernel,
        "my_half",
        parity(),
        1,
        [
            (array, (rows, columns), lambda i, at, part=part: (at[0] * 2 + part, 0))
            for array, rows in zip(arrays, quarters)
            for part in range(2)
        ],
        [((sum(quarters), columns), BF16, (sum(quarters), columns), lambda i, at: (0, 0))] * 2,
    )


def pack(arrays):
    rows = sum(array.shape[0] for array in arrays)
    columns = arrays[0].shape[1]
    quarter = rows // 4

    def kernel(index_ref, *refs):
        ins, (out, *parts) = refs[: len(arrays)], refs[len(arrays) :]
        start = 0
        for ref in ins:
            out[start : start + ref.shape[0]] = ref[...]
            start += ref.shape[0]
        for side in range(2):

            @pl.when(index_ref[0] == side)
            def _(side=side):
                for at, part in enumerate(parts):
                    low = (2 * side + at) * quarter
                    part[...] = out[low : low + quarter]

    return call(
        kernel,
        "pack",
        1,
        [(parity().astype(jnp.int32)[None], None, None)] + [whole(array) for array in arrays],
        [whole_out((rows, columns), BF16)] + [whole_out((quarter, columns), BF16)] * 2,
    )


def other_half(first, second):
    return swap(first, "dp", 1), swap(second, "dp", 2)


def per_device(
    tokens, bucket, lengths, w_query, b_query, w_key, w_value, b_value, w_out, b_out, gain1, shift1,
    w_in, b_in, w_down, b_down, gain2, shift2, cotangent,
):
    rows, depth = tokens.shape
    width = w_query.shape[1]
    me = lax.axis_index("tensor")
    line = lambda v: v.astype(F32)[None]
    b_out, gain1, shift1, b_down, gain2, shift2 = map(line, (b_out, gain1, shift1, b_down, gain2, shift2))

    row = jnp.concatenate((b_query, b_value, jnp.zeros((depth - 2 * width,), BF16)))
    biases = jnp.pad(jnp.stack((row, b_in)), ((0, EXTRA - 2), (0, 0)))
    own, *parts = pack((w_query.T, w_key.T, w_value.T, w_out, biases))
    p1 = swap(own, "tensor", 1)
    pa, pb = [swap(item, "tensor", 2) for item in parts]
    wide = my_half((w_in, w_down))
    wa, wb = [swap(item, "tensor", 2) for item in wide]
    in1 = swap(w_in, "tensor", 1)
    down1 = swap(w_down, "tensor", 1)

    place_y = me.astype(jnp.int32)[None]
    (p2,) = arrange((pa, pb, *other_half(pa, pb)), 2 * parity(), cost=0)
    p3 = swap(p2, "tensor", 1)
    qn, kn, vn, cn, lsen, *wn, qf, kf = attend((bucket, lengths, place_y), tokens, own, p1, (*wide, p2, wa))
    qr, kr, vr, cr, lser, *wr = attend((qf, kf), tokens, p2, p3)
    wa, wb = gate(wa, cn), gate(wb, cn)
    others = other_half(wa, wb)
    residual, normed = join(tokens, cn, cr, (own, p1, p2, p3), b_out, gain1, shift1)
    in2, down2 = arrange((wa, wb, *others), 2 * parity(), split=2, after=(normed,))
    in3, down3 = swap(in2, "tensor", 1), swap(down2, "tensor", 1)
    actn, facn = widen(normed, w_in, in1, own, p1, (in2,))
    actr, facr = widen(normed, in2, in3, p2, p3)
    block_out, grad_summed, grad_ffn, sums2 = narrow(
        actn, actr, (w_down, down1, down2, down3), residual, gain1, shift1, b_down, gain2, shift2, cotangent
    )
    low, *highs = groups(dp_bits())
    d3, d2 = down_grad(grad_ffn, ((actr, 1), (actr, 0)))
    d1, d0 = down_grad(grad_ffn, ((actn, 1), (actn, 0)))
    (dfar,) = combine((d2, swap(d3, "tensor", 1)), after=(d0,), cost=10)
    i3, i2, fb3, fb2, grad_normed = ffn_back(
        grad_ffn, normed, grad_summed, (((facr, 1), down3, in3), ((facr, 0), down2, in2)), (dfar,)
    )
    i1, i0, fb1, fb0, grad_normed = ffn_back(
        grad_ffn, normed, grad_normed, (((facn, 1), down1, in1), ((facn, 0), w_down, w_in))
    )
    dfar = swap(dfar, "tensor", 2)
    i1 = swap(gate(i1, dfar), "tensor", 1)
    (ifar,) = combine((i2, swap(gate(i3, i0, dfar), "tensor", 1)), cost=10)
    dsum = scatter((d0, swap(d1, "tensor", 1), dfar), low, (i0,), 10)
    saved_r = (cr, qr, kr, vr, lser, qf, kf, *wr)
    saved_n = (cn, qn, kn, vn, lsen, qf, kf, *wn)
    a2, a3, grad_tokens, grad_attn, sums1 = attend_back(
        (grad_normed, residual, gain1), tokens, saved_r, (p2, p3), (fb2, fb3, sums2), (dsum[0], ifar)
    )
    ifar = swap(ifar, "tensor", 2)
    a3 = swap(gate(a3, dsum[1], ifar), "tensor", 1)
    (afar,) = combine((a2, a3), cost=10)
    dsum = scatter(dsum, highs[0], (a2,), 0)
    isum = scatter((i0, i1, ifar), low, (a3,), 10)
    a0, a1, grad_tokens = attend_back(
        (grad_attn, grad_tokens), tokens, saved_n, (own, p1), (fb0, fb1, sums2, sums1), (dsum[0], isum[0], afar)
    )
    afar = swap(afar, "tensor", 2)
    a1 = swap(gate(a1, afar, *dsum[1:], *isum[1:]), "tensor", 1)
    high, more = highs[0], highs[1:]
    asum = scatter((a0, a1, afar), low, cost=0)
    (dsum,) = combine(dsum, after=(asum[0],), cost=0)
    dparts = gather(sum_whole(dsum, more), high)
    isum = scatter(isum, high, (asum[0],), 0)
    asum = scatter(asum, high, (*dparts[1:], *isum[1:]), 0)
    dparts = gather(ordered(dparts, high)[0], low)
    (isum,) = combine(isum, cost=0)
    iparts = gather(sum_whole(isum, more), high)
    (asum,) = combine(asum, after=(dparts[1],), cost=0)
    aparts = gather(sum_whole(asum, more), high)
    iparts = gather(ordered(iparts, high)[0], low)
    (asum,) = ordered(aparts, high)
    (grad_wd,) = ordered(dparts, low, (w_down.shape[0],))
    (grad_wi,) = ordered(iparts, low, (depth,))
    *grad_qkv, grad_wo, small = ordered(gather(asum, low), low, (width,) * 4 + (8,))
    grad_wq, grad_wk, grad_wv = [item.T for item in grad_qkv]
    return (
        block_out,
        grad_tokens,
        grad_wq,
        small[0, :width],
        grad_wk,
        grad_wv,
        small[0, width : 2 * width],
        grad_wo,
        small[2],
        small[3],
        small[4],
        grad_wi,
        small[1],
        grad_wd,
        small[7],
        small[5],
        small[6],
    )


def solution(mesh):
    group = P(("dp", "tensor"), None)
    column, row, part, full = P(None, "tensor"), P("tensor", None), P("tensor"), P()
    in_specs = (
        group, P("dp"), P("dp", None), column, part, column, column, part, row,
        full, full, full, column, part, row, full, full, full, group,
    )
    out_specs = (
        group, group, column, part, column, column, part, row,
        full, full, full, column, part, row, full, full, full,
    )
    return jax.shard_map(
        per_device, mesh=mesh, in_specs=in_specs, out_specs=out_specs, check_vma=False
    )
```
